32 devices in a mesh: src: 8 (over z, x), tgt: 4 (over y, core).
Axes of the slice: x: 2, y: 2, z: 4, core: 2. Of those that a mesh axis runs over, the one named last changes fastest.
Arguments:
- source_cells: float32 [32, 65536], P(None, 'src'), may hold values from -25 to 25
- target_cells: float32 [32, 65536], P(None, 'tgt'), may hold values from -25 to 25
- source_counts: int32 [64], P('src'), may hold values from 256 to 1024, as said below
- target_counts: int32 [64], P('tgt'), may hold values from 256 to 1024, as said below
- source_weight: float32 [65536], P('src'), may hold values from -8 to 8
- target_weight: float32 [65536], P('tgt'), may hold values from -8 to 8
- start_potential: float32 [65536], P('tgt'), may hold values from -6 to 6
- pair_blocks: int32 [8, 4, 2, 16], P('src', 'tgt'), may hold values from 0 to 15, as said below
- pair_count: int32 [8, 4], P('src', 'tgt'), may hold values from 4 to 16, as said below
Outputs:
- source_potential: float32 [65536], P('src')
- target_potential: float32 [65536], P('tgt')
The draws below stay inside these ranges and needn't reach their ends.
Inputs may be any that keep to these rules, and one draw needn't show every extreme that they name: `source_counts`: every block has at least 256 live cells; some block has all 1024 in every draw. `target_counts`: every block has at least 256 live cells; some block has all 1024 in every draw. `pair_count`: some device holds exactly 16 pairs in every draw. `pair_blocks`: entry 0 is below 8, entry 1 below 16. The first pair_count slots of a device are distinct pairs; later slots hold valid numbers that are not used. Every source block has a pair on some device of its src index, every target block on some device of its tgt index.
All inputs are finite; a program needn't handle non-finite values.
Results may differ from the reference program's by a relative error of at most 0.0003.
Values sent between devices are 32-bit elements; how exact they have to be, the bound alone decides.
No kernel may reach another device: no remote copies, remote signals or barrier semaphores. Data moves between devices by JAX's collectives and lax.ppermute only.
A program may use at most 192 MiB of HBM per device.

```python
import jax
import jax.numpy as jnp
from jax import lax

EMBED = 32
BLOCK = 1024
SOURCE_DEV = 8
TARGET_DEV = 16
SLOTS = 16
ITERS = 2
SOURCE_CELLS = 65536
TARGET_CELLS = 65536
N_SRC = 8
N_TGT = 4


def embed_cells(key, width):
    values = jnp.clip(jax.random.normal(jax.random.fold_in(key, 7), (EMBED, width), jnp.float32), -6.0, 6.0)
    return values


def draw_source_cells(key, part):
    return embed_cells(jax.random.fold_in(key, 201), SOURCE_CELLS)


def draw_target_cells(key, part):
    return embed_cells(jax.random.fold_in(key, 202), TARGET_CELLS)


def block_counts(key, number):
    counts = jax.random.randint(jax.random.fold_in(key, 1), (number,), BLOCK // 4, BLOCK + 1)
    chosen = jax.random.randint(jax.random.fold_in(key, 2), (), 0, number)
    return jnp.where(jnp.arange(number) == chosen, BLOCK, counts).astype(jnp.int32)


def draw_source_counts(key, part):
    return block_counts(jax.random.fold_in(key, 301), SOURCE_DEV * N_SRC)


def draw_target_counts(key, part):
    return block_counts(jax.random.fold_in(key, 302), TARGET_DEV * N_TGT)


def needed_pairs():
    return max((SOURCE_DEV + N_TGT - 1) // N_TGT, (TARGET_DEV + N_SRC - 1) // N_SRC)


def draw_pair_count(key, part):
    devices = N_SRC * N_TGT
    least = needed_pairs()
    lower = max(least, SLOTS // 4)
    upper = max(least, 3 * SLOTS // 4)
    counts = jax.random.randint(jax.random.fold_in(key, 101), (devices,), lower, upper + 1)
    chosen = jax.random.randint(jax.random.fold_in(key, 102), (), 0, devices)
    counts = jnp.where(jnp.arange(devices) == chosen, SLOTS, counts)
    return counts.reshape(N_SRC, N_TGT).astype(jnp.int32)


def draw_pair_blocks(key, part):
    devices = N_SRC * N_TGT
    choices_all = SOURCE_DEV * TARGET_DEV
    least = needed_pairs()
    keys = jax.random.split(jax.random.fold_in(key, 103), devices)
    ranks = jax.vmap(lambda single: jax.random.permutation(single, choices_all))(keys)
    device = jnp.arange(devices, dtype=jnp.int32)
    steps_k = jnp.arange(least, dtype=jnp.int32)
    source_part = (device[:, None] % N_TGT + steps_k[None, :] * N_TGT) % SOURCE_DEV
    target_part = (device[:, None] // N_TGT + steps_k[None, :] * N_SRC) % TARGET_DEV
    needed = source_part * TARGET_DEV + target_part
    matched = jnp.any(jnp.arange(choices_all)[None, None, :] == needed[:, :, None], axis=1)
    ranks = jnp.where(matched, -1, ranks)
    order = jnp.argsort(ranks, axis=1, stable=True)[:, :SLOTS]
    stacked = jnp.stack([order // TARGET_DEV, order % TARGET_DEV], axis=1)
    return stacked.reshape(N_SRC, N_TGT, 2, SLOTS).astype(jnp.int32)


def steps_of(rng, extent, cuts, low, top_value):
    gain, own = 1.0, jax.random.fold_in(rng, 6)
    for position, shards_of in cuts:
        draws = jnp.exp(jax.random.uniform(jax.random.fold_in(own, position), (shards_of,), jnp.float32, low / len(cuts), top_value / len(cuts)))
        gain = gain * jnp.repeat(draws, extent[position] // shards_of).reshape([-1 if axis == position else 1 for axis in range(len(extent))])
    return gain


def normal_values(stream_key, extent, scale, limit, shards=(), kind=jnp.bfloat16):
    gain = steps_of(stream_key, extent, shards, -0.22, 0.18) if shards else 1.0
    drawn = jax.random.normal(stream_key, extent, jnp.float32) * scale * gain
    return jnp.minimum(jnp.maximum(drawn, -limit), limit).astype(kind)


def setup_inputs(seed: int = 0) -> dict:
    splits = jax.random.split(jax.random.key(seed), 10)
    source_cells = draw_source_cells(jax.random.fold_in(splits[9], 71), 0)
    target_cells = draw_target_cells(jax.random.fold_in(splits[9], 71), 0)
    source_counts = draw_source_counts(jax.random.fold_in(splits[9], 71), 0)
    target_counts = draw_target_counts(jax.random.fold_in(splits[9], 71), 0)
    source_weight = normal_values(splits[4], (SOURCE_CELLS,), 2.0, 8.0, ((0, 8),), jnp.float32)
    target_weight = normal_values(splits[5], (TARGET_CELLS,), 2.0, 8.0, ((0, 4),), jnp.float32)
    start_potential = normal_values(splits[6], (TARGET_CELLS,), 1.0, 6.0, ((0, 4),), jnp.float32)
    pair_blocks = draw_pair_blocks(jax.random.fold_in(splits[9], 71), 0)
    pair_count = draw_pair_count(jax.random.fold_in(splits[9], 71), 0)
    return {"source_cells": source_cells, "target_cells": target_cells, "source_counts": source_counts, "target_counts": target_counts, "source_weight": source_weight, "target_weight": target_weight, "start_potential": start_potential, "pair_blocks": pair_blocks, "pair_count": pair_count}


entropy_scale = 0.1
very_negative = -1.0e30


def combine_stats(first, second):
    top = jnp.maximum(first[0], second[0])
    total = first[1] * jnp.exp(first[0] - top) + second[1] * jnp.exp(second[0] - top)
    return (top, total)


def block_cost(source_block, target_block):
    cross = lax.dot_general(source_block, target_block, (((0,), (0,)), ((), ())), precision=lax.Precision.HIGHEST, preferred_element_type=jnp.float32)
    source_sq = jnp.sum(source_block * source_block, axis=0)
    target_sq = jnp.sum(target_block * target_block, axis=0)
    return (source_sq[:, None] + target_sq[None, :] - 2.0 * cross) / source_block.shape[0]


def potential_from(stats, log_weight, live):
    safe_total = jnp.where(live, stats[1], 1.0)
    value = entropy_scale * log_weight - entropy_scale * (stats[0] + jnp.log(safe_total))
    return jnp.where(live, value, 0.0)


def reference(source_cells, target_cells, source_counts, target_counts, source_weight, target_weight, start_potential, pair_blocks, pair_count):
    positions = jnp.arange(BLOCK, dtype=jnp.int32)
    source_live = (positions[None, :] < source_counts[:, None]).reshape(-1)
    target_live = (positions[None, :] < target_counts[:, None]).reshape(-1)
    flat_pairs = pair_blocks.reshape(N_SRC * N_TGT, 2, SLOTS)
    flat_count = pair_count.reshape(-1)
    total_slots = N_SRC * N_TGT * SLOTS

    def locate(index):
        device = index // SLOTS
        slot = index % SLOTS
        source_block = ((device // N_TGT) * SOURCE_DEV + flat_pairs[device, 0, slot]).astype(jnp.int32)
        target_block = ((device % N_TGT) * TARGET_DEV + flat_pairs[device, 1, slot]).astype(jnp.int32)
        return source_block, target_block, slot < flat_count[device]

    def half(potential, rows):
        length = SOURCE_CELLS if rows else TARGET_CELLS
        init = (jnp.full((length,), very_negative, jnp.float32), jnp.zeros((length,), jnp.float32))

        def advance(index, stats):
            source_block, target_block, used = locate(index)

            def work(stats):
                source_start = (source_block * BLOCK).astype(jnp.int32)
                target_start = (target_block * BLOCK).astype(jnp.int32)
                cost = block_cost(lax.dynamic_slice_in_dim(source_cells, source_start, BLOCK, 1), lax.dynamic_slice_in_dim(target_cells, target_start, BLOCK, 1))
                if rows:
                    other = lax.dynamic_slice_in_dim(potential, target_start, BLOCK)
                    other_live = lax.dynamic_slice_in_dim(target_live, target_start, BLOCK)
                    scores = jnp.where(other_live[None, :], (other[None, :] - cost) / entropy_scale, very_negative)
                    axis, start = 1, source_start
                else:
                    other = lax.dynamic_slice_in_dim(potential, source_start, BLOCK)
                    other_live = lax.dynamic_slice_in_dim(source_live, source_start, BLOCK)
                    scores = jnp.where(other_live[:, None], (other[:, None] - cost) / entropy_scale, very_negative)
                    axis, start = 0, target_start
                top = jnp.max(scores, axis=axis)
                total = jnp.sum(jnp.exp(scores - jnp.expand_dims(top, axis)), axis=axis)
                old = (lax.dynamic_slice_in_dim(stats[0], start, BLOCK), lax.dynamic_slice_in_dim(stats[1], start, BLOCK))
                new = combine_stats(old, (top, total))
                return (lax.dynamic_update_slice_in_dim(stats[0], new[0], start, 0), lax.dynamic_update_slice_in_dim(stats[1], new[1], start, 0))

            return lax.cond(used, work, lambda kept: kept, stats)

        return lax.fori_loop(0, total_slots, advance, init)

    target_pot = start_potential
    source_pot = jnp.zeros((SOURCE_CELLS,), jnp.float32)
    for repeat in range(ITERS):
        source_pot = potential_from(half(target_pot, True), source_weight, source_live)
        target_pot = potential_from(half(source_pot, False), target_weight, target_live)
    return source_pot, target_pot
```

```python
import math

import jax
import jax.numpy as jnp
from jax import lax
from jax.experimental import pallas as pl
from jax.experimental.pallas import tpu as pltpu
from jax.sharding import PartitionSpec as P

F32 = jnp.float32
BF16 = jnp.bfloat16
BLOCK = 1024
LANES = 128
TILES = BLOCK // LANES
CHUNK = 256
PER_BLOCK = BLOCK // CHUNK
UNROLL = 8
SHIFT = 8
DEAD = -1e30
LOW, HIGH = 2.0**-96, 2.0**120
ENTROPY = 0.1
LOG2E = math.log2(math.e)
POT = LOG2E / ENTROPY
VMEM_LIMIT = 48 * 1024 * 1024


def split3(value):
    high = value.astype(BF16).astype(F32)
    rest = value - high
    middle = rest.astype(BF16).astype(F32)
    return high, middle, (rest - middle).astype(BF16).astype(F32)


def position():
    return lax.broadcasted_iota(jnp.int32, (TILES, LANES), 0) * LANES + lax.broadcasted_iota(
        jnp.int32, (TILES, LANES), 1
    )


def block_rows(b):
    return pl.ds(pl.multiple_of(b * TILES, TILES), TILES)


def merge(parts):
    top = parts[0]
    for part in parts[1:]:
        top = jnp.maximum(top, part)
    total = jnp.exp2(parts[0] - top)
    for part in parts[1:]:
        total = total + jnp.exp2(part - top)
    return top + jnp.log2(total)


def list_units(pairs, count, source_counts, target_counts, units):
    last = units.shape[0] - 1
    rows = source_counts.shape[0] * PER_BLOCK

    def pair(p, n):
        sb, tb = pairs[0, 0, 0, p], pairs[0, 0, 1, p]
        nr = (source_counts[sb] + CHUNK - 1) // CHUNK
        nc = (target_counts[tb] + CHUNK - 1) // CHUNK

        def row(r, n):
            base = ((sb * PER_BLOCK + r) << SHIFT) + tb * PER_BLOCK

            def column(c, n):
                units[n] = base + c
                return n + 1

            return lax.fori_loop(0, nc, column, n)

        return lax.fori_loop(0, nr, row, n)

    n = lax.fori_loop(0, count[0, 0], pair, 0)
    steps = (n + UNROLL - 1) // UNROLL

    def fill(i, carry):
        units[i] = rows << SHIFT
        return carry

    lax.fori_loop(n, steps * UNROLL, fill, 0)
    units[last] = steps


def mark(side, pairs, count, counts, limit):
    def clear(b, carry):
        limit[b] = 0
        return carry

    def touch(p, carry):
        b = pairs[0, 0, side, p]
        limit[b] = counts[b]
        return carry

    lax.fori_loop(0, counts.shape[0], clear, 0)
    lax.fori_loop(0, count[0, 0], touch, 0)


class Scores:
    def __init__(self, units, x1, x2, y, ye):
        self.units, self.x1, self.x2, self.y, self.ye = units, x1, x2, y, ye
        self.row_chunks = x1.shape[0] // CHUNK
        self.col_chunks = y.shape[1] // CHUNK

    def steps(self):
        return self.units[self.units.shape[0] - 1]

    def at(self, t):
        unit = self.units[t]
        row = unit >> SHIFT
        col = unit & ((1 << SHIFT) - 1)
        r0 = pl.multiple_of(jnp.minimum(row, self.row_chunks - 1) * CHUNK, CHUNK)
        c0 = pl.multiple_of(col * CHUNK, CHUNK)
        lhs = jnp.concatenate([self.x1[pl.ds(r0, CHUNK), :], self.x2[pl.ds(r0, CHUNK), :]], axis=1)
        cols = pl.ds(c0, CHUNK)
        if self.ye is None:
            rhs = self.y[:, cols]
        else:
            rhs = jnp.concatenate([self.y[0:128, cols], self.ye[:, cols], self.y[144:256, cols]], axis=0)
        value = jnp.dot(lhs, rhs, preferred_element_type=F32)
        return value, row, jnp.where(row == self.row_chunks, self.col_chunks, col)

    def each(self, body):
        def step(s, carry):
            for u in range(UNROLL):
                body(*self.at(s * UNROLL + u))
            return carry

        lax.fori_loop(0, self.steps(), step, 0)

    def each_single(self, body):
        def step(t, carry):
            body(*self.at(t))
            return carry

        lax.fori_loop(0, self.steps() * UNROLL, step, 0)


def fill_ref(ref, rows, value):
    def body(i, carry):
        ref[pl.ds(pl.multiple_of(i * rows, rows), rows), :] = jnp.full((rows, ref.shape[1]), value, F32)
        return carry

    lax.fori_loop(0, ref.shape[0] // rows, body, 0)


def row_chunk(row):
    return pl.ds(pl.multiple_of(row * CHUNK, CHUNK), CHUNK)


def col_chunk(col):
    return pl.ds(pl.multiple_of(col * 8, 8), 8)


def check(total, b, limit):
    fine = (total >= LOW) & (total <= HIGH)
    return jnp.where(fine | (position() >= limit[b]), 0.0, 1.0)


def row_sums(acc, b):
    rows = []
    for r in range(TILES):
        start = pl.multiple_of(b * BLOCK + r * LANES, LANES)
        rows.append(jnp.sum(acc[pl.ds(start, LANES), :].T, axis=0, keepdims=True))
    return jnp.concatenate(rows, axis=0)


def row_half(scores, limit, offset, out, acc, tops):
    blocks = out.shape[0] // TILES
    fill_ref(acc, CHUNK, 0.0)

    def add(value, row, col):
        e = jnp.exp2(value)
        part = e[:, :LANES]
        for k in range(1, CHUNK // LANES):
            part = part + e[:, k * LANES : (k + 1) * LANES]
        acc[row_chunk(row), :] += part

    scores.each(add)

    def finish(b, bad):
        total = row_sums(acc, b)
        out[block_rows(b), :] = jnp.where(total > 0.0, offset + jnp.log2(total), DEAD)
        return jnp.maximum(bad, check(total, b, limit))

    bad = lax.fori_loop(0, blocks, finish, jnp.zeros((TILES, LANES), F32))

    @pl.when(jnp.max(bad) > 0.0)
    def _():
        fill_ref(acc, CHUNK, DEAD)

        def highest(value, row, col):
            part = value[:, :LANES]
            for k in range(1, CHUNK // LANES):
                part = jnp.maximum(part, value[:, k * LANES : (k + 1) * LANES])
            acc[row_chunk(row), :] = jnp.maximum(acc[row_chunk(row), :], part)

        scores.each_single(highest)

        def spread(i, carry):
            top = jnp.max(acc[row_chunk(i), :], axis=1, keepdims=True)
            top = jnp.where(top > 0.5 * DEAD, top, 0.0)
            tops[row_chunk(i), :] = jnp.broadcast_to(top, (CHUNK, LANES))
            return carry

        lax.fori_loop(0, acc.shape[0] // CHUNK, spread, 0)
        fill_ref(acc, CHUNK, 0.0)

        def add_below(value, row, col):
            top = tops[row_chunk(row), :]
            part = jnp.exp2(value[:, :LANES] - top)
            for k in range(1, CHUNK // LANES):
                part = part + jnp.exp2(value[:, k * LANES : (k + 1) * LANES] - top)
            acc[row_chunk(row), :] += part

        scores.each_single(add_below)

        def finish_below(b, carry):
            total = row_sums(acc, b)
            rows = []
            for r in range(TILES):
                start = pl.multiple_of(b * BLOCK + r * LANES, LANES)
                rows.append(tops[pl.ds(start, LANES), :].T[0:1, :])
            top = jnp.concatenate(rows, axis=0)
            out[block_rows(b), :] = jnp.where(total > 0.0, (offset + top) + jnp.log2(total), DEAD)
            return carry

        lax.fori_loop(0, blocks, finish_below, 0)


def col_tile(acc, b, reduce):
    rows = []
    for c in range(PER_BLOCK):
        line = reduce(acc[col_chunk(b * PER_BLOCK + c), :], axis=0, keepdims=True)
        for k in range(CHUNK // LANES):
            rows.append(line[:, k * LANES : (k + 1) * LANES])
    return jnp.concatenate(rows, axis=0)


def col_half(scores, limit, offset, out, acc, tops):
    blocks = out.shape[0] // TILES
    fill_ref(acc, 8, 0.0)

    def add(value, row, col):
        e = jnp.exp2(value)
        acc[col_chunk(col), :] += jnp.sum(e.reshape(CHUNK // 8, 8, CHUNK), axis=0)

    scores.each(add)

    def finish(b, bad):
        total = col_tile(acc, b, jnp.sum)
        out[block_rows(b), :] = jnp.where(total > 0.0, offset + jnp.log2(total), DEAD)
        return jnp.maximum(bad, check(total, b, limit))

    bad = lax.fori_loop(0, blocks, finish, jnp.zeros((TILES, LANES), F32))

    @pl.when(jnp.max(bad) > 0.0)
    def _():
        fill_ref(tops, 8, DEAD)

        def highest(value, row, col):
            part = jnp.max(value.reshape(CHUNK // 8, 8, CHUNK), axis=0)
            tops[col_chunk(col), :] = jnp.maximum(tops[col_chunk(col), :], part)

        scores.each_single(highest)

        def spread(i, carry):
            top = jnp.max(tops[col_chunk(i), :], axis=0, keepdims=True)
            top = jnp.where(top > 0.5 * DEAD, top, 0.0)
            tops[col_chunk(i), :] = jnp.broadcast_to(top, (8, CHUNK))
            return carry

        lax.fori_loop(0, tops.shape[0] // 8, spread, 0)
        fill_ref(acc, 8, 0.0)

        def add_below(value, row, col):
            e = jnp.exp2(value.reshape(CHUNK // 8, 8, CHUNK) - tops[col_chunk(col), :][None])
            acc[col_chunk(col), :] += jnp.sum(e, axis=0)

        scores.each_single(add_below)

        def finish_below(b, carry):
            total = col_tile(acc, b, jnp.sum)
            top = col_tile(tops, b, jnp.max)
            out[block_rows(b), :] = jnp.where(total > 0.0, (offset + top) + jnp.log2(total), DEAD)
            return carry

        lax.fori_loop(0, blocks, finish_below, 0)


def put_in_columns(potential, counts, offset, ye):
    sub = lax.broadcasted_iota(jnp.int32, (16, LANES), 0)

    def body(b, carry):
        value = jnp.where(position() < counts[b], potential[block_rows(b), :] - offset, DEAD)
        high, middle, low = split3(value)
        for k in range(TILES):
            rows = jnp.where(
                sub == 0,
                high[k : k + 1, :],
                jnp.where(sub == 1, middle[k : k + 1, :], jnp.where(sub == 2, low[k : k + 1, :], 1.0)),
            )
            rows = jnp.where(sub < 6, rows, 0.0)
            ye[:, pl.ds(pl.multiple_of(b * BLOCK + k * LANES, LANES), LANES)] = rows.astype(BF16)
        return carry

    lax.fori_loop(0, counts.shape[0], body, 0)


def put_in_rows(potential, counts, offset, x2, x2f):
    sub = lax.broadcasted_iota(jnp.int32, (LANES, LANES), 0)
    lane = lax.broadcasted_iota(jnp.int32, (LANES, LANES), 1)

    def body(b, carry):
        value = jnp.where(position() < counts[b], potential[block_rows(b), :] - offset, DEAD)
        high, middle, low = split3(value)
        for k in range(TILES):
            rows = jnp.where(
                sub == 3,
                high[k : k + 1, :],
                jnp.where(sub == 4, middle[k : k + 1, :], jnp.where(sub == 5, low[k : k + 1, :], 0.0)),
            )
            at = pl.ds(pl.multiple_of(b * BLOCK + k * LANES, LANES), LANES)
            x2f[at, :] = jnp.where(lane < 6, rows.T, x2[at, :].astype(F32)).astype(BF16)
        return carry

    lax.fori_loop(0, counts.shape[0], body, 0)


def update(parts, weight, counts, potential):
    def body(b, top):
        at = block_rows(b)
        value = LOG2E * weight[at, :] - merge([part[at, :] for part in parts])
        potential[at, :] = value
        return jnp.maximum(top, jnp.where(position() < counts[b], value, DEAD))

    return jnp.max(lax.fori_loop(0, counts.shape[0], body, jnp.full((TILES, LANES), DEAD, F32)))


def write_potential(potential, square, counts, embed, out):
    def body(b, carry):
        at = block_rows(b)
        value = potential[at, :] * (1.0 / POT) + square[at, :] * (1.0 / embed)
        out[at, :] = jnp.where(position() < counts[b], value, 0.0)
        return carry

    lax.fori_loop(0, counts.shape[0], body, 0)


def first_kernel(
    x, y, g0, pairs, count, sc, tc, out, x1, x2, yc, xsq, ysq, units, acc, tops, gamma, limit
):
    embed = x.shape[0]
    scale = 2.0 * POT / embed
    list_units(pairs, count, sc, tc, units)
    mark(0, pairs, count, sc, limit)

    def target(b, top):
        rows = []
        for k in range(TILES):
            at = pl.ds(pl.multiple_of(b * BLOCK + k * LANES, LANES), LANES)
            value = y[:, at]
            high, middle, low = split3(value)
            pieces = [high, middle, high, low, jnp.zeros((64, LANES), F32), high, middle]
            yc[:, at] = jnp.concatenate([p.astype(BF16) for p in pieces], axis=0)
            rows.append(jnp.sum(value * value, axis=0, keepdims=True))
        square = jnp.concatenate(rows, axis=0)
        ysq[block_rows(b), :] = square
        value = POT * g0[block_rows(b), :] - (POT / embed) * square
        gamma[block_rows(b), :] = value
        return jnp.maximum(top, jnp.where(position() < tc[b], value, DEAD))

    offset = jnp.max(lax.fori_loop(0, tc.shape[0], target, jnp.full((TILES, LANES), DEAD, F32)))
    put_in_columns(gamma, tc, offset, yc.at[128:144, :])

    def source(b, carry):
        rows = []
        sub = lax.broadcasted_iota(jnp.int32, (64, LANES), 0)
        ones = jnp.where(sub < 3, 1.0, 0.0)
        for k in range(TILES):
            at = pl.ds(pl.multiple_of(b * BLOCK + k * LANES, LANES), LANES)
            value = x[:, at]
            high, middle, low = split3(value * scale)
            x1[at, :] = jnp.concatenate([high, high, middle, high], axis=0).T.astype(BF16)
            x2[at, :] = jnp.concatenate([ones, low, middle], axis=0).T.astype(BF16)
            rows.append(jnp.sum(value * value, axis=0, keepdims=True))
        xsq[block_rows(b), :] = jnp.concatenate(rows, axis=0)
        return carry

    lax.fori_loop(0, sc.shape[0], source, 0)
    row_half(Scores(units, x1, x2, yc, None), limit, offset, out, acc, tops)


def col_kernel(parts_number, embed, *refs):
    parts = refs[:parts_number]
    (weight, square, pairs, count, sc, tc, units, x1, x2, yc) = refs[parts_number : parts_number + 10]
    out, f_out, acc, tops, x2f, phi, limit = refs[parts_number + 10 :]
    mark(1, pairs, count, tc, limit)
    offset = update(parts, weight, sc, phi)
    write_potential(phi, square, sc, embed, f_out)
    put_in_rows(phi, sc, offset, x2, x2f)
    col_half(Scores(units, x1, x2f, yc, None), limit, offset, out, acc, tops)


def row_kernel(parts_number, *refs):
    parts = refs[:parts_number]
    (weight, pairs, count, sc, tc, units, x1, x2, yc) = refs[parts_number : parts_number + 9]
    out, acc, tops, ye, gamma, limit = refs[parts_number + 9 :]
    mark(0, pairs, count, sc, limit)
    offset = update(parts, weight, tc, gamma)
    put_in_columns(gamma, tc, offset, ye)
    row_half(Scores(units, x1, x2, yc, ye), limit, offset, out, acc, tops)


def last_kernel(parts_number, embed, *refs):
    parts = refs[:parts_number]
    weight, square, tc, g_out, gamma = refs[parts_number:]
    update(parts, weight, tc, gamma)
    write_potential(gamma, square, tc, embed, g_out)


def exchange(value, axis):
    size = lax.axis_size(axis)

    def swap(value, turn):
        return lax.ppermute(value, axis, [(i, turn(i)) for i in range(size)])

    if size & (size - 1):
        return [value] + [swap(value, lambda i, k=k: (i + k) % size) for k in range(1, size)]
    parts = [value]
    bit = size
    while bit > 1:
        value = merge(parts) if len(parts) > 1 else parts[0]
        step = max(bit // 4, 1)
        masks = range(step, bit, step)
        parts = [value] + [swap(value, lambda i, m=m: i ^ m) for m in masks]
        bit = step
    return parts


def on_device(x, y, source_counts, target_counts, source_weight, target_weight, start, pair_blocks, pair_count):
    embed, source_len = x.shape
    target_len = y.shape[1]
    a = source_weight.reshape(-1, LANES)
    b = target_weight.reshape(-1, LANES)
    g0 = start.reshape(-1, LANES)
    slots = pair_blocks.shape[3]
    unit_slots = -(-slots * PER_BLOCK * PER_BLOCK // UNROLL) * UNROLL + 1
    vmem = pl.BlockSpec(memory_space=pltpu.VMEM)
    smem = pl.BlockSpec(memory_space=pltpu.SMEM)
    params = pltpu.CompilerParams(vmem_limit_bytes=VMEM_LIMIT)
    source_tile = jax.ShapeDtypeStruct((source_len // LANES, LANES), F32)
    target_tile = jax.ShapeDtypeStruct((target_len // LANES, LANES), F32)
    row_acc = pltpu.VMEM((source_len + CHUNK, LANES), F32)
    col_acc = pltpu.VMEM(((target_len // CHUNK + 1) * 8, CHUNK), F32)
    source_scratch = pltpu.VMEM(source_tile.shape, F32)
    target_scratch = pltpu.VMEM(target_tile.shape, F32)
    source_limit = pltpu.SMEM(source_counts.shape, jnp.int32)
    target_limit = pltpu.SMEM(target_counts.shape, jnp.int32)
    sizes = (pair_blocks, pair_count, source_counts, target_counts)

    part, x1, x2, yc, xsq, ysq, units = pl.pallas_call(
        first_kernel,
        in_specs=[vmem] * 3 + [smem] * 4,
        out_specs=[vmem] * 6 + [smem],
        out_shape=[
            source_tile,
            jax.ShapeDtypeStruct((source_len, 128), BF16),
            jax.ShapeDtypeStruct((source_len, 128), BF16),
            jax.ShapeDtypeStruct((256, target_len), BF16),
            source_tile,
            target_tile,
            jax.ShapeDtypeStruct((unit_slots,), jnp.int32),
        ],
        scratch_shapes=[row_acc, row_acc, target_scratch, source_limit],
        compiler_params=params,
        name="rows_first",
    )(x, y, g0, *sizes)
    common = (*sizes, units, x1, x2, yc)
    common_specs = [smem] * 5 + [vmem] * 3

    def columns(parts):
        return pl.pallas_call(
            lambda *refs: col_kernel(len(parts), embed, *refs),
            in_specs=[vmem] * (len(parts) + 2) + common_specs,
            out_specs=[vmem] * 2,
            out_shape=[target_tile, source_tile],
            scratch_shapes=[col_acc, col_acc, pltpu.VMEM((source_len, 128), BF16), source_scratch, target_limit],
            compiler_params=params,
            name="columns",
        )(*parts, a, xsq, *common)

    def rows(parts):
        return pl.pallas_call(
            lambda *refs: row_kernel(len(parts), *refs),
            in_specs=[vmem] * (len(parts) + 1) + common_specs,
            out_specs=vmem,
            out_shape=source_tile,
            scratch_shapes=[row_acc, row_acc, pltpu.VMEM((16, target_len), BF16), target_scratch, source_limit],
            compiler_params=params,
            name="rows",
        )(*parts, b, *common)

    part, _ = columns(exchange(part, "tgt"))
    part = rows(exchange(part, "src"))
    part, f = columns(exchange(part, "tgt"))
    parts = exchange(part, "src")
    g = pl.pallas_call(
        lambda *refs: last_kernel(len(parts), embed, *refs),
        in_specs=[vmem] * (len(parts) + 2) + [smem],
        out_specs=vmem,
        out_shape=target_tile,
        scratch_shapes=[target_scratch],
        compiler_params=params,
        name="last",
    )(*parts, b, ysq, target_counts)
    return f.reshape(-1), g.reshape(-1)


def solution(mesh):
    in_specs = (
        P(None, "src"),
        P(None, "tgt"),
        P("src"),
        P("tgt"),
        P("src"),
        P("tgt"),
        P("tgt"),
        P("src", "tgt", None, None),
        P("src", "tgt"),
    )
    out_specs = (P("src"), P("tgt"))
    return jax.shard_map(on_device, mesh=mesh, in_specs=in_specs, out_specs=out_specs, check_vma=False)
```

```python
import math

import jax
import jax.numpy as jnp
from jax import lax
from jax.experimental import pallas as pl
from jax.experimental.pallas import tpu as pltpu
from jax.sharding import PartitionSpec as P

F32 = jnp.float32
BF16 = jnp.bfloat16
BLOCK = 1024
LANES = 128
TILES = BLOCK // LANES
CHUNK = 256
PER_BLOCK = BLOCK // CHUNK
UNROLL = 16
BITS = 8
EXTRA = 96
DEAD = -1e30
LOW, HIGH = 2.0**-96, 2.0**120
ENTROPY = 0.1
LOG2E = math.log2(math.e)
POT = LOG2E / ENTROPY
VMEM_LIMIT = 20 * 1024 * 1024


def split3(value):
    high = value.astype(BF16).astype(F32)
    rest = value - high
    middle = rest.astype(BF16).astype(F32)
    return high, middle, rest - middle


def position():
    return lax.broadcasted_iota(jnp.int32, (TILES, LANES), 0) * LANES + lax.broadcasted_iota(
        jnp.int32, (TILES, LANES), 1
    )


def block_rows(b):
    return pl.ds(pl.multiple_of(b * TILES, TILES), TILES)


def lane_tile(b, k):
    return pl.ds(pl.multiple_of(b * BLOCK + k * LANES, LANES), LANES)


def row_chunk(row):
    return pl.ds(pl.multiple_of(row * CHUNK, CHUNK), CHUNK)


def col_chunk(col):
    return pl.ds(pl.multiple_of(col * 8, 8), 8)


def merge(parts):
    top = parts[0]
    for part in parts[1:]:
        top = jnp.maximum(top, part)
    total = jnp.exp2(parts[0] - top)
    for part in parts[1:]:
        total = total + jnp.exp2(part - top)
    return top + jnp.log2(total)


class Table:
    def __init__(self, slots, sources, targets):
        most = (slots * PER_BLOCK * PER_BLOCK + 1) // 2 + sources * PER_BLOCK
        self.sources, self.targets = sources, targets
        self.steps = -(-most // UNROLL) * UNROLL
        self.source_count = self.steps + 1
        self.target_count = self.source_count + sources
        self.source_limit = self.target_count + targets
        self.target_limit = self.source_limit + sources
        self.size = self.target_limit + targets

    def fill(self, pairs, count, source_counts, target_counts, table, columns):
        number = count[0, 0]
        nowhere = self.targets * PER_BLOCK

        def clear_source(b, carry):
            table[self.source_count + b] = source_counts[b]
            table[self.source_limit + b] = 0
            return carry

        def clear_target(b, carry):
            table[self.target_count + b] = target_counts[b]
            table[self.target_limit + b] = 0
            return carry

        lax.fori_loop(0, self.sources, clear_source, 0)
        lax.fori_loop(0, self.targets, clear_target, 0)

        def touch(p, carry):
            sb, tb = pairs[0, 0, 0, p], pairs[0, 0, 1, p]
            table[self.source_limit + sb] = source_counts[sb]
            table[self.target_limit + tb] = target_counts[tb]
            return carry

        lax.fori_loop(0, number, touch, 0)

        def source(sb, n):
            def pair(p, m):
                def take(m):
                    tb = pairs[0, 0, 1, p]
                    chunks = (target_counts[tb] + CHUNK - 1) // CHUNK

                    def put(c, carry):
                        columns[m + c] = tb * PER_BLOCK + c
                        return carry

                    lax.fori_loop(0, chunks, put, 0)
                    return m + chunks

                return lax.cond(pairs[0, 0, 0, p] == sb, take, lambda m: m, m)

            m = lax.fori_loop(0, number, pair, 0)
            columns[m] = nowhere
            twos = (m + 1) // 2

            def row(r, n):
                base = (sb * PER_BLOCK + r) << (2 * BITS)

                def put(c, carry):
                    table[n + c] = base + (columns[2 * c] << BITS) + columns[2 * c + 1]
                    return carry

                lax.fori_loop(0, twos, put, 0)
                return n + twos

            return lax.fori_loop(0, (source_counts[sb] + CHUNK - 1) // CHUNK, row, n)

        n = lax.fori_loop(0, self.sources, source, 0)
        steps = (n + UNROLL - 1) // UNROLL

        def fill(i, carry):
            table[i] = (nowhere << BITS) + nowhere
            return carry

        lax.fori_loop(n, steps * UNROLL, fill, 0)
        table[self.steps] = steps


class Scores:
    def __init__(self, table, at, x1, x2, y, ye):
        self.table, self.place, self.x1, self.x2, self.y, self.ye = table, at, x1, x2, y, ye

    def unit(self, t):
        unit = self.table[t]
        mask = (1 << BITS) - 1
        row, cols = unit >> (2 * BITS), ((unit >> BITS) & mask, unit & mask)
        at = row_chunk(row)
        lhs = jnp.concatenate([self.x1[at, :], self.x2[at, :]], axis=1)
        values = []
        for col in cols:
            at = pl.ds(pl.multiple_of(col * CHUNK, CHUNK), CHUNK)
            if self.ye is None:
                rhs = self.y[:, at]
            else:
                rhs = [self.y[0:EXTRA, at], self.ye[:, at], self.y[EXTRA + 16 :, at]]
                rhs = jnp.concatenate(rhs, axis=0)
            values.append(jnp.dot(lhs, rhs, preferred_element_type=F32))
        return row, cols, values

    def each(self, body, unroll):
        def step(s, carry):
            for u in range(unroll):
                body(*self.unit(s * unroll + u))
            return carry

        lax.fori_loop(0, self.table[self.place.steps] * (UNROLL // unroll), step, 0)


def fill_ref(ref, rows, value):
    def body(i, carry):
        ref[pl.ds(pl.multiple_of(i * rows, rows), rows), :] = jnp.full((rows, ref.shape[1]), value, F32)
        return carry

    lax.fori_loop(0, ref.shape[0] // rows, body, 0)


def check(total, limit):
    fine = (total >= LOW) & (total <= HIGH)
    return jnp.where(fine | (position() >= limit), 0.0, 1.0)


def row_sums(acc, b):
    rows = [jnp.sum(acc[lane_tile(b, r), :].T, axis=0, keepdims=True) for r in range(TILES)]
    return jnp.concatenate(rows, axis=0)


def across(values, combine):
    parts = [v[:, k * LANES : (k + 1) * LANES] for v in values for k in range(CHUNK // LANES)]
    while len(parts) > 1:
        parts = [combine(a, b) for a, b in zip(parts[::2], parts[1::2])]
    return parts[0]


def row_half(scores, offset, out, acc, tops):
    blocks = out.shape[0] // TILES
    fill_ref(acc, CHUNK, 0.0)

    def add(row, cols, values):
        acc[row_chunk(row), :] += across([jnp.exp2(v) for v in values], jnp.add)

    scores.each(add, UNROLL)

    def finish(b, bad):
        total = row_sums(acc, b)
        out[block_rows(b), :] = jnp.where(total > 0.0, offset + jnp.log2(total), DEAD)
        return jnp.maximum(bad, check(total, scores.table[scores.place.source_limit + b]))

    bad = lax.fori_loop(0, blocks, finish, jnp.zeros((TILES, LANES), F32), unroll=2)

    @pl.when(jnp.max(bad) > 0.0)
    def _():
        fill_ref(acc, CHUNK, DEAD)

        def highest(row, cols, values):
            acc[row_chunk(row), :] = jnp.maximum(acc[row_chunk(row), :], across(values, jnp.maximum))

        scores.each(highest, 1)

        def spread(i, carry):
            top = jnp.max(acc[row_chunk(i), :], axis=1, keepdims=True)
            top = jnp.where(top > 0.5 * DEAD, top, 0.0)
            tops[row_chunk(i), :] = jnp.broadcast_to(top, (CHUNK, LANES))
            return carry

        lax.fori_loop(0, acc.shape[0] // CHUNK, spread, 0)
        fill_ref(acc, CHUNK, 0.0)

        def add_below(row, cols, values):
            top = tops[row_chunk(row), :]
            top = jnp.concatenate([top] * (CHUNK // LANES), axis=1)
            acc[row_chunk(row), :] += across([jnp.exp2(v - top) for v in values], jnp.add)

        scores.each(add_below, 1)

        def finish_below(b, carry):
            total = row_sums(acc, b)
            top = jnp.concatenate([tops[lane_tile(b, r), :].T[0:1, :] for r in range(TILES)], axis=0)
            out[block_rows(b), :] = jnp.where(total > 0.0, (offset + top) + jnp.log2(total), DEAD)
            return carry

        lax.fori_loop(0, blocks, finish_below, 0)


def col_tile(acc, b, reduce):
    rows = []
    for c in range(PER_BLOCK):
        line = reduce(acc[col_chunk(b * PER_BLOCK + c), :], axis=0, keepdims=True)
        for k in range(CHUNK // LANES):
            rows.append(line[:, k * LANES : (k + 1) * LANES])
    return jnp.concatenate(rows, axis=0)


def col_half(scores, offset, out, acc, tops):
    blocks = out.shape[0] // TILES
    fill_ref(acc, 8, 0.0)

    def add(row, cols, values):
        for col, value in zip(cols, values):
            acc[col_chunk(col), :] += jnp.sum(jnp.exp2(value).reshape(CHUNK // 8, 8, CHUNK), axis=0)

    scores.each(add, UNROLL)

    def finish(b, bad):
        total = col_tile(acc, b, jnp.sum)
        out[block_rows(b), :] = jnp.where(total > 0.0, offset + jnp.log2(total), DEAD)
        return jnp.maximum(bad, check(total, scores.table[scores.place.target_limit + b]))

    bad = lax.fori_loop(0, blocks, finish, jnp.zeros((TILES, LANES), F32), unroll=4)

    @pl.when(jnp.max(bad) > 0.0)
    def _():
        fill_ref(tops, 8, DEAD)

        def highest(row, cols, values):
            for col, value in zip(cols, values):
                part = jnp.max(value.reshape(CHUNK // 8, 8, CHUNK), axis=0)
                tops[col_chunk(col), :] = jnp.maximum(tops[col_chunk(col), :], part)

        scores.each(highest, 1)

        def spread(i, carry):
            top = jnp.max(tops[col_chunk(i), :], axis=0, keepdims=True)
            top = jnp.where(top > 0.5 * DEAD, top, 0.0)
            tops[col_chunk(i), :] = jnp.broadcast_to(top, (8, CHUNK))
            return carry

        lax.fori_loop(0, tops.shape[0] // 8, spread, 0)
        fill_ref(acc, 8, 0.0)

        def add_below(row, cols, values):
            for col, value in zip(cols, values):
                e = jnp.exp2(value.reshape(CHUNK // 8, 8, CHUNK) - tops[col_chunk(col), :][None])
                acc[col_chunk(col), :] += jnp.sum(e, axis=0)

        scores.each(add_below, 1)

        def finish_below(b, carry):
            total = col_tile(acc, b, jnp.sum)
            top = col_tile(tops, b, jnp.max)
            out[block_rows(b), :] = jnp.where(total > 0.0, (offset + top) + jnp.log2(total), DEAD)
            return carry

        lax.fori_loop(0, blocks, finish_below, 0)


def put_in_columns(potential, table, start, blocks, offset, ye):
    sub = lax.broadcasted_iota(jnp.int32, (16, LANES), 0)

    def body(b, carry):
        value = jnp.where(position() < table[start + b], potential[block_rows(b), :] - offset, DEAD)
        high, middle, low = split3(value)
        for k in range(TILES):
            at = slice(k, k + 1)
            rows = jnp.where(sub == 1, middle[at, :], jnp.where(sub == 2, low[at, :], 0.0))
            ye[:, lane_tile(b, k)] = jnp.where(sub == 0, high[at, :], rows).astype(BF16)
        return carry

    lax.fori_loop(0, blocks, body, 0, unroll=2)
    for k in range(CHUNK // LANES):
        at = pl.ds(blocks * BLOCK + k * LANES, LANES)
        ye[:, at] = jnp.where(sub == 0, DEAD, 0.0).astype(BF16)


def put_in_rows(potential, table, start, blocks, offset, x1, x1f):
    sub = lax.broadcasted_iota(jnp.int32, (8, LANES), 0)
    above = jnp.zeros((EXTRA, LANES), F32)
    below = jnp.zeros((LANES - EXTRA - 8, LANES), F32)

    def body(b, carry):
        value = jnp.where(position() < table[start + b], potential[block_rows(b), :] - offset, DEAD)
        high, middle, low = split3(value)
        for k in range(TILES):
            at = slice(k, k + 1)
            rows = jnp.where(sub == 4, middle[at, :], jnp.where(sub == 5, low[at, :], 0.0))
            rows = jnp.where(sub == 3, high[at, :], rows)
            turned = jnp.concatenate([above, rows, below], axis=0).T.astype(BF16)
            x1f[lane_tile(b, k), :] = x1[lane_tile(b, k), :] + turned
        return carry

    lax.fori_loop(0, blocks, body, 0)


def update(parts, weight, table, start, blocks, potential):
    def body(b, top):
        at = block_rows(b)
        value = LOG2E * weight[at, :] - merge([part[at, :] for part in parts])
        potential[at, :] = value
        return jnp.maximum(top, jnp.where(position() < table[start + b], value, DEAD))

    return jnp.max(lax.fori_loop(0, blocks, body, jnp.full((TILES, LANES), DEAD, F32), unroll=4))


def first_kernel(
    place,
    count, x_hbm, y_hbm, g0_hbm, b_hbm, pairs_hbm, sc_hbm, tc_hbm,
    out, x1, x2, yc, xsq, base, table,
    acc, tops, ye, gamma, x, y, g0, weight, pairs, sc, tc, columns, sems,
):
    embed = x.shape[0]
    scale = 2.0 * POT / embed
    here = [(pairs_hbm, pairs), (sc_hbm, sc), (tc_hbm, tc)]
    here += [(y_hbm, y), (g0_hbm, g0), (b_hbm, weight), (x_hbm, x)]
    copies = [pltpu.make_async_copy(a, b, sems.at[i]) for i, (a, b) in enumerate(here)]
    for copy in copies:
        copy.start()
    for copy in copies[:3]:
        copy.wait()
    place.fill(pairs, count, sc, tc, table, columns)
    for copy in copies[3:6]:
        copy.wait()
    sub = lax.broadcasted_iota(jnp.int32, (LANES - EXTRA, LANES), 0)
    static = jnp.where((sub >= 3) & (sub < 6), 1.0, 0.0)
    zero = jnp.zeros((LANES - EXTRA, LANES), F32)

    def target(b, top):
        rows = []
        for k in range(TILES):
            at = lane_tile(b, k)
            value = y[:, at]
            high, middle, low = split3(value)
            pieces = [high, high, high, static, middle, middle, low, zero]
            yc[:, at] = jnp.concatenate([p.astype(BF16) for p in pieces], axis=0)
            rows.append(jnp.sum(value * value, axis=0, keepdims=True))
        square = jnp.concatenate(rows, axis=0)
        live = position() < tc[b]
        at = block_rows(b)
        base[at, :] = jnp.where(live, ENTROPY * weight[at, :] + (1.0 / embed) * square, DEAD)
        value = POT * g0[at, :] - (POT / embed) * square
        gamma[at, :] = value
        return jnp.maximum(top, jnp.where(live, value, DEAD))

    blocks = tc.shape[0]
    offset = jnp.max(lax.fori_loop(0, blocks, target, jnp.full((TILES, LANES), DEAD, F32)))
    for k in range(CHUNK // LANES):
        at = pl.ds(blocks * BLOCK + k * LANES, LANES)
        pieces = [zero, zero, zero, static, zero, zero, zero, zero]
        yc[:, at] = jnp.concatenate([p.astype(BF16) for p in pieces], axis=0)
    put_in_columns(gamma, table, place.target_count, blocks, offset, ye)
    copies[6].wait()
    ones = jnp.where(sub < 3, 1.0, 0.0)
    lane = lax.broadcasted_iota(jnp.int32, (LANES, LANES), 1)

    def source(b, carry):
        rows = []
        for k in range(TILES):
            at = lane_tile(b, k)
            value = x[:, at]
            high, middle, low = split3(value * scale)
            turned = jnp.concatenate([high, middle, low, ones], axis=0).T
            x1[at, :] = turned.astype(BF16)
            x2[at, :] = jnp.where(lane < 64, turned, pltpu.roll(turned, 64, 1)).astype(BF16)
            rows.append(jnp.sum(value * value, axis=0, keepdims=True))
        xsq[block_rows(b), :] = jnp.concatenate(rows, axis=0)
        return carry

    lax.fori_loop(0, sc.shape[0], source, 0)
    row_half(Scores(table, place, x1, x2, yc, ye), offset, out, acc, tops)


def col_kernel(place, number, embed, final, *refs):
    parts = refs[:number]
    weight, square, table, x1, x2, yc, out = refs[number : number + 7]
    rest = list(refs[number + 7 :])
    f_hbm = rest.pop(0) if final else None
    acc, tops, x1f, phi = rest[:4]
    blocks, start = place.sources, place.source_count
    offset = update(parts, weight, table, start, blocks, phi)
    if final:
        f_out, sem = rest[4:]

        def write(b, carry):
            at = block_rows(b)
            value = phi[at, :] * (1.0 / POT) + square[at, :] * (1.0 / embed)
            f_out[at, :] = jnp.where(position() < table[start + b], value, 0.0)
            return carry

        lax.fori_loop(0, blocks, write, 0, unroll=2)
        copy = pltpu.make_async_copy(f_out, f_hbm, sem)
        copy.start()
    put_in_rows(phi, table, start, blocks, offset, x1, x1f)
    col_half(Scores(table, place, x1f, x2, yc, None), offset, out, acc, tops)
    if final:
        copy.wait()


def row_kernel(place, number, *refs):
    parts = refs[:number]
    weight, table, x1, x2, yc, out, acc, tops, ye, gamma = refs[number:]
    blocks, start = place.targets, place.target_count
    offset = update(parts, weight, table, start, blocks, gamma)
    put_in_columns(gamma, table, start, blocks, offset, ye)
    row_half(Scores(table, place, x1, x2, yc, ye), offset, out, acc, tops)


def exchange(value, axis):
    size = lax.axis_size(axis)

    def swap(value, turn):
        return lax.ppermute(value, axis, [(i, turn(i)) for i in range(size)])

    if size & (size - 1):
        return [value] + [swap(value, lambda i, k=k: (i + k) % size) for k in range(1, size)]
    parts = [value]
    bit = size
    while bit > 1:
        value = merge(parts) if len(parts) > 1 else parts[0]
        step = max(bit // 4, 1)
        masks = range(step, bit, step)
        parts = [value] + [swap(value, lambda i, m=m: i ^ m) for m in masks]
        bit = step
    return parts


def on_device(x, y, source_counts, target_counts, source_weight, target_weight, start, pair_blocks, pair_count):
    embed, source_len = x.shape
    target_len = y.shape[1]
    a = source_weight.reshape(-1, LANES)
    b = target_weight.reshape(-1, LANES)
    g0 = start.reshape(-1, LANES)
    slots = pair_blocks.shape[3]
    place = Table(slots, source_counts.shape[0], target_counts.shape[0])
    vmem = pl.BlockSpec(memory_space=pltpu.VMEM)
    smem = pl.BlockSpec(memory_space=pltpu.SMEM)
    hbm = pl.BlockSpec(memory_space=pltpu.HBM)
    params = pltpu.CompilerParams(vmem_limit_bytes=VMEM_LIMIT)
    source_tile = jax.ShapeDtypeStruct((source_len // LANES, LANES), F32)
    target_tile = jax.ShapeDtypeStruct((target_len // LANES, LANES), F32)
    row_acc = pltpu.VMEM((source_len, LANES), F32)
    col_acc = pltpu.VMEM(((target_len // CHUNK + 1) * 8, CHUNK), F32)
    source_scratch = pltpu.VMEM(source_tile.shape, F32)
    target_scratch = pltpu.VMEM(target_tile.shape, F32)
    columns_extra = pltpu.VMEM((16, target_len + CHUNK), BF16)

    def smem_like(value):
        return pltpu.SMEM(value.shape, value.dtype)

    first = (x, y, g0, b, pair_blocks, source_counts, target_counts)
    part, x1, x2, yc, xsq, base, table = pl.pallas_call(
        lambda *refs: first_kernel(place, *refs),
        in_specs=[smem] + [hbm] * 7,
        out_specs=[vmem] * 6 + [smem],
        out_shape=[
            source_tile,
            jax.ShapeDtypeStruct((source_len, LANES), BF16),
            jax.ShapeDtypeStruct((source_len, LANES), BF16),
            jax.ShapeDtypeStruct((2 * LANES, target_len + CHUNK), BF16),
            source_tile,
            target_tile,
            jax.ShapeDtypeStruct((place.size,), jnp.int32),
        ],
        scratch_shapes=[
            row_acc,
            row_acc,
            columns_extra,
            target_scratch,
            pltpu.VMEM(x.shape, F32),
            pltpu.VMEM(y.shape, F32),
            target_scratch,
            target_scratch,
            smem_like(pair_blocks),
            smem_like(source_counts),
            smem_like(target_counts),
            pltpu.SMEM((slots * PER_BLOCK + 1,), jnp.int32),
            pltpu.SemaphoreType.DMA((7,)),
        ],
        compiler_params=params,
        name="rows_first",
    )(pair_count, *[pltpu.with_memory_space_constraint(v, pltpu.HBM) for v in first])
    common = (table, x1, x2, yc)
    common_specs = [smem] + [vmem] * 3

    def columns(parts, final):
        scratch = [col_acc, col_acc, pltpu.VMEM((source_len, LANES), BF16), source_scratch]
        return pl.pallas_call(
            lambda *refs: col_kernel(place, len(parts), embed, final, *refs),
            in_specs=[vmem] * (len(parts) + 2) + common_specs,
            out_specs=[vmem, hbm] if final else [vmem],
            out_shape=[target_tile, source_tile] if final else [target_tile],
            scratch_shapes=scratch + ([source_scratch, pltpu.SemaphoreType.DMA] if final else []),
            compiler_params=params,
            name="columns",
        )(*parts, a, xsq, *common)

    def rows(parts):
        return pl.pallas_call(
            lambda *refs: row_kernel(place, len(parts), *refs),
            in_specs=[vmem] * (len(parts) + 1) + common_specs,
            out_specs=vmem,
            out_shape=source_tile,
            scratch_shapes=[row_acc, row_acc, columns_extra, target_scratch],
            compiler_params=params,
            name="rows",
        )(*parts, b, *common)

    (part,) = columns(exchange(part, "tgt"), False)
    part = rows(exchange(part, "src"))
    part, f = columns(exchange(part, "tgt"), True)
    merged = merge(exchange(part, "src"))
    g = jnp.where(base > 0.5 * DEAD, base - merged * (1.0 / POT), 0.0)
    return f.reshape(-1), g.reshape(-1)


def solution(mesh):
    in_specs = (
        P(None, "src"),
        P(None, "tgt"),
        P("src"),
        P("tgt"),
        P("src"),
        P("tgt"),
        P("tgt"),
        P("src", "tgt", None, None),
        P("src", "tgt"),
    )
    out_specs = (P("src"), P("tgt"))
    return jax.shard_map(on_device, mesh=mesh, in_specs=in_specs, out_specs=out_specs, check_vma=False)
```

```python
import math

import jax
import jax.numpy as jnp
from jax import lax
from jax.experimental import pallas as pl
from jax.experimental.pallas import tpu as pltpu
from jax.sharding import PartitionSpec as P

F32 = jnp.float32
BF16 = jnp.bfloat16
BLOCK = 1024
LANES = 128
TILES = BLOCK // LANES
CHUNK = 256
PER_BLOCK = BLOCK // CHUNK
UNROLL = 16
BITS = 8
EXTRA = 96
DEAD = -1e30
LOW, HIGH = 2.0**-96, 2.0**120
ENTROPY = 0.1
LOG2E = math.log2(math.e)
POT = LOG2E / ENTROPY
VMEM_LIMIT = 20 * 1024 * 1024


def split3(value):
    high = value.astype(BF16).astype(F32)
    rest = value - high
    middle = rest.astype(BF16).astype(F32)
    return high, middle, rest - middle


def position():
    return lax.broadcasted_iota(jnp.int32, (TILES, LANES), 0) * LANES + lax.broadcasted_iota(
        jnp.int32, (TILES, LANES), 1
    )


def block_rows(b):
    return pl.ds(pl.multiple_of(b * TILES, TILES), TILES)


def lane_tile(b, k):
    return pl.ds(pl.multiple_of(b * BLOCK + k * LANES, LANES), LANES)


def row_chunk(row):
    return pl.ds(pl.multiple_of(row * CHUNK, CHUNK), CHUNK)


def col_chunk(col):
    return pl.ds(pl.multiple_of(col * 8, 8), 8)


def merge(parts):
    top = parts[0]
    for part in parts[1:]:
        top = jnp.maximum(top, part)
    total = jnp.exp2(parts[0] - top)
    for part in parts[1:]:
        total = total + jnp.exp2(part - top)
    return top + jnp.log2(total)


class Table:
    def __init__(self, slots, sources, targets):
        most = (slots * PER_BLOCK * PER_BLOCK + 1) // 2 + sources * PER_BLOCK
        self.sources, self.targets = sources, targets
        self.source_limit = 1
        self.target_limit = self.source_limit + sources
        self.units = self.target_limit + targets
        self.size = self.units + -(-most // UNROLL) * UNROLL
        self.columns = slots * PER_BLOCK + sources

    def fill(self, pairs, count, source_counts, target_counts, table, columns, wanted, place):
        number = count[0, 0]
        nowhere = self.targets * PER_BLOCK

        for i in range(self.units):
            table[i] = 0
        for b in range(self.sources):
            wanted[b] = 0

        def chunks_of(live):
            return (live + CHUNK - 1) // CHUNK

        def measure(p, carry):
            sb, tb = pairs[0, 0, 0, p], pairs[0, 0, 1, p]
            table[self.source_limit + sb] = source_counts[sb]
            table[self.target_limit + tb] = target_counts[tb]
            wanted[sb] += chunks_of(target_counts[tb])
            return carry

        lax.fori_loop(0, number, measure, 0)
        m = 0
        starts = []
        for b in range(self.sources):
            starts.append(m)
            place[b] = m
            columns[m + wanted[b]] = nowhere
            m = m + wanted[b] + (wanted[b] & 1)

        def put(p, carry):
            sb, tb = pairs[0, 0, 0, p], pairs[0, 0, 1, p]
            start = place[sb]
            chunks = chunks_of(target_counts[tb])
            for c in range(PER_BLOCK):
                columns[jnp.where(c < chunks, start + c, self.columns)] = tb * PER_BLOCK + c
            place[sb] = start + chunks
            return carry

        lax.fori_loop(0, number, put, 0)
        n = self.units
        for b in range(self.sources):
            twos = (wanted[b] + 1) >> 1
            rows = [((b * PER_BLOCK + r) << (2 * BITS)) for r in range(PER_BLOCK)]

            def emit(c, carry, first=starts[b], n=n, twos=twos, rows=rows):
                word = (columns[first + 2 * c] << BITS) + columns[first + 2 * c + 1]
                for r in range(PER_BLOCK):
                    table[n + r * twos + c] = rows[r] + word
                return carry

            lax.fori_loop(0, twos, emit, 0)
            n = n + twos * chunks_of(source_counts[b])
        steps = (n - self.units + UNROLL - 1) // UNROLL

        def fill(i, carry):
            table[i] = (nowhere << BITS) + nowhere
            return carry

        lax.fori_loop(n, self.units + steps * UNROLL, fill, 0)
        table[0] = steps


class Scores:
    def __init__(self, table, place, x1, x2, y, ye):
        self.table, self.place, self.x1, self.x2, self.y, self.ye = table, place, x1, x2, y, ye
        self.zero = jnp.zeros((LANES - EXTRA, CHUNK), BF16)
        sub = lax.broadcasted_iota(jnp.int32, (LANES - EXTRA, CHUNK), 0)
        self.static = jnp.where((sub >= 3) & (sub < 6), 1.0, 0.0).astype(BF16)

    def unit(self, t):
        unit = self.table[self.place.units + t]
        mask = (1 << BITS) - 1
        row, cols = unit >> (2 * BITS), ((unit >> BITS) & mask, unit & mask)
        at = row_chunk(row)
        lhs = jnp.concatenate([self.x1[at, :], self.x2[at, :]], axis=1)
        values = []
        part = self.y.shape[0] // 3
        for col in cols:
            at = pl.ds(pl.multiple_of(col * CHUNK, CHUNK), CHUNK)
            high, middle, low = (self.y[k * part : (k + 1) * part, at] for k in range(3))
            extra = [self.static] if self.ye is None else [self.ye[:, at], self.zero[16:]]
            rhs = jnp.concatenate([high, high, high, *extra, middle, middle, low, self.zero], axis=0)
            values.append(jnp.dot(lhs, rhs, preferred_element_type=F32))
        return row, cols, values

    def each(self, body, unroll):
        def step(s, carry):
            for u in range(unroll):
                body(*self.unit(s * unroll + u))
            return carry

        lax.fori_loop(0, self.table[0] * (UNROLL // unroll), step, 0)


def fill_ref(ref, rows, value):
    def body(i, carry):
        ref[pl.ds(pl.multiple_of(i * rows, rows), rows), :] = jnp.full((rows, ref.shape[1]), value, F32)
        return carry

    lax.fori_loop(0, ref.shape[0] // rows, body, 0)


def check(total, limit):
    fine = (total >= LOW) & (total <= HIGH)
    return jnp.where(fine | (position() >= limit), 0.0, 1.0)


def row_sums(acc, b):
    rows = [jnp.sum(acc[lane_tile(b, r), :].T, axis=0, keepdims=True) for r in range(TILES)]
    return jnp.concatenate(rows, axis=0)


def across(values, combine):
    parts = [v[:, k * LANES : (k + 1) * LANES] for v in values for k in range(CHUNK // LANES)]
    while len(parts) > 1:
        parts = [combine(a, b) for a, b in zip(parts[::2], parts[1::2])]
    return parts[0]


def row_half(scores, offset, out, acc, tops):
    blocks = out.shape[0] // TILES
    fill_ref(acc, CHUNK, 0.0)

    def add(row, cols, values):
        acc[row_chunk(row), :] += across([jnp.exp2(v) for v in values], jnp.add)

    scores.each(add, UNROLL)

    def finish(b, bad):
        total = row_sums(acc, b)
        out[block_rows(b), :] = jnp.where(total > 0.0, offset + jnp.log2(total), DEAD)
        return jnp.maximum(bad, check(total, scores.table[scores.place.source_limit + b]))

    bad = lax.fori_loop(0, blocks, finish, jnp.zeros((TILES, LANES), F32), unroll=2)

    @pl.when(jnp.max(bad) > 0.0)
    def _():
        fill_ref(acc, CHUNK, DEAD)

        def highest(row, cols, values):
            acc[row_chunk(row), :] = jnp.maximum(acc[row_chunk(row), :], across(values, jnp.maximum))

        scores.each(highest, 1)

        def spread(i, carry):
            top = jnp.max(acc[row_chunk(i), :], axis=1, keepdims=True)
            top = jnp.where(top > 0.5 * DEAD, top, 0.0)
            tops[row_chunk(i), :] = jnp.broadcast_to(top, (CHUNK, LANES))
            return carry

        lax.fori_loop(0, acc.shape[0] // CHUNK, spread, 0)
        fill_ref(acc, CHUNK, 0.0)

        def add_below(row, cols, values):
            top = tops[row_chunk(row), :]
            top = jnp.concatenate([top] * (CHUNK // LANES), axis=1)
            acc[row_chunk(row), :] += across([jnp.exp2(v - top) for v in values], jnp.add)

        scores.each(add_below, 1)

        def finish_below(b, carry):
            total = row_sums(acc, b)
            top = jnp.concatenate([tops[lane_tile(b, r), :].T[0:1, :] for r in range(TILES)], axis=0)
            out[block_rows(b), :] = jnp.where(total > 0.0, (offset + top) + jnp.log2(total), DEAD)
            return carry

        lax.fori_loop(0, blocks, finish_below, 0)


def col_tile(acc, b, reduce):
    rows = []
    for c in range(PER_BLOCK):
        line = reduce(acc[col_chunk(b * PER_BLOCK + c), :], axis=0, keepdims=True)
        for k in range(CHUNK // LANES):
            rows.append(line[:, k * LANES : (k + 1) * LANES])
    return jnp.concatenate(rows, axis=0)


def col_half(scores, offset, out, acc, tops):
    blocks = out.shape[0] // TILES
    fill_ref(acc, 8, 0.0)

    def add(row, cols, values):
        for col, value in zip(cols, values):
            acc[col_chunk(col), :] += jnp.sum(jnp.exp2(value).reshape(CHUNK // 8, 8, CHUNK), axis=0)

    scores.each(add, UNROLL)

    def finish(b, bad):
        total = col_tile(acc, b, jnp.sum)
        out[block_rows(b), :] = jnp.where(total > 0.0, offset + jnp.log2(total), DEAD)
        return jnp.maximum(bad, check(total, scores.table[scores.place.target_limit + b]))

    bad = lax.fori_loop(0, blocks, finish, jnp.zeros((TILES, LANES), F32), unroll=4)

    @pl.when(jnp.max(bad) > 0.0)
    def _():
        fill_ref(tops, 8, DEAD)

        def highest(row, cols, values):
            for col, value in zip(cols, values):
                part = jnp.max(value.reshape(CHUNK // 8, 8, CHUNK), axis=0)
                tops[col_chunk(col), :] = jnp.maximum(tops[col_chunk(col), :], part)

        scores.each(highest, 1)

        def spread(i, carry):
            top = jnp.max(tops[col_chunk(i), :], axis=0, keepdims=True)
            top = jnp.where(top > 0.5 * DEAD, top, 0.0)
            tops[col_chunk(i), :] = jnp.broadcast_to(top, (8, CHUNK))
            return carry

        lax.fori_loop(0, tops.shape[0] // 8, spread, 0)
        fill_ref(acc, 8, 0.0)

        def add_below(row, cols, values):
            for col, value in zip(cols, values):
                e = jnp.exp2(value.reshape(CHUNK // 8, 8, CHUNK) - tops[col_chunk(col), :][None])
                acc[col_chunk(col), :] += jnp.sum(e, axis=0)

        scores.each(add_below, 1)

        def finish_below(b, carry):
            total = col_tile(acc, b, jnp.sum)
            top = col_tile(tops, b, jnp.max)
            out[block_rows(b), :] = jnp.where(total > 0.0, (offset + top) + jnp.log2(total), DEAD)
            return carry

        lax.fori_loop(0, blocks, finish_below, 0)


def put_in_columns(potential, offset, ye):
    sub = lax.broadcasted_iota(jnp.int32, (16, LANES), 0)
    blocks = potential.shape[0] // TILES

    def body(b, carry):
        high, middle, low = split3(potential[block_rows(b), :] - offset)
        for k in range(TILES):
            at = slice(k, k + 1)
            rows = jnp.where(sub == 1, middle[at, :], jnp.where(sub == 2, low[at, :], 0.0))
            ye[:, lane_tile(b, k)] = jnp.where(sub == 0, high[at, :], rows).astype(BF16)
        return carry

    lax.fori_loop(0, blocks, body, 0, unroll=2)
    for k in range(CHUNK // LANES):
        at = pl.ds(blocks * BLOCK + k * LANES, LANES)
        ye[:, at] = jnp.where(sub == 0, DEAD, 0.0).astype(BF16)


def put_in_rows(potential, offset, x1, x1f):
    sub = lax.broadcasted_iota(jnp.int32, (8, LANES), 0)
    above = jnp.zeros((EXTRA, LANES), F32)
    below = jnp.zeros((LANES - EXTRA - 8, LANES), F32)

    def body(b, carry):
        high, middle, low = split3(potential[block_rows(b), :] - offset)
        for k in range(TILES):
            at = slice(k, k + 1)
            rows = jnp.where(sub == 4, middle[at, :], jnp.where(sub == 5, low[at, :], 0.0))
            rows = jnp.where(sub == 3, high[at, :], rows)
            turned = jnp.concatenate([above, rows, below], axis=0).T.astype(BF16)
            x1f[lane_tile(b, k), :] = x1[lane_tile(b, k), :] + turned
        return carry

    lax.fori_loop(0, potential.shape[0] // TILES, body, 0)


def update(parts, weight, potential):
    weight = weight[...]
    value = jnp.where(weight > 0.5 * DEAD, weight - merge([part[...] for part in parts]), DEAD)
    potential[...] = value
    return jnp.max(value)


def first_kernel(
    place,
    count, x_hbm, y_hbm, g0_hbm, b_hbm, a_hbm, pairs_hbm, sc_hbm, tc_hbm,
    out, x1, x2, yc, xsq, aw, base, bw, table_out,
    acc, tops, ye, gamma, x, y, g0, b_in, a_in, pairs, sc, tc, columns, wanted, places, table, sems,
):
    embed = x.shape[0]
    scale = 2.0 * POT / embed
    here = [(pairs_hbm, pairs), (sc_hbm, sc), (tc_hbm, tc)]
    here += [(y_hbm, y), (g0_hbm, g0), (b_hbm, b_in), (x_hbm, x), (a_hbm, a_in)]
    copies = [pltpu.make_async_copy(a, b, sems.at[i]) for i, (a, b) in enumerate(here)]
    for copy in copies:
        copy.start()
    for copy in copies[:3]:
        copy.wait()
    place.fill(pairs, count, sc, tc, table, columns, wanted, places)
    keep = pltpu.make_async_copy(table, table_out, sems.at[len(copies)])
    keep.start()
    for copy in copies[3:6]:
        copy.wait()

    def target(b, top):
        rows = []
        for k in range(TILES):
            at = lane_tile(b, k)
            value = y[:, at]
            yc[:, at] = jnp.concatenate([p.astype(BF16) for p in split3(value)], axis=0)
            rows.append(jnp.sum(value * value, axis=0, keepdims=True))
        square = jnp.concatenate(rows, axis=0)
        live = position() < tc[b]
        at = block_rows(b)
        base[at, :] = jnp.where(live, ENTROPY * b_in[at, :] + (1.0 / embed) * square, DEAD)
        bw[at, :] = jnp.where(live, LOG2E * b_in[at, :], DEAD)
        value = jnp.where(live, POT * g0[at, :] - (POT / embed) * square, DEAD)
        gamma[at, :] = value
        return jnp.maximum(top, value)

    blocks = tc.shape[0]
    offset = jnp.max(lax.fori_loop(0, blocks, target, jnp.full((TILES, LANES), DEAD, F32)))
    yc[:, pl.ds(blocks * BLOCK, CHUNK)] = jnp.zeros((yc.shape[0], CHUNK), BF16)
    put_in_columns(gamma, offset, ye)
    for copy in copies[6:]:
        copy.wait()
    sub = lax.broadcasted_iota(jnp.int32, (LANES - EXTRA, LANES), 0)
    ones = jnp.where(sub < 3, 1.0, 0.0)
    lane = lax.broadcasted_iota(jnp.int32, (LANES, LANES), 1)

    def source(b, carry):
        rows = []
        for k in range(TILES):
            at = lane_tile(b, k)
            value = x[:, at]
            turned = jnp.concatenate([*split3(value * scale), ones], axis=0).T
            x1[at, :] = turned.astype(BF16)
            x2[at, :] = jnp.where(lane < 64, turned, pltpu.roll(turned, 64, 1)).astype(BF16)
            rows.append(jnp.sum(value * value, axis=0, keepdims=True))
        at = block_rows(b)
        xsq[at, :] = jnp.concatenate(rows, axis=0)
        aw[at, :] = jnp.where(position() < sc[b], LOG2E * a_in[at, :], DEAD)
        return carry

    lax.fori_loop(0, sc.shape[0], source, 0)
    row_half(Scores(table, place, x1, x2, yc, ye), offset, out, acc, tops)
    keep.wait()


def col_kernel(place, number, embed, final, *refs):
    parts = refs[:number]
    weight, square, table_hbm, x1, x2, yc, out = refs[number : number + 7]
    rest = list(refs[number + 7 :])
    f_hbm = rest.pop(0) if final else None
    acc, tops, x1f, phi, table, sems = rest[:6]
    fetch = pltpu.make_async_copy(table_hbm, table, sems.at[0])
    fetch.start()
    offset = update(parts, weight, phi)
    if final:
        f_out = rest[6]
        value = phi[...]
        f = value * (1.0 / POT) + square[...] * (1.0 / embed)
        f_out[...] = jnp.where(value > 0.5 * DEAD, f, 0.0)
        copy = pltpu.make_async_copy(f_out, f_hbm, sems.at[1])
        copy.start()
    put_in_rows(phi, offset, x1, x1f)
    fetch.wait()
    col_half(Scores(table, place, x1f, x2, yc, None), offset, out, acc, tops)
    if final:
        copy.wait()


def row_kernel(place, number, *refs):
    parts = refs[:number]
    weight, table_hbm, x1, x2, yc, out, acc, tops, ye, gamma, table, sem = refs[number:]
    fetch = pltpu.make_async_copy(table_hbm, table, sem)
    fetch.start()
    offset = update(parts, weight, gamma)
    put_in_columns(gamma, offset, ye)
    fetch.wait()
    row_half(Scores(table, place, x1, x2, yc, ye), offset, out, acc, tops)


def exchange(value, axis):
    size = lax.axis_size(axis)

    def swap(value, turn):
        return lax.ppermute(value, axis, [(i, turn(i)) for i in range(size)])

    if size & (size - 1):
        return [value] + [swap(value, lambda i, k=k: (i + k) % size) for k in range(1, size)]
    parts = [value]
    bit = size
    while bit > 1:
        value = merge(parts) if len(parts) > 1 else parts[0]
        step = max(bit // 4, 1)
        masks = range(step, bit, step)
        parts = [value] + [swap(value, lambda i, m=m: i ^ m) for m in masks]
        bit = step
    return parts


def on_device(x, y, source_counts, target_counts, source_weight, target_weight, start, pair_blocks, pair_count):
    embed, source_len = x.shape
    target_len = y.shape[1]
    a = source_weight.reshape(-1, LANES)
    b = target_weight.reshape(-1, LANES)
    g0 = start.reshape(-1, LANES)
    slots = pair_blocks.shape[3]
    place = Table(slots, source_counts.shape[0], target_counts.shape[0])
    vmem = pl.BlockSpec(memory_space=pltpu.VMEM)
    smem = pl.BlockSpec(memory_space=pltpu.SMEM)
    hbm = pl.BlockSpec(memory_space=pltpu.HBM)
    anywhere = pl.BlockSpec(memory_space=pl.ANY)
    table_scratch = pltpu.SMEM((place.size,), jnp.int32)
    params = pltpu.CompilerParams(vmem_limit_bytes=VMEM_LIMIT)
    source_tile = jax.ShapeDtypeStruct((source_len // LANES, LANES), F32)
    target_tile = jax.ShapeDtypeStruct((target_len // LANES, LANES), F32)
    row_acc = pltpu.VMEM((source_len, LANES), F32)
    col_acc = pltpu.VMEM(((target_len // CHUNK + 1) * 8, CHUNK), F32)
    source_scratch = pltpu.VMEM(source_tile.shape, F32)
    target_scratch = pltpu.VMEM(target_tile.shape, F32)
    columns_extra = pltpu.VMEM((16, target_len + CHUNK), BF16)

    def smem_like(value):
        return pltpu.SMEM(value.shape, value.dtype)

    first = (x, y, g0, b, a, pair_blocks, source_counts, target_counts)
    part, x1, x2, yc, xsq, aw, base, bw, table = pl.pallas_call(
        lambda *refs: first_kernel(place, *refs),
        in_specs=[smem] + [hbm] * 8,
        out_specs=[vmem] * 8 + [anywhere],
        out_shape=[
            source_tile,
            jax.ShapeDtypeStruct((source_len, LANES), BF16),
            jax.ShapeDtypeStruct((source_len, LANES), BF16),
            jax.ShapeDtypeStruct((3 * embed, target_len + CHUNK), BF16),
            source_tile,
            source_tile,
            target_tile,
            target_tile,
            jax.ShapeDtypeStruct((place.size,), jnp.int32),
        ],
        scratch_shapes=[
            row_acc,
            row_acc,
            columns_extra,
            target_scratch,
            pltpu.VMEM(x.shape, F32),
            pltpu.VMEM(y.shape, F32),
            target_scratch,
            target_scratch,
            source_scratch,
            smem_like(pair_blocks),
            smem_like(source_counts),
            smem_like(target_counts),
            pltpu.SMEM((place.columns + 1,), jnp.int32),
            smem_like(source_counts),
            smem_like(source_counts),
            table_scratch,
            pltpu.SemaphoreType.DMA((9,)),
        ],
        compiler_params=params,
        name="rows_first",
    )(pair_count, *[pltpu.with_memory_space_constraint(v, pltpu.HBM) for v in first])
    common = (table, x1, x2, yc)
    common_specs = [anywhere] + [vmem] * 3

    def columns(parts, final):
        scratch = [col_acc, col_acc, pltpu.VMEM((source_len, LANES), BF16), source_scratch, table_scratch]
        scratch.append(pltpu.SemaphoreType.DMA((2,)))
        return pl.pallas_call(
            lambda *refs: col_kernel(place, len(parts), embed, final, *refs),
            in_specs=[vmem] * (len(parts) + 2) + common_specs,
            out_specs=[vmem, hbm] if final else [vmem],
            out_shape=[target_tile, source_tile] if final else [target_tile],
            scratch_shapes=scratch + ([source_scratch] if final else []),
            compiler_params=params,
            name="columns",
        )(*parts, aw, xsq, *common)

    def rows(parts):
        return pl.pallas_call(
            lambda *refs: row_kernel(place, len(parts), *refs),
            in_specs=[vmem] * (len(parts) + 1) + common_specs,
            out_specs=vmem,
            out_shape=source_tile,
            scratch_shapes=[
                row_acc,
                row_acc,
                columns_extra,
                target_scratch,
                table_scratch,
                pltpu.SemaphoreType.DMA,
            ],
            compiler_params=params,
            name="rows",
        )(*parts, bw, *common)

    (part,) = columns(exchange(part, "tgt"), False)
    part = rows(exchange(part, "src"))
    part, f = columns(exchange(part, "tgt"), True)
    merged = merge(exchange(part, "src"))
    g = jnp.where(base > 0.5 * DEAD, base - merged * (1.0 / POT), 0.0)
    return f.reshape(-1), g.reshape(-1)


def solution(mesh):
    in_specs = (
        P(None, "src"),
        P(None, "tgt"),
        P("src"),
        P("tgt"),
        P("src"),
        P("tgt"),
        P("tgt"),
        P("src", "tgt", None, None),
        P("src", "tgt"),
    )
    out_specs = (P("src"), P("tgt"))
    return jax.shard_map(on_device, mesh=mesh, in_specs=in_specs, out_specs=out_specs, check_vma=False)
```

```python
import functools
import math

import jax
import jax.numpy as jnp
from jax import lax
from jax.experimental import pallas as pl
from jax.experimental.pallas import tpu as pltpu
from jax.sharding import PartitionSpec as P

F32 = jnp.float32
BF16 = jnp.bfloat16
BLOCK = 1024
LANES = 128
TILES = BLOCK // LANES
CHUNK = 256
PER_BLOCK = BLOCK // CHUNK
UNROLL = 16
KEPT = 5
BITS = 8
EXTRA = 96
DEAD = -1e30
LOW, HIGH = 2.0**-96, 2.0**120
ENTROPY = 0.1
LOG2E = math.log2(math.e)
POT = LOG2E / ENTROPY
VMEM_LIMIT = 10 * 1024 * 1024


def split3(value):
    high = value.astype(BF16).astype(F32)
    rest = value - high
    middle = rest.astype(BF16).astype(F32)
    return high, middle, rest - middle


def position():
    return lax.broadcasted_iota(jnp.int32, (TILES, LANES), 0) * LANES + lax.broadcasted_iota(
        jnp.int32, (TILES, LANES), 1
    )


def block_rows(b):
    return pl.ds(pl.multiple_of(b * TILES, TILES), TILES)


def lane_tile(b, k):
    return pl.ds(pl.multiple_of(b * BLOCK + k * LANES, LANES), LANES)


def row_chunk(row):
    return pl.ds(pl.multiple_of(row * CHUNK, CHUNK), CHUNK)


def col_chunk(col):
    return pl.ds(pl.multiple_of(col * 8, 8), 8)


def merge(parts):
    top = parts[0]
    for part in parts[1:]:
        top = jnp.maximum(top, part)
    total = jnp.exp2(parts[0] - top)
    for part in parts[1:]:
        total = total + jnp.exp2(part - top)
    return top + jnp.log2(total)


class Table:
    def __init__(self, slots, sources, targets):
        self.most = -(-slots * PER_BLOCK * PER_BLOCK // (2 * UNROLL)) * UNROLL
        self.sources, self.targets = sources, targets
        self.source_limit = 1
        self.target_limit = self.source_limit + sources
        self.units = self.target_limit + targets
        self.size = self.units + self.most
        self.columns = slots * PER_BLOCK + sources

    def fill(self, pairs, count, source_counts, target_counts, table, columns, wanted, place):
        number = count[0, 0]
        nowhere = self.targets * PER_BLOCK

        for i in range(self.units):
            table[i] = 0
        for b in range(self.sources):
            wanted[b] = 0

        def chunks_of(live):
            return (live + CHUNK - 1) // CHUNK

        def measure(p, carry):
            sb, tb = pairs[0, 0, 0, p], pairs[0, 0, 1, p]
            table[self.source_limit + sb] = source_counts[sb]
            table[self.target_limit + tb] = target_counts[tb]
            wanted[sb] += chunks_of(target_counts[tb])
            return carry

        lax.fori_loop(0, number, measure, 0)
        m = 0
        starts = []
        for b in range(self.sources):
            starts.append(m)
            place[b] = m
            columns[m + wanted[b]] = nowhere
            m = m + wanted[b] + (wanted[b] & 1)

        def put(p, carry):
            sb, tb = pairs[0, 0, 0, p], pairs[0, 0, 1, p]
            start = place[sb]
            chunks = chunks_of(target_counts[tb])
            for c in range(PER_BLOCK):
                columns[jnp.where(c < chunks, start + c, self.columns)] = tb * PER_BLOCK + c
            place[sb] = start + chunks
            return carry

        lax.fori_loop(0, number, put, 0)
        n = self.units
        for b in range(self.sources):
            twos = (wanted[b] + 1) >> 1
            rows = [((b * PER_BLOCK + r) << (2 * BITS)) for r in range(PER_BLOCK)]

            def emit(c, carry, first=starts[b], n=n, twos=twos, rows=rows):
                word = (columns[first + 2 * c] << BITS) + columns[first + 2 * c + 1]
                for r in range(PER_BLOCK):
                    table[n + r * twos + c] = rows[r] + word
                return carry

            lax.fori_loop(0, twos, emit, 0)
            n = n + twos * chunks_of(source_counts[b])
        steps = (n - self.units + UNROLL - 1) // UNROLL

        def fill(i, carry):
            table[i] = (nowhere << BITS) + nowhere
            return carry

        lax.fori_loop(n, self.units + steps * UNROLL, fill, 0)
        table[0] = steps


def chunks_of_unit(table, place, t):
    unit = table[place.units + t]
    mask = (1 << BITS) - 1
    return unit >> (2 * BITS), ((unit >> BITS) & mask, unit & mask)


def dither(shape):
    lane = lax.broadcasted_iota(jnp.int32, shape, len(shape) - 1)
    return ((lane * 37) & 63).astype(F32) * (1.0 / 64)


class Scores:
    def __init__(self, table, place, x1, x2, y, ye, ones=(3, 6)):
        self.table, self.place, self.x1, self.x2, self.y, self.ye = table, place, x1, x2, y, ye
        self.zero = jnp.zeros((LANES - EXTRA, CHUNK), BF16)
        sub = lax.broadcasted_iota(jnp.int32, (LANES - EXTRA, CHUNK), 0)
        lo, hi = ones
        self.static = jnp.where((sub >= lo) & (sub < hi), 1.0, 0.0).astype(BF16)

    def unit(self, t):
        row, cols = chunks_of_unit(self.table, self.place, t)
        at = row_chunk(row)
        lhs = jnp.concatenate([self.x1[at, :], self.x2[at, :]], axis=1)
        values = []
        part = self.y.shape[0] // 3
        for col in cols:
            at = pl.ds(pl.multiple_of(col * CHUNK, CHUNK), CHUNK)
            high, middle, low = (self.y[k * part : (k + 1) * part, at] for k in range(3))
            extra = [self.static] if self.ye is None else [self.ye[:, at], self.zero[16:]]
            rhs = jnp.concatenate([high, high, high, *extra, middle, middle, low, self.zero], axis=0)
            values.append(jnp.dot(lhs, rhs, preferred_element_type=F32))
        return row, cols, values

    def each(self, body, unroll, first=0, last=None):
        def step(s, carry):
            for u in range(unroll):
                body(s * unroll + u, *self.unit(s * unroll + u))
            return carry

        steps = self.table[0] if last is None else jnp.minimum(self.table[0], last)
        each = UNROLL // unroll
        lax.fori_loop(first * each, steps * each, step, 0)


def fill_ref(ref, rows, value):
    def body(i, carry):
        ref[pl.ds(pl.multiple_of(i * rows, rows), rows), :] = jnp.full((rows, ref.shape[1]), value, F32)
        return carry

    lax.fori_loop(0, ref.shape[0] // rows, body, 0)


def check(total, limit, low):
    fine = (total >= low) & (total <= HIGH)
    return jnp.where(fine | (position() >= limit), 0.0, 1.0)


def row_tile(acc, b, reduce):
    rows = [reduce(acc[lane_tile(b, r), :].T, axis=0, keepdims=True) for r in range(TILES)]
    return jnp.concatenate(rows, axis=0)


def across(values, combine):
    parts = [v[:, k * LANES : (k + 1) * LANES] for v in values for k in range(CHUNK // LANES)]
    while len(parts) > 1:
        parts = [combine(a, b) for a, b in zip(parts[::2], parts[1::2])]
    return parts[0]


def row_half(run, finished, scores, prepare, offset, out, acc, tops):
    blocks = out.shape[0] // TILES
    fill_ref(acc, CHUNK, 0.0)
    run()
    low, scale = finished()

    def finish(b, bad):
        total = row_tile(acc, b, jnp.sum)
        out[block_rows(b), :] = jnp.where(total > 0.0, (offset - scale) + jnp.log2(total), DEAD)
        return jnp.maximum(bad, check(total, scores.table[scores.place.source_limit + b], low))

    bad = lax.fori_loop(0, blocks, finish, jnp.zeros((TILES, LANES), F32), unroll=2)

    @pl.when(jnp.max(bad) > 0.0)
    def _():
        prepare()
        fill_ref(acc, CHUNK, DEAD)

        def highest(t, row, cols, values):
            acc[row_chunk(row), :] = jnp.maximum(acc[row_chunk(row), :], across(values, jnp.maximum))

        scores.each(highest, 1)

        def keep_top(b, carry):
            top = row_tile(acc, b, jnp.max)
            tops[block_rows(b), :] = jnp.where(top > 0.5 * DEAD, top, 0.0)
            return carry

        lax.fori_loop(0, blocks, keep_top, 0)
        fill_ref(acc, CHUNK, 0.0)

        def add_below(t, row, cols, values):
            lines = []
            for k in range(CHUNK // LANES):
                line = tops[pl.ds(row * (CHUNK // LANES) + k, 1), :]
                lines.append(jnp.broadcast_to(line, (LANES, LANES)).T)
            top = jnp.concatenate([jnp.concatenate(lines, axis=0)] * (CHUNK // LANES), axis=1)
            acc[row_chunk(row), :] += across([jnp.exp2(v - top) for v in values], jnp.add)

        scores.each(add_below, 1)

        def finish_below(b, carry):
            total = row_tile(acc, b, jnp.sum)
            top = tops[block_rows(b), :]
            out[block_rows(b), :] = jnp.where(total > 0.0, (offset + top) + jnp.log2(total), DEAD)
            return carry

        lax.fori_loop(0, blocks, finish_below, 0)


def col_tile(acc, b, reduce):
    rows = []
    for c in range(PER_BLOCK):
        line = reduce(acc[col_chunk(b * PER_BLOCK + c), :], axis=0, keepdims=True)
        for k in range(CHUNK // LANES):
            rows.append(line[:, k * LANES : (k + 1) * LANES])
    return jnp.concatenate(rows, axis=0)


def col_half(kept, factors, low, scores, prepare, offset, out, acc, tops):
    blocks = out.shape[0] // TILES
    table, place = scores.table, scores.place
    fill_ref(acc, 8, 0.0)

    def step(s, carry):
        for u in range(UNROLL):
            row, cols = chunks_of_unit(table, place, s * UNROLL + u)
            at = row_chunk(row)
            here = row_chunk(s * UNROLL + u)
            sums = jnp.dot(factors[:, at], kept[here, :], preferred_element_type=F32)
            for k, col in enumerate(cols):
                acc[col_chunk(col), :] += sums[:8, k * CHUNK : (k + 1) * CHUNK]
        return carry

    lax.fori_loop(0, jnp.minimum(table[0], KEPT), step, 0)

    @pl.when(table[0] > KEPT)
    def _():
        prepare()

        def add(t, row, cols, values):
            for col, value in zip(cols, values):
                acc[col_chunk(col), :] += jnp.sum(jnp.exp2(value).reshape(CHUNK // 8, 8, CHUNK), axis=0)

        scores.each(add, 2, KEPT)

    def finish(b, bad):
        total = col_tile(acc, b, jnp.sum)
        out[block_rows(b), :] = jnp.where(total > 0.0, offset + jnp.log2(total), DEAD)
        return jnp.maximum(bad, check(total, table[place.target_limit + b], low))

    bad = lax.fori_loop(0, blocks, finish, jnp.zeros((TILES, LANES), F32), unroll=4)

    @pl.when(jnp.max(bad) > 0.0)
    def _():
        prepare()
        fill_ref(tops, 8, DEAD)

        def highest(t, row, cols, values):
            for col, value in zip(cols, values):
                part = jnp.max(value.reshape(CHUNK // 8, 8, CHUNK), axis=0)
                tops[col_chunk(col), :] = jnp.maximum(tops[col_chunk(col), :], part)

        scores.each(highest, 1)

        def spread(i, carry):
            top = jnp.max(tops[col_chunk(i), :], axis=0, keepdims=True)
            top = jnp.where(top > 0.5 * DEAD, top, 0.0)
            tops[col_chunk(i), :] = jnp.broadcast_to(top, (8, CHUNK))
            return carry

        lax.fori_loop(0, tops.shape[0] // 8, spread, 0)
        fill_ref(acc, 8, 0.0)

        def add_below(t, row, cols, values):
            for col, value in zip(cols, values):
                e = jnp.exp2(value.reshape(CHUNK // 8, 8, CHUNK) - tops[col_chunk(col), :][None])
                acc[col_chunk(col), :] += jnp.sum(e, axis=0)

        scores.each(add_below, 1)

        def finish_below(b, carry):
            total = col_tile(acc, b, jnp.sum)
            top = col_tile(tops, b, jnp.max)
            out[block_rows(b), :] = jnp.where(total > 0.0, (offset + top) + jnp.log2(total), DEAD)
            return carry

        lax.fori_loop(0, blocks, finish_below, 0)


def put_parts(value_of, blocks, rows):
    sub = lax.broadcasted_iota(jnp.int32, (16, LANES), 0)

    def body(b, carry):
        high, middle, low = split3(value_of(b))
        for k in range(TILES):
            at = slice(k, k + 1)
            parts = jnp.where(sub == 1, middle[at, :], jnp.where(sub == 2, low[at, :], 0.0))
            rows[:, lane_tile(b, k)] = jnp.where(sub == 0, high[at, :], parts).astype(BF16)
        return carry

    lax.fori_loop(0, blocks, body, 0, unroll=2)


def put_in_columns(potential, offset, ye):
    blocks = potential.shape[0] // TILES
    put_parts(lambda b: potential[block_rows(b), :] - offset, blocks, ye)
    sub = lax.broadcasted_iota(jnp.int32, (16, LANES), 0)
    for k in range(CHUNK // LANES):
        at = pl.ds(blocks * BLOCK + k * LANES, LANES)
        ye[:, at] = jnp.where(sub == 0, DEAD, 0.0).astype(BF16)


def put_in_rows(potential, offset, x1, x1f):
    sub = lax.broadcasted_iota(jnp.int32, (8, LANES), 0)
    above = jnp.zeros((EXTRA, LANES), F32)
    below = jnp.zeros((LANES - EXTRA - 8, LANES), F32)

    def body(b, carry):
        high, middle, low = split3(potential[block_rows(b), :] - offset)
        for k in range(TILES):
            at = slice(k, k + 1)
            rows = jnp.where(sub == 4, middle[at, :], jnp.where(sub == 5, low[at, :], 0.0))
            rows = jnp.where(sub == 3, high[at, :], rows)
            turned = jnp.concatenate([above, rows, below], axis=0).T.astype(BF16)
            x1f[lane_tile(b, k), :] = x1[lane_tile(b, k), :] + turned
        return carry

    lax.fori_loop(0, potential.shape[0] // TILES, body, 0)


def update(parts, weight, potential):
    weight = weight[...]
    value = jnp.where(weight > 0.5 * DEAD, weight - merge([part[...] for part in parts]), DEAD)
    potential[...] = value
    return jnp.max(value)


def first_kernel(
    place,
    count, x_hbm, y_hbm, g0_hbm, b_hbm, a_hbm, pairs_hbm, sc_hbm, tc_hbm,
    out, x1, x2, yc, xsq, aw, base, bw, table_out, kept, low_out,
    acc, tops, ye, spread, peak, gamma, x, y, g0, b_in, a_in, pairs, sc, tc, columns, wanted, places, table, sems,
):
    embed = x.shape[0]
    scale = 2.0 * POT / embed
    here = [(pairs_hbm, pairs), (sc_hbm, sc), (tc_hbm, tc)]
    here += [(y_hbm, y), (g0_hbm, g0), (b_hbm, b_in), (x_hbm, x), (a_hbm, a_in)]
    copies = [pltpu.make_async_copy(a, b, sems.at[i]) for i, (a, b) in enumerate(here)]
    for copy in copies:
        copy.start()
    for copy in copies[:3]:
        copy.wait()
    place.fill(pairs, count, sc, tc, table, columns, wanted, places)
    keep = pltpu.make_async_copy(table, table_out, sems.at[len(copies)])
    keep.start()
    for copy in copies[3:6]:
        copy.wait()

    def target(b, top):
        rows = []
        for k in range(TILES):
            at = lane_tile(b, k)
            value = y[:, at]
            yc[:, at] = jnp.concatenate([p.astype(BF16) for p in split3(value)], axis=0)
            rows.append(jnp.sum(value * value, axis=0, keepdims=True))
        square = jnp.concatenate(rows, axis=0)
        live = position() < tc[b]
        at = block_rows(b)
        base[at, :] = jnp.where(live, ENTROPY * b_in[at, :] + (1.0 / embed) * square, DEAD)
        bw[at, :] = jnp.where(live, LOG2E * b_in[at, :], DEAD)
        value = jnp.where(live, POT * g0[at, :] - (POT / embed) * square, DEAD)
        gamma[at, :] = value
        return jnp.maximum(top, value)

    blocks = tc.shape[0]
    offset = jnp.max(lax.fori_loop(0, blocks, target, jnp.full((TILES, LANES), DEAD, F32)))
    yc[:, pl.ds(blocks * BLOCK, CHUNK)] = jnp.zeros((yc.shape[0], CHUNK), BF16)

    def widen(b, carry):
        value = jnp.exp2(gamma[block_rows(b), :] - offset)
        for k in range(TILES):
            spread[:, lane_tile(b, k)] = jnp.broadcast_to(value[k : k + 1, :], (8, LANES))
        return carry

    lax.fori_loop(0, blocks, widen, 0, unroll=2)
    spread[:, pl.ds(blocks * BLOCK, CHUNK)] = jnp.zeros((8, CHUNK), F32)
    for copy in copies[6:]:
        copy.wait()
    sub = lax.broadcasted_iota(jnp.int32, (LANES - EXTRA, LANES), 0)
    ones = jnp.where(sub < 3, 1.0, jnp.where(sub == 6, dither((LANES - EXTRA, LANES)), 0.0))
    lane = lax.broadcasted_iota(jnp.int32, (LANES, LANES), 1)

    def source(b, carry):
        rows = []
        for k in range(TILES):
            at = lane_tile(b, k)
            value = x[:, at]
            turned = jnp.concatenate([*split3(value * scale), ones], axis=0).T
            x1[at, :] = turned.astype(BF16)
            x2[at, :] = jnp.where(lane < 64, turned, pltpu.roll(turned, 64, 1)).astype(BF16)
            rows.append(jnp.sum(value * value, axis=0, keepdims=True))
        at = block_rows(b)
        xsq[at, :] = jnp.concatenate(rows, axis=0)
        aw[at, :] = jnp.where(position() < sc[b], LOG2E * a_in[at, :], DEAD)
        return carry

    lax.fori_loop(0, sc.shape[0], source, 0)
    peak[...] = jnp.zeros(peak.shape, BF16)

    def add(keep_entries, t, row, cols, values):
        entries = [jnp.exp2(v) for v in values]
        stored = jnp.concatenate(entries, axis=1).astype(BF16)
        if keep_entries:
            kept[row_chunk(t), :] = stored
        peak[...] = jnp.maximum(peak[...], jnp.max(stored.reshape(CHUNK // 16, 16, 2 * CHUNK), axis=0))
        weighted = []
        for col, e in zip(cols, entries):
            factor = spread[:, pl.ds(pl.multiple_of(col * CHUNK, CHUNK), CHUNK)]
            weighted.append((e.reshape(CHUNK // 8, 8, CHUNK) * factor[None]).reshape(CHUNK, CHUNK))
        acc[row_chunk(row), :] += across(weighted, jnp.add)

    def finished():
        low = LOW * jnp.maximum(jnp.max(peak[...].astype(F32)), 1.0)
        low_out[...] = jnp.full(low_out.shape, low, F32)
        return low, dither((TILES, LANES))

    plain = Scores(table, place, x1, x2, yc, None, (6, 7))
    exact = Scores(table, place, x1, x2, yc, ye)

    def run():
        plain.each(functools.partial(add, True), UNROLL, 0, KEPT)
        plain.each(functools.partial(add, False), UNROLL, KEPT)

    row_half(run, finished, exact, lambda: put_in_columns(gamma, offset, ye), offset, out, acc, tops)
    keep.wait()


def col_kernel(place, number, embed, final, *refs):
    parts = refs[:number]
    weight, square, kept, low, table_hbm, x1, x2, yc, out = refs[number : number + 9]
    rest = list(refs[number + 9 :])
    f_hbm = rest.pop(0) if final else None
    acc, tops, factors, x1f, phi, table, sems = rest[:7]
    fetch = pltpu.make_async_copy(table_hbm, table, sems.at[0])
    fetch.start()
    offset = update(parts, weight, phi)
    if final:
        f_out = rest[7]
        value = phi[...]
        f = value * (1.0 / POT) + square[...] * (1.0 / embed)
        f_out[...] = jnp.where(value > 0.5 * DEAD, f, 0.0)
        copy = pltpu.make_async_copy(f_out, f_hbm, sems.at[1])
        copy.start()
    scale = dither((TILES, LANES))
    put_parts(lambda b: jnp.exp2((phi[block_rows(b), :] - offset) - scale), place.sources, factors)
    fetch.wait()
    exact = Scores(table, place, x1f, x2, yc, None)
    prepare = lambda: put_in_rows(phi, offset, x1, x1f)
    col_half(kept, factors, low[...], exact, prepare, offset, out, acc, tops)
    if final:
        copy.wait()


def row_kernel(place, number, *refs):
    parts = refs[:number]
    weight, table_hbm, x1, x2, yc, out, acc, tops, ye, gamma, table, sem = refs[number:]
    fetch = pltpu.make_async_copy(table_hbm, table, sem)
    fetch.start()
    offset = update(parts, weight, gamma)
    put_in_columns(gamma, offset, ye)
    fetch.wait()
    exact = Scores(table, place, x1, x2, yc, ye)

    def add(t, row, cols, values):
        acc[row_chunk(row), :] += across([jnp.exp2(v) for v in values], jnp.add)

    run = lambda: exact.each(add, UNROLL)
    row_half(run, lambda: (LOW, 0.0), exact, lambda: None, offset, out, acc, tops)


def exchange(value, axis):
    size = lax.axis_size(axis)

    def swap(value, turn):
        return lax.ppermute(value, axis, [(i, turn(i)) for i in range(size)])

    if size & (size - 1):
        return [value] + [swap(value, lambda i, k=k: (i + k) % size) for k in range(1, size)]
    parts = [value]
    bit = size
    while bit > 1:
        value = merge(parts) if len(parts) > 1 else parts[0]
        step = max(bit // 4, 1)
        masks = range(step, bit, step)
        parts = [value] + [swap(value, lambda i, m=m: i ^ m) for m in masks]
        bit = step
    return parts


def on_device(x, y, source_counts, target_counts, source_weight, target_weight, start, pair_blocks, pair_count):
    embed, source_len = x.shape
    target_len = y.shape[1]
    a = source_weight.reshape(-1, LANES)
    b = target_weight.reshape(-1, LANES)
    g0 = start.reshape(-1, LANES)
    slots = pair_blocks.shape[3]
    place = Table(slots, source_counts.shape[0], target_counts.shape[0])
    vmem = pl.BlockSpec(memory_space=pltpu.VMEM)
    smem = pl.BlockSpec(memory_space=pltpu.SMEM)
    hbm = pl.BlockSpec(memory_space=pltpu.HBM)
    anywhere = pl.BlockSpec(memory_space=pl.ANY)
    table_scratch = pltpu.SMEM((place.size,), jnp.int32)
    params = pltpu.CompilerParams(vmem_limit_bytes=VMEM_LIMIT)
    source_tile = jax.ShapeDtypeStruct((source_len // LANES, LANES), F32)
    target_tile = jax.ShapeDtypeStruct((target_len // LANES, LANES), F32)
    row_acc = pltpu.VMEM((source_len, LANES), F32)
    col_acc = pltpu.VMEM(((target_len // CHUNK + 1) * 8, CHUNK), F32)
    source_scratch = pltpu.VMEM(source_tile.shape, F32)
    target_scratch = pltpu.VMEM(target_tile.shape, F32)
    columns_extra = pltpu.VMEM((16, target_len + CHUNK), BF16)

    def smem_like(value):
        return pltpu.SMEM(value.shape, value.dtype)

    first = (x, y, g0, b, a, pair_blocks, source_counts, target_counts)
    part, x1, x2, yc, xsq, aw, base, bw, table, kept, low = pl.pallas_call(
        lambda *refs: first_kernel(place, *refs),
        in_specs=[smem] + [hbm] * 8,
        out_specs=[vmem] * 8 + [anywhere] + [vmem] * 2,
        out_shape=[
            source_tile,
            jax.ShapeDtypeStruct((source_len, LANES), BF16),
            jax.ShapeDtypeStruct((source_len, LANES), BF16),
            jax.ShapeDtypeStruct((3 * embed, target_len + CHUNK), BF16),
            source_tile,
            source_tile,
            target_tile,
            target_tile,
            jax.ShapeDtypeStruct((place.size,), jnp.int32),
            pltpu.VMEM((KEPT * UNROLL * CHUNK, 2 * CHUNK), BF16),
            jax.ShapeDtypeStruct((TILES, LANES), F32),
        ],
        scratch_shapes=[
            row_acc,
            source_scratch,
            columns_extra,
            pltpu.VMEM((8, target_len + CHUNK), F32),
            pltpu.VMEM((16, 2 * CHUNK), BF16),
            target_scratch,
            pltpu.VMEM(x.shape, F32),
            pltpu.VMEM(y.shape, F32),
            target_scratch,
            target_scratch,
            source_scratch,
            smem_like(pair_blocks),
            smem_like(source_counts),
            smem_like(target_counts),
            pltpu.SMEM((place.columns + 1,), jnp.int32),
            smem_like(source_counts),
            smem_like(source_counts),
            table_scratch,
            pltpu.SemaphoreType.DMA((9,)),
        ],
        compiler_params=params,
        name="rows_first",
    )(pair_count, *[pltpu.with_memory_space_constraint(v, pltpu.HBM) for v in first])
    common = (table, x1, x2, yc)
    common_specs = [anywhere] + [vmem] * 3

    def columns(parts, final):
        scratch = [col_acc, col_acc, pltpu.VMEM((16, source_len), BF16)]
        scratch += [pltpu.VMEM((source_len, LANES), BF16), source_scratch, table_scratch]
        scratch.append(pltpu.SemaphoreType.DMA((2,)))
        return pl.pallas_call(
            lambda *refs: col_kernel(place, len(parts), embed, final, *refs),
            in_specs=[vmem] * (len(parts) + 4) + common_specs,
            out_specs=[vmem, hbm] if final else [vmem],
            out_shape=[target_tile, source_tile] if final else [target_tile],
            scratch_shapes=scratch + ([source_scratch] if final else []),
            compiler_params=params,
            name="columns",
        )(*parts, aw, xsq, kept, low, *common)

    def rows(parts):
        return pl.pallas_call(
            lambda *refs: row_kernel(place, len(parts), *refs),
            in_specs=[vmem] * (len(parts) + 1) + common_specs,
            out_specs=vmem,
            out_shape=source_tile,
            scratch_shapes=[
                row_acc,
                source_scratch,
                columns_extra,
                target_scratch,
                table_scratch,
                pltpu.SemaphoreType.DMA,
            ],
            compiler_params=params,
            name="rows",
        )(*parts, bw, *common)

    (part,) = columns(exchange(part, "tgt"), False)
    part = rows(exchange(part, "src"))
    part, f = columns(exchange(part, "tgt"), True)
    merged = merge(exchange(part, "src"))
    g = jnp.where(base > 0.5 * DEAD, base - merged * (1.0 / POT), 0.0)
    return f.reshape(-1), g.reshape(-1)


def solution(mesh):
    in_specs = (
        P(None, "src"),
        P(None, "tgt"),
        P("src"),
        P("tgt"),
        P("src"),
        P("tgt"),
        P("tgt"),
        P("src", "tgt", None, None),
        P("src", "tgt"),
    )
    out_specs = (P("src"), P("tgt"))
    return jax.shard_map(on_device, mesh=mesh, in_specs=in_specs, out_specs=out_specs, check_vma=False)
```

```python
import functools
import math

import jax
import jax.numpy as jnp
from jax import lax
from jax.experimental import pallas as pl
from jax.experimental.pallas import tpu as pltpu
from jax.sharding import PartitionSpec as P

F32 = jnp.float32
BF16 = jnp.bfloat16
BLOCK = 1024
LANES = 128
TILES = BLOCK // LANES
CHUNK = 256
PER_BLOCK = BLOCK // CHUNK
UNROLL = 18
KEPT = 5
BITS = 8
EXTRA = 96
DEAD = -1e30
LOW, HIGH = 2.0**-96, 2.0**120
HEAD = 48.0
ENTROPY = 0.1
LOG2E = math.log2(math.e)
POT = LOG2E / ENTROPY
VMEM_LIMIT = 10 * 1024 * 1024


def split3(value):
    high = value.astype(BF16).astype(F32)
    rest = value - high
    middle = rest.astype(BF16).astype(F32)
    return high, middle, rest - middle


def position():
    return lax.broadcasted_iota(jnp.int32, (TILES, LANES), 0) * LANES + lax.broadcasted_iota(
        jnp.int32, (TILES, LANES), 1
    )


def block_rows(b):
    return pl.ds(pl.multiple_of(b * TILES, TILES), TILES)


def lane_tile(b, k):
    return pl.ds(pl.multiple_of(b * BLOCK + k * LANES, LANES), LANES)


def row_chunk(row):
    return pl.ds(pl.multiple_of(row * CHUNK, CHUNK), CHUNK)


def col_chunk(col):
    return pl.ds(pl.multiple_of(col * 8, 8), 8)


def merge(parts):
    top = parts[0]
    for part in parts[1:]:
        top = jnp.maximum(top, part)
    total = jnp.exp2(parts[0] - top)
    for part in parts[1:]:
        total = total + jnp.exp2(part - top)
    return top + jnp.log2(total)


class Table:
    def __init__(self, slots, sources, targets):
        self.most = -(-slots * PER_BLOCK * PER_BLOCK // (2 * UNROLL)) * UNROLL
        self.sources, self.targets = sources, targets
        self.source_limit = 1
        self.target_limit = self.source_limit + sources
        self.units = self.target_limit + targets
        self.size = self.units + self.most
        self.columns = slots * PER_BLOCK + sources

    def fill(self, pairs, count, source_counts, target_counts, table, columns, wanted, place):
        number = count[0, 0]
        nowhere = self.targets * PER_BLOCK

        for i in range(self.units):
            table[i] = 0
        for b in range(self.sources):
            wanted[b] = 0

        def chunks_of(live):
            return (live + CHUNK - 1) // CHUNK

        def measure(p, carry):
            sb, tb = pairs[0, 0, 0, p], pairs[0, 0, 1, p]
            table[self.source_limit + sb] = source_counts[sb]
            table[self.target_limit + tb] = target_counts[tb]
            wanted[sb] += chunks_of(target_counts[tb])
            return carry

        lax.fori_loop(0, number, measure, 0)
        m = 0
        starts = []
        for b in range(self.sources):
            starts.append(m)
            place[b] = m
            columns[m + wanted[b]] = nowhere
            m = m + wanted[b] + (wanted[b] & 1)

        def put(p, carry):
            sb, tb = pairs[0, 0, 0, p], pairs[0, 0, 1, p]
            start = place[sb]
            chunks = chunks_of(target_counts[tb])
            for c in range(PER_BLOCK):
                columns[jnp.where(c < chunks, start + c, self.columns)] = tb * PER_BLOCK + c
            place[sb] = start + chunks
            return carry

        lax.fori_loop(0, number, put, 0)
        n = self.units
        for b in range(self.sources):
            twos = (wanted[b] + 1) >> 1
            rows = [((b * PER_BLOCK + r) << (2 * BITS)) for r in range(PER_BLOCK)]

            def emit(c, carry, first=starts[b], n=n, twos=twos, rows=rows):
                word = (columns[first + 2 * c] << BITS) + columns[first + 2 * c + 1]
                for r in range(PER_BLOCK):
                    table[n + r * twos + c] = rows[r] + word
                return carry

            lax.fori_loop(0, twos, emit, 0)
            n = n + twos * chunks_of(source_counts[b])
        steps = (n - self.units + UNROLL - 1) // UNROLL

        def fill(i, carry):
            table[i] = (nowhere << BITS) + nowhere
            return carry

        lax.fori_loop(n, self.units + steps * UNROLL, fill, 0)
        table[0] = steps


def chunks_of_unit(table, place, t):
    unit = table[place.units + t]
    mask = (1 << BITS) - 1
    return unit >> (2 * BITS), ((unit >> BITS) & mask, unit & mask)


def dither(shape):
    lane = lax.broadcasted_iota(jnp.int32, shape, len(shape) - 1)
    return ((lane * 37) & 63).astype(F32) * (1.0 / 64)


class Scores:
    def __init__(self, table, place, x1, x2, y, ye, ones=(3, 6)):
        self.table, self.place, self.x1, self.x2, self.y, self.ye = table, place, x1, x2, y, ye
        self.zero = jnp.zeros((LANES - EXTRA, CHUNK), BF16)
        sub = lax.broadcasted_iota(jnp.int32, (LANES - EXTRA, CHUNK), 0)
        lo, hi = ones
        self.static = jnp.where((sub >= lo) & (sub < hi), 1.0, 0.0).astype(BF16)

    def unit(self, t):
        row, cols = chunks_of_unit(self.table, self.place, t)
        at = row_chunk(row)
        lhs = jnp.concatenate([self.x1[at, :], self.x2[at, :]], axis=1)
        values = []
        part = self.y.shape[0] // 3
        for col in cols:
            at = pl.ds(pl.multiple_of(col * CHUNK, CHUNK), CHUNK)
            high, middle, low = (self.y[k * part : (k + 1) * part, at] for k in range(3))
            extra = [self.static] if self.ye is None else [self.ye[:, at], self.zero[16:]]
            rhs = jnp.concatenate([high, high, high, *extra, middle, middle, low, self.zero], axis=0)
            values.append(jnp.dot(lhs, rhs, preferred_element_type=F32))
        return row, cols, values

    def each(self, body, unroll, first=0, last=None):
        def step(s, carry):
            for u in range(unroll):
                body(s * unroll + u, *self.unit(s * unroll + u))
            return carry

        steps = self.table[0] if last is None else jnp.minimum(self.table[0], last)
        each = UNROLL // unroll
        lax.fori_loop(first * each, steps * each, step, 0)


def fill_ref(ref, rows, value):
    def body(i, carry):
        ref[pl.ds(pl.multiple_of(i * rows, rows), rows), :] = jnp.full((rows, ref.shape[1]), value, F32)
        return carry

    lax.fori_loop(0, ref.shape[0] // rows, body, 0)


def check(total, limit, low):
    fine = (total >= low) & (total <= HIGH)
    return jnp.where(fine | (position() >= limit), 0.0, 1.0)


def row_tile(acc, b, reduce):
    rows = [reduce(acc[lane_tile(b, r), :].T, axis=0, keepdims=True) for r in range(TILES)]
    return jnp.concatenate(rows, axis=0)


def across(values, combine):
    parts = [v[:, k * LANES : (k + 1) * LANES] for v in values for k in range(CHUNK // LANES)]
    while len(parts) > 1:
        parts = [combine(a, b) for a, b in zip(parts[::2], parts[1::2])]
    return parts[0]


def row_half(run, finished, scores, prepare, offset, out, acc, tops):
    blocks = out.shape[0] // TILES
    fill_ref(acc, CHUNK, 0.0)
    run()
    low, scale = finished()

    def finish(b, bad):
        total = row_tile(acc, b, jnp.sum)
        out[block_rows(b), :] = jnp.where(total > 0.0, (offset - scale) + jnp.log2(total), DEAD)
        return jnp.maximum(bad, check(total, scores.table[scores.place.source_limit + b], low))

    bad = lax.fori_loop(0, blocks, finish, jnp.zeros((TILES, LANES), F32), unroll=2)

    @pl.when(jnp.max(bad) > 0.0)
    def _():
        prepare()
        fill_ref(acc, CHUNK, DEAD)

        def highest(t, row, cols, values):
            acc[row_chunk(row), :] = jnp.maximum(acc[row_chunk(row), :], across(values, jnp.maximum))

        scores.each(highest, 1)

        def keep_top(b, carry):
            top = row_tile(acc, b, jnp.max)
            tops[block_rows(b), :] = jnp.where(top > 0.5 * DEAD, top, 0.0)
            return carry

        lax.fori_loop(0, blocks, keep_top, 0)
        fill_ref(acc, CHUNK, 0.0)

        def add_below(t, row, cols, values):
            lines = []
            for k in range(CHUNK // LANES):
                line = tops[pl.ds(row * (CHUNK // LANES) + k, 1), :]
                lines.append(jnp.broadcast_to(line, (LANES, LANES)).T)
            top = jnp.concatenate([jnp.concatenate(lines, axis=0)] * (CHUNK // LANES), axis=1)
            acc[row_chunk(row), :] += across([jnp.exp2(v - top) for v in values], jnp.add)

        scores.each(add_below, 1)

        def finish_below(b, carry):
            total = row_tile(acc, b, jnp.sum)
            top = tops[block_rows(b), :]
            out[block_rows(b), :] = jnp.where(total > 0.0, (offset + top) + jnp.log2(total), DEAD)
            return carry

        lax.fori_loop(0, blocks, finish_below, 0)


def col_tile(acc, b, reduce):
    rows = []
    for c in range(PER_BLOCK):
        line = reduce(acc[col_chunk(b * PER_BLOCK + c), :], axis=0, keepdims=True)
        for k in range(CHUNK // LANES):
            rows.append(line[:, k * LANES : (k + 1) * LANES])
    return jnp.concatenate(rows, axis=0)


def col_half(kept, factors, low, scores, prepare, offset, out, acc, tops):
    blocks = out.shape[0] // TILES
    table, place = scores.table, scores.place
    fill_ref(acc, 8, 0.0)

    def step(s, carry):
        for u in range(UNROLL):
            row, cols = chunks_of_unit(table, place, s * UNROLL + u)
            at = row_chunk(row)
            here = row_chunk(s * UNROLL + u)
            sums = jnp.dot(factors[:, at], kept[here, :], preferred_element_type=F32)
            for k, col in enumerate(cols):
                acc[col_chunk(col), :] += sums[:8, k * CHUNK : (k + 1) * CHUNK]
        return carry

    lax.fori_loop(0, jnp.minimum(table[0], KEPT), step, 0)

    @pl.when(table[0] > KEPT)
    def _():
        prepare()

        def add(t, row, cols, values):
            for col, value in zip(cols, values):
                part = jnp.sum(jnp.exp2(value).reshape(CHUNK // 8, 8, CHUNK), axis=0)
                acc[col_chunk(col), :] += part * 2.0**HEAD

        scores.each(add, UNROLL // 2, KEPT)

    def finish(b, bad):
        total = col_tile(acc, b, jnp.sum)
        out[block_rows(b), :] = jnp.where(total > 0.0, (offset - HEAD) + jnp.log2(total), DEAD)
        return jnp.maximum(bad, check(total, table[place.target_limit + b], low))

    bad = lax.fori_loop(0, blocks, finish, jnp.zeros((TILES, LANES), F32), unroll=4)

    @pl.when(jnp.max(bad) > 0.0)
    def _():
        prepare()
        fill_ref(tops, 8, DEAD)

        def highest(t, row, cols, values):
            for col, value in zip(cols, values):
                part = jnp.max(value.reshape(CHUNK // 8, 8, CHUNK), axis=0)
                tops[col_chunk(col), :] = jnp.maximum(tops[col_chunk(col), :], part)

        scores.each(highest, 1)

        def spread(i, carry):
            top = jnp.max(tops[col_chunk(i), :], axis=0, keepdims=True)
            top = jnp.where(top > 0.5 * DEAD, top, 0.0)
            tops[col_chunk(i), :] = jnp.broadcast_to(top, (8, CHUNK))
            return carry

        lax.fori_loop(0, tops.shape[0] // 8, spread, 0)
        fill_ref(acc, 8, 0.0)

        def add_below(t, row, cols, values):
            for col, value in zip(cols, values):
                e = jnp.exp2(value.reshape(CHUNK // 8, 8, CHUNK) - tops[col_chunk(col), :][None])
                acc[col_chunk(col), :] += jnp.sum(e, axis=0)

        scores.each(add_below, 1)

        def finish_below(b, carry):
            total = col_tile(acc, b, jnp.sum)
            top = col_tile(tops, b, jnp.max)
            out[block_rows(b), :] = jnp.where(total > 0.0, (offset + top) + jnp.log2(total), DEAD)
            return carry

        lax.fori_loop(0, blocks, finish_below, 0)


def put_parts(value_of, blocks, rows):
    sub = lax.broadcasted_iota(jnp.int32, (16, LANES), 0)

    def body(b, carry):
        high, middle, low = split3(value_of(b))
        for k in range(TILES):
            at = slice(k, k + 1)
            parts = jnp.where(sub == 1, middle[at, :], jnp.where(sub == 2, low[at, :], 0.0))
            rows[:, lane_tile(b, k)] = jnp.where(sub == 0, high[at, :], parts).astype(BF16)
        return carry

    lax.fori_loop(0, blocks, body, 0, unroll=2)


def put_in_columns(potential, offset, ye):
    blocks = potential.shape[0] // TILES
    put_parts(lambda b: potential[block_rows(b), :] - offset, blocks, ye)
    sub = lax.broadcasted_iota(jnp.int32, (16, LANES), 0)
    for k in range(CHUNK // LANES):
        at = pl.ds(blocks * BLOCK + k * LANES, LANES)
        ye[:, at] = jnp.where(sub == 0, DEAD, 0.0).astype(BF16)


def put_in_rows(potential, offset, x1, x1f):
    sub = lax.broadcasted_iota(jnp.int32, (8, LANES), 0)
    above = jnp.zeros((EXTRA, LANES), F32)
    below = jnp.zeros((LANES - EXTRA - 8, LANES), F32)

    def body(b, carry):
        high, middle, low = split3(potential[block_rows(b), :] - offset)
        for k in range(TILES):
            at = slice(k, k + 1)
            rows = jnp.where(sub == 4, middle[at, :], jnp.where(sub == 5, low[at, :], 0.0))
            rows = jnp.where(sub == 3, high[at, :], rows)
            turned = jnp.concatenate([above, rows, below], axis=0).T.astype(BF16)
            x1f[lane_tile(b, k), :] = x1[lane_tile(b, k), :] + turned
        return carry

    lax.fori_loop(0, potential.shape[0] // TILES, body, 0)


def update(parts, weight, potential):
    weight = weight[...]
    value = jnp.where(weight > 0.5 * DEAD, weight - merge([part[...] for part in parts]), DEAD)
    potential[...] = value
    return jnp.max(value)


def first_kernel(
    place,
    count, x_hbm, y_hbm, g0_hbm, b_hbm, a_hbm, pairs_hbm, sc_hbm, tc_hbm,
    out, x1, x2, yc, xsq, aw, base, bw, table_out, kept, low_out,
    acc, tops, ye, spread, gamma, x, y, g0, b_in, a_in, pairs, sc, tc, columns, wanted, places, table, sems,
):
    embed = x.shape[0]
    scale = 2.0 * POT / embed
    here = [(pairs_hbm, pairs), (sc_hbm, sc), (tc_hbm, tc)]
    here += [(y_hbm, y), (g0_hbm, g0), (b_hbm, b_in), (x_hbm, x), (a_hbm, a_in)]
    copies = [pltpu.make_async_copy(a, b, sems.at[i]) for i, (a, b) in enumerate(here)]
    for copy in copies:
        copy.start()
    for copy in copies[:3]:
        copy.wait()
    place.fill(pairs, count, sc, tc, table, columns, wanted, places)
    keep = pltpu.make_async_copy(table, table_out, sems.at[len(copies)])
    keep.start()
    for copy in copies[3:6]:
        copy.wait()

    def target(b, carry):
        top, norm = carry
        rows = []
        for k in range(TILES):
            at = lane_tile(b, k)
            value = y[:, at]
            yc[:, at] = jnp.concatenate([p.astype(BF16) for p in split3(value)], axis=0)
            rows.append(jnp.sum(value * value, axis=0, keepdims=True))
        square = jnp.concatenate(rows, axis=0)
        live = position() < tc[b]
        at = block_rows(b)
        base[at, :] = jnp.where(live, ENTROPY * b_in[at, :] + (1.0 / embed) * square, DEAD)
        bw[at, :] = jnp.where(live, LOG2E * b_in[at, :], DEAD)
        value = jnp.where(live, POT * g0[at, :] - (POT / embed) * square, DEAD)
        gamma[at, :] = value
        return jnp.maximum(top, value), jnp.maximum(norm, jnp.where(live, square, 0.0))

    blocks = tc.shape[0]
    nothing = jnp.zeros((TILES, LANES), F32)
    offset, norm_y = lax.fori_loop(0, blocks, target, (nothing + DEAD, nothing))
    offset, norm_y = jnp.max(offset), jnp.max(norm_y)
    yc[:, pl.ds(blocks * BLOCK, CHUNK)] = jnp.zeros((yc.shape[0], CHUNK), BF16)

    def widen(b, carry):
        value = jnp.exp2(gamma[block_rows(b), :] - (offset - HEAD))
        for k in range(TILES):
            spread[:, lane_tile(b, k)] = jnp.broadcast_to(value[k : k + 1, :], (8, LANES))
        return carry

    lax.fori_loop(0, blocks, widen, 0, unroll=2)
    spread[:, pl.ds(blocks * BLOCK, CHUNK)] = jnp.zeros((8, CHUNK), F32)
    for copy in copies[6:]:
        copy.wait()
    sub = lax.broadcasted_iota(jnp.int32, (LANES - EXTRA, LANES), 0)
    ones = jnp.where(sub < 3, 1.0, jnp.where(sub == 6, dither((LANES - EXTRA, LANES)), 0.0))
    lane = lax.broadcasted_iota(jnp.int32, (LANES, LANES), 1)

    def source(b, norm):
        rows = []
        for k in range(TILES):
            at = lane_tile(b, k)
            value = x[:, at]
            turned = jnp.concatenate([*split3(value * scale), ones], axis=0).T
            x1[at, :] = turned.astype(BF16)
            x2[at, :] = jnp.where(lane < 64, turned, pltpu.roll(turned, 64, 1)).astype(BF16)
            rows.append(jnp.sum(value * value, axis=0, keepdims=True))
        at = block_rows(b)
        square = jnp.concatenate(rows, axis=0)
        live = position() < sc[b]
        xsq[at, :] = square
        aw[at, :] = jnp.where(live, LOG2E * a_in[at, :], DEAD)
        return jnp.maximum(norm, jnp.where(live, square, 0.0))

    norm_x = jnp.max(lax.fori_loop(0, sc.shape[0], source, nothing))

    def add(keep_entries, t, row, cols, values):
        entries = [jnp.exp2(v) for v in values]
        stored = jnp.concatenate(entries, axis=1).astype(BF16)
        if keep_entries:
            kept[row_chunk(t), :] = stored
        weighted = []
        for col, e in zip(cols, entries):
            factor = spread[:, pl.ds(pl.multiple_of(col * CHUNK, CHUNK), CHUNK)]
            weighted.append((e.reshape(CHUNK // 8, 8, CHUNK) * factor[None]).reshape(CHUNK, CHUNK))
        acc[row_chunk(row), :] += across(weighted, jnp.add)

    def finished():
        low = LOW * jnp.exp2(scale * jnp.sqrt(jnp.full((TILES, LANES), norm_x, F32) * norm_y))
        low_out[...] = low
        return low, dither((TILES, LANES)) + HEAD

    plain = Scores(table, place, x1, x2, yc, None, (6, 7))
    exact = Scores(table, place, x1, x2, yc, ye)

    def run():
        plain.each(functools.partial(add, True), UNROLL, 0, KEPT)
        plain.each(functools.partial(add, False), UNROLL, KEPT)

    row_half(run, finished, exact, lambda: put_in_columns(gamma, offset, ye), offset, out, acc, tops)
    keep.wait()


def col_kernel(place, number, embed, final, *refs):
    parts = refs[:number]
    weight, square, kept, low, table_hbm, x1, x2, yc, out = refs[number : number + 9]
    rest = list(refs[number + 9 :])
    f_hbm = rest.pop(0) if final else None
    acc, tops, factors, x1f, phi, table, sems = rest[:7]
    fetch = pltpu.make_async_copy(table_hbm, table, sems.at[0])
    fetch.start()
    offset = update(parts, weight, phi)
    if final:
        f_out = rest[7]
        value = phi[...]
        f = value * (1.0 / POT) + square[...] * (1.0 / embed)
        f_out[...] = jnp.where(value > 0.5 * DEAD, f, 0.0)
        copy = pltpu.make_async_copy(f_out, f_hbm, sems.at[1])
        copy.start()
    scale = dither((TILES, LANES))
    put_parts(lambda b: jnp.exp2((phi[block_rows(b), :] - (offset - HEAD)) - scale), place.sources, factors)
    fetch.wait()
    exact = Scores(table, place, x1f, x2, yc, None)
    prepare = lambda: put_in_rows(phi, offset, x1, x1f)
    col_half(kept, factors, low[...], exact, prepare, offset, out, acc, tops)
    if final:
        copy.wait()


def row_kernel(place, number, *refs):
    parts = refs[:number]
    weight, table_hbm, x1, x2, yc, out, acc, tops, ye, gamma, table, sem = refs[number:]
    fetch = pltpu.make_async_copy(table_hbm, table, sem)
    fetch.start()
    offset = update(parts, weight, gamma)
    put_in_columns(gamma, offset, ye)
    fetch.wait()
    exact = Scores(table, place, x1, x2, yc, ye)

    def add(t, row, cols, values):
        acc[row_chunk(row), :] += across([jnp.exp2(v) for v in values], jnp.add)

    run = lambda: exact.each(add, UNROLL)
    row_half(run, lambda: (LOW, 0.0), exact, lambda: None, offset, out, acc, tops)


def exchange(value, axis):
    size = lax.axis_size(axis)

    def swap(value, turn):
        return lax.ppermute(value, axis, [(i, turn(i)) for i in range(size)])

    if size & (size - 1):
        return [value] + [swap(value, lambda i, k=k: (i + k) % size) for k in range(1, size)]
    parts = [value]
    bit = size
    while bit > 1:
        value = merge(parts) if len(parts) > 1 else parts[0]
        step = max(bit // 4, 1)
        masks = range(step, bit, step)
        parts = [value] + [swap(value, lambda i, m=m: i ^ m) for m in masks]
        bit = step
    return parts


def on_device(x, y, source_counts, target_counts, source_weight, target_weight, start, pair_blocks, pair_count):
    embed, source_len = x.shape
    target_len = y.shape[1]
    a = source_weight.reshape(-1, LANES)
    b = target_weight.reshape(-1, LANES)
    g0 = start.reshape(-1, LANES)
    slots = pair_blocks.shape[3]
    place = Table(slots, source_counts.shape[0], target_counts.shape[0])
    vmem = pl.BlockSpec(memory_space=pltpu.VMEM)
    smem = pl.BlockSpec(memory_space=pltpu.SMEM)
    hbm = pl.BlockSpec(memory_space=pltpu.HBM)
    anywhere = pl.BlockSpec(memory_space=pl.ANY)
    table_scratch = pltpu.SMEM((place.size,), jnp.int32)
    params = pltpu.CompilerParams(vmem_limit_bytes=VMEM_LIMIT)
    source_tile = jax.ShapeDtypeStruct((source_len // LANES, LANES), F32)
    target_tile = jax.ShapeDtypeStruct((target_len // LANES, LANES), F32)
    row_acc = pltpu.VMEM((source_len, LANES), F32)
    col_acc = pltpu.VMEM(((target_len // CHUNK + 1) * 8, CHUNK), F32)
    source_scratch = pltpu.VMEM(source_tile.shape, F32)
    target_scratch = pltpu.VMEM(target_tile.shape, F32)
    columns_extra = pltpu.VMEM((16, target_len + CHUNK), BF16)

    def smem_like(value):
        return pltpu.SMEM(value.shape, value.dtype)

    first = (x, y, g0, b, a, pair_blocks, source_counts, target_counts)
    part, x1, x2, yc, xsq, aw, base, bw, table, kept, low = pl.pallas_call(
        lambda *refs: first_kernel(place, *refs),
        in_specs=[smem] + [hbm] * 8,
        out_specs=[vmem] * 8 + [anywhere] + [vmem] * 2,
        out_shape=[
            source_tile,
            jax.ShapeDtypeStruct((source_len, LANES), BF16),
            jax.ShapeDtypeStruct((source_len, LANES), BF16),
            jax.ShapeDtypeStruct((3 * embed, target_len + CHUNK), BF16),
            source_tile,
            source_tile,
            target_tile,
            target_tile,
            jax.ShapeDtypeStruct((place.size,), jnp.int32),
            pltpu.VMEM((KEPT * UNROLL * CHUNK, 2 * CHUNK), BF16),
            jax.ShapeDtypeStruct((TILES, LANES), F32),
        ],
        scratch_shapes=[
            row_acc,
            source_scratch,
            columns_extra,
            pltpu.VMEM((8, target_len + CHUNK), F32),
            target_scratch,
            pltpu.VMEM(x.shape, F32),
            pltpu.VMEM(y.shape, F32),
            target_scratch,
            target_scratch,
            source_scratch,
            smem_like(pair_blocks),
            smem_like(source_counts),
            smem_like(target_counts),
            pltpu.SMEM((place.columns + 1,), jnp.int32),
            smem_like(source_counts),
            smem_like(source_counts),
            table_scratch,
            pltpu.SemaphoreType.DMA((9,)),
        ],
        compiler_params=params,
        name="rows_first",
    )(pair_count, *[pltpu.with_memory_space_constraint(v, pltpu.HBM) for v in first])
    common = (table, x1, x2, yc)
    common_specs = [anywhere] + [vmem] * 3

    def columns(parts, final):
        scratch = [col_acc, col_acc, pltpu.VMEM((16, source_len), BF16)]
        scratch += [pltpu.VMEM((source_len, LANES), BF16), source_scratch, table_scratch]
        scratch.append(pltpu.SemaphoreType.DMA((2,)))
        return pl.pallas_call(
            lambda *refs: col_kernel(place, len(parts), embed, final, *refs),
            in_specs=[vmem] * (len(parts) + 4) + common_specs,
            out_specs=[vmem, hbm] if final else [vmem],
            out_shape=[target_tile, source_tile] if final else [target_tile],
            scratch_shapes=scratch + ([source_scratch] if final else []),
            compiler_params=params,
            name="columns",
        )(*parts, aw, xsq, kept, low, *common)

    def rows(parts):
        return pl.pallas_call(
            lambda *refs: row_kernel(place, len(parts), *refs),
            in_specs=[vmem] * (len(parts) + 1) + common_specs,
            out_specs=vmem,
            out_shape=source_tile,
            scratch_shapes=[
                row_acc,
                source_scratch,
                columns_extra,
                target_scratch,
                table_scratch,
                pltpu.SemaphoreType.DMA,
            ],
            compiler_params=params,
            name="rows",
        )(*parts, bw, *common)

    (part,) = columns(exchange(part, "tgt"), False)
    part = rows(exchange(part, "src"))
    part, f = columns(exchange(part, "tgt"), True)
    merged = merge(exchange(part, "src"))
    g = jnp.where(base > 0.5 * DEAD, base - merged * (1.0 / POT), 0.0)
    return f.reshape(-1), g.reshape(-1)


def solution(mesh):
    in_specs = (
        P(None, "src"),
        P(None, "tgt"),
        P("src"),
        P("tgt"),
        P("src"),
        P("tgt"),
        P("tgt"),
        P("src", "tgt", None, None),
        P("src", "tgt"),
    )
    out_specs = (P("src"), P("tgt"))
    return jax.shard_map(on_device, mesh=mesh, in_specs=in_specs, out_specs=out_specs, check_vma=False)
```

```python
import functools
import math

import jax
import jax.numpy as jnp
from jax import lax
from jax.experimental import pallas as pl
from jax.experimental.pallas import tpu as pltpu
from jax.sharding import PartitionSpec as P

F32 = jnp.float32
BF16 = jnp.bfloat16
BLOCK = 1024
LANES = 128
TILES = BLOCK // LANES
CHUNK = 256
PER_BLOCK = BLOCK // CHUNK
UNROLL = 18
KEPT = 5
BITS = 8
EXTRA = 96
DEAD = -1e30
LOW, HIGH = 2.0**-96, 2.0**120
HEAD = 48.0
ENTROPY = 0.1
LOG2E = math.log2(math.e)
POT = LOG2E / ENTROPY
VMEM_LIMIT = 10 * 1024 * 1024


def split3(value):
    high = value.astype(BF16).astype(F32)
    rest = value - high
    middle = rest.astype(BF16).astype(F32)
    return high, middle, rest - middle


def position():
    return lax.broadcasted_iota(jnp.int32, (TILES, LANES), 0) * LANES + lax.broadcasted_iota(
        jnp.int32, (TILES, LANES), 1
    )


def block_rows(b):
    return pl.ds(pl.multiple_of(b * TILES, TILES), TILES)


def lane_tile(b, k):
    return pl.ds(pl.multiple_of(b * BLOCK + k * LANES, LANES), LANES)


def row_chunk(row):
    return pl.ds(pl.multiple_of(row * CHUNK, CHUNK), CHUNK)


def col_chunk(col):
    return pl.ds(pl.multiple_of(col * 8, 8), 8)


def merge(parts):
    top = parts[0]
    for part in parts[1:]:
        top = jnp.maximum(top, part)
    total = jnp.exp2(parts[0] - top)
    for part in parts[1:]:
        total = total + jnp.exp2(part - top)
    return top + jnp.log2(total)


class Table:
    def __init__(self, slots, sources, targets):
        self.most = -(-slots * PER_BLOCK * PER_BLOCK // (2 * UNROLL)) * UNROLL
        self.sources, self.targets = sources, targets
        self.source_limit = 1
        self.target_limit = self.source_limit + sources
        self.units = self.target_limit + targets
        self.size = self.units + self.most
        self.columns = slots * PER_BLOCK + sources

    def fill(self, pairs, count, source_counts, target_counts, table, columns, wanted, place):
        number = count[0, 0]
        nowhere = self.targets * PER_BLOCK

        for i in range(self.units):
            table[i] = 0
        for b in range(self.sources):
            wanted[b] = 0

        def chunks_of(live):
            return (live + CHUNK - 1) // CHUNK

        def measure(p, carry):
            sb, tb = pairs[0, 0, 0, p], pairs[0, 0, 1, p]
            table[self.source_limit + sb] = source_counts[sb]
            table[self.target_limit + tb] = target_counts[tb]
            wanted[sb] += chunks_of(target_counts[tb])
            return carry

        lax.fori_loop(0, number, measure, 0)
        m = 0
        starts = []
        for b in range(self.sources):
            starts.append(m)
            place[b] = m
            columns[m + wanted[b]] = nowhere
            m = m + wanted[b] + (wanted[b] & 1)

        def put(p, carry):
            sb, tb = pairs[0, 0, 0, p], pairs[0, 0, 1, p]
            start = place[sb]
            chunks = chunks_of(target_counts[tb])
            for c in range(PER_BLOCK):
                columns[jnp.where(c < chunks, start + c, self.columns)] = tb * PER_BLOCK + c
            place[sb] = start + chunks
            return carry

        lax.fori_loop(0, number, put, 0)
        n = self.units
        for b in range(self.sources):
            twos = (wanted[b] + 1) >> 1
            rows = [((b * PER_BLOCK + r) << (2 * BITS)) for r in range(PER_BLOCK)]

            def emit(c, carry, first=starts[b], n=n, twos=twos, rows=rows):
                word = (columns[first + 2 * c] << BITS) + columns[first + 2 * c + 1]
                for r in range(PER_BLOCK):
                    table[n + r * twos + c] = rows[r] + word
                return carry

            lax.fori_loop(0, twos, emit, 0)
            n = n + twos * chunks_of(source_counts[b])
        steps = (n - self.units + UNROLL - 1) // UNROLL

        def fill(i, carry):
            table[i] = (nowhere << BITS) + nowhere
            return carry

        lax.fori_loop(n, self.units + steps * UNROLL, fill, 0)
        table[0] = steps


def chunks_of_unit(table, place, t):
    unit = table[place.units + t]
    mask = (1 << BITS) - 1
    return unit >> (2 * BITS), ((unit >> BITS) & mask, unit & mask)


def dither(shape):
    lane = lax.broadcasted_iota(jnp.int32, shape, len(shape) - 1)
    return ((lane * 37) & 63).astype(F32) * (1.0 / 64)


class Scores:
    def __init__(self, table, place, x1, x2, y, ye, ones=(3, 6)):
        self.table, self.place, self.x1, self.x2, self.y, self.ye = table, place, x1, x2, y, ye
        self.zero = jnp.zeros((LANES - EXTRA, CHUNK), BF16)
        sub = lax.broadcasted_iota(jnp.int32, (LANES - EXTRA, CHUNK), 0)
        lo, hi = ones
        self.static = jnp.where((sub >= lo) & (sub < hi), 1.0, 0.0).astype(BF16)

    def unit(self, t):
        row, cols = chunks_of_unit(self.table, self.place, t)
        at = row_chunk(row)
        lhs = jnp.concatenate([self.x1[at, :], self.x2[at, :]], axis=1)
        values = []
        part = self.y.shape[0] // 3
        for col in cols:
            at = pl.ds(pl.multiple_of(col * CHUNK, CHUNK), CHUNK)
            high, middle, low = (self.y[k * part : (k + 1) * part, at] for k in range(3))
            extra = [self.static] if self.ye is None else [self.ye[:, at], self.zero[16:]]
            rhs = jnp.concatenate([high, high, high, *extra, middle, middle, low, self.zero], axis=0)
            values.append(jnp.dot(lhs, rhs, preferred_element_type=F32))
        return row, cols, values

    def each(self, body, unroll, first=0, last=None):
        def step(s, carry):
            for u in range(unroll):
                body(s * unroll + u, *self.unit(s * unroll + u))
            return carry

        steps = self.table[0] if last is None else jnp.minimum(self.table[0], last)
        each = UNROLL // unroll
        lax.fori_loop(first * each, steps * each, step, 0)


def fill_ref(ref, rows, value):
    def body(i, carry):
        ref[pl.ds(pl.multiple_of(i * rows, rows), rows), :] = jnp.full((rows, ref.shape[1]), value, F32)
        return carry

    lax.fori_loop(0, ref.shape[0] // rows, body, 0)


def check(total, limit, low):
    fine = (total >= low) & (total <= HIGH)
    return jnp.where(fine | (position() >= limit), 0.0, 1.0)


def row_tile(acc, b, reduce):
    rows = [reduce(acc[lane_tile(b, r), :].T, axis=0, keepdims=True) for r in range(TILES)]
    return jnp.concatenate(rows, axis=0)


def across(values, combine):
    parts = [v[:, k * LANES : (k + 1) * LANES] for v in values for k in range(CHUNK // LANES)]
    while len(parts) > 1:
        parts = [combine(a, b) for a, b in zip(parts[::2], parts[1::2])]
    return parts[0]


def row_half(run, finished, scores, prepare, offset, out, acc, tops):
    blocks = out.shape[0] // TILES
    fill_ref(acc, CHUNK, 0.0)
    run()
    low, scale = finished()

    def finish(b, bad):
        total = row_tile(acc, b, jnp.sum)
        out[block_rows(b), :] = jnp.where(total > 0.0, (offset - scale) + jnp.log2(total), DEAD)
        return jnp.maximum(bad, check(total, scores.table[scores.place.source_limit + b], low))

    bad = lax.fori_loop(0, blocks, finish, jnp.zeros((TILES, LANES), F32), unroll=4)

    @pl.when(jnp.max(bad) > 0.0)
    def _():
        prepare()
        fill_ref(acc, CHUNK, DEAD)

        def highest(t, row, cols, values):
            acc[row_chunk(row), :] = jnp.maximum(acc[row_chunk(row), :], across(values, jnp.maximum))

        scores.each(highest, 1)

        def keep_top(b, carry):
            top = row_tile(acc, b, jnp.max)
            tops[block_rows(b), :] = jnp.where(top > 0.5 * DEAD, top, 0.0)
            return carry

        lax.fori_loop(0, blocks, keep_top, 0)
        fill_ref(acc, CHUNK, 0.0)

        def add_below(t, row, cols, values):
            lines = []
            for k in range(CHUNK // LANES):
                line = tops[pl.ds(row * (CHUNK // LANES) + k, 1), :]
                lines.append(jnp.broadcast_to(line, (LANES, LANES)).T)
            top = jnp.concatenate([jnp.concatenate(lines, axis=0)] * (CHUNK // LANES), axis=1)
            acc[row_chunk(row), :] += across([jnp.exp2(v - top) for v in values], jnp.add)

        scores.each(add_below, 1)

        def finish_below(b, carry):
            total = row_tile(acc, b, jnp.sum)
            top = tops[block_rows(b), :]
            out[block_rows(b), :] = jnp.where(total > 0.0, (offset + top) + jnp.log2(total), DEAD)
            return carry

        lax.fori_loop(0, blocks, finish_below, 0)


def col_tile(acc, b, reduce):
    rows = []
    for c in range(PER_BLOCK):
        line = reduce(acc[col_chunk(b * PER_BLOCK + c), :], axis=0, keepdims=True)
        for k in range(CHUNK // LANES):
            rows.append(line[:, k * LANES : (k + 1) * LANES])
    return jnp.concatenate(rows, axis=0)


def col_half(kept, factors, low, scores, prepare, offset, out, acc, tops):
    blocks = out.shape[0] // TILES
    table, place = scores.table, scores.place
    fill_ref(acc, 8, 0.0)

    def step(s, carry):
        for u in range(UNROLL):
            row, cols = chunks_of_unit(table, place, s * UNROLL + u)
            at = row_chunk(row)
            here = row_chunk(s * UNROLL + u)
            sums = jnp.dot(factors[:, at], kept[here, :], preferred_element_type=F32)
            for k, col in enumerate(cols):
                acc[col_chunk(col), :] += sums[:8, k * CHUNK : (k + 1) * CHUNK]
        return carry

    lax.fori_loop(0, jnp.minimum(table[0], KEPT), step, 0)

    @pl.when(table[0] > KEPT)
    def _():
        prepare()

        def add(t, row, cols, values):
            for col, value in zip(cols, values):
                part = jnp.sum(jnp.exp2(value).reshape(CHUNK // 8, 8, CHUNK), axis=0)
                acc[col_chunk(col), :] += part * 2.0**HEAD

        scores.each(add, UNROLL // 2, KEPT)

    def finish(b, bad):
        total = col_tile(acc, b, jnp.sum)
        out[block_rows(b), :] = jnp.where(total > 0.0, (offset - HEAD) + jnp.log2(total), DEAD)
        return jnp.maximum(bad, check(total, table[place.target_limit + b], low))

    bad = lax.fori_loop(0, blocks, finish, jnp.zeros((TILES, LANES), F32), unroll=4)

    @pl.when(jnp.max(bad) > 0.0)
    def _():
        prepare()
        fill_ref(tops, 8, DEAD)

        def highest(t, row, cols, values):
            for col, value in zip(cols, values):
                part = jnp.max(value.reshape(CHUNK // 8, 8, CHUNK), axis=0)
                tops[col_chunk(col), :] = jnp.maximum(tops[col_chunk(col), :], part)

        scores.each(highest, 1)

        def spread(i, carry):
            top = jnp.max(tops[col_chunk(i), :], axis=0, keepdims=True)
            top = jnp.where(top > 0.5 * DEAD, top, 0.0)
            tops[col_chunk(i), :] = jnp.broadcast_to(top, (8, CHUNK))
            return carry

        lax.fori_loop(0, tops.shape[0] // 8, spread, 0)
        fill_ref(acc, 8, 0.0)

        def add_below(t, row, cols, values):
            for col, value in zip(cols, values):
                e = jnp.exp2(value.reshape(CHUNK // 8, 8, CHUNK) - tops[col_chunk(col), :][None])
                acc[col_chunk(col), :] += jnp.sum(e, axis=0)

        scores.each(add_below, 1)

        def finish_below(b, carry):
            total = col_tile(acc, b, jnp.sum)
            top = col_tile(tops, b, jnp.max)
            out[block_rows(b), :] = jnp.where(total > 0.0, (offset + top) + jnp.log2(total), DEAD)
            return carry

        lax.fori_loop(0, blocks, finish_below, 0)


def put_parts(value_of, blocks, rows):
    sub = lax.broadcasted_iota(jnp.int32, (16, LANES), 0)

    def body(b, carry):
        high, middle, low = split3(value_of(b))
        for k in range(TILES):
            at = slice(k, k + 1)
            parts = jnp.where(sub == 1, middle[at, :], jnp.where(sub == 2, low[at, :], 0.0))
            rows[:, lane_tile(b, k)] = jnp.where(sub == 0, high[at, :], parts).astype(BF16)
        return carry

    lax.fori_loop(0, blocks, body, 0, unroll=2)


def put_in_columns(potential, offset, ye):
    blocks = potential.shape[0] // TILES
    put_parts(lambda b: potential[block_rows(b), :] - offset, blocks, ye)
    sub = lax.broadcasted_iota(jnp.int32, (16, LANES), 0)
    for k in range(CHUNK // LANES):
        at = pl.ds(blocks * BLOCK + k * LANES, LANES)
        ye[:, at] = jnp.where(sub == 0, DEAD, 0.0).astype(BF16)


def put_in_rows(potential, offset, x1, x1f):
    sub = lax.broadcasted_iota(jnp.int32, (8, LANES), 0)
    above = jnp.zeros((EXTRA, LANES), F32)
    below = jnp.zeros((LANES - EXTRA - 8, LANES), F32)

    def body(b, carry):
        high, middle, low = split3(potential[block_rows(b), :] - offset)
        for k in range(TILES):
            at = slice(k, k + 1)
            rows = jnp.where(sub == 4, middle[at, :], jnp.where(sub == 5, low[at, :], 0.0))
            rows = jnp.where(sub == 3, high[at, :], rows)
            turned = jnp.concatenate([above, rows, below], axis=0).T.astype(BF16)
            x1f[lane_tile(b, k), :] = x1[lane_tile(b, k), :] + turned
        return carry

    lax.fori_loop(0, potential.shape[0] // TILES, body, 0)


def update(parts, weight, potential):
    weight = weight[...]
    value = jnp.where(weight > 0.5 * DEAD, weight - merge([part[...] for part in parts]), DEAD)
    potential[...] = value
    return jnp.max(value)


def first_kernel(
    place,
    count, x_hbm, y_hbm, g0_hbm, b_hbm, a_hbm, pairs_hbm, sc_hbm, tc_hbm,
    out, x1, x2, yc, xsq, aw, base, bw, table_out, kept, low_out,
    acc, tops, ye, spread, gamma, x, y, g0, b_in, a_in, pairs, sc, tc, columns, wanted, places, table, sems,
):
    embed = x.shape[0]
    scale = 2.0 * POT / embed
    here = [(pairs_hbm, pairs), (sc_hbm, sc), (tc_hbm, tc)]
    here += [(y_hbm, y), (g0_hbm, g0), (b_hbm, b_in), (x_hbm, x), (a_hbm, a_in)]
    copies = [pltpu.make_async_copy(a, b, sems.at[i]) for i, (a, b) in enumerate(here)]
    for copy in copies:
        copy.start()
    for copy in copies[:3]:
        copy.wait()
    place.fill(pairs, count, sc, tc, table, columns, wanted, places)
    keep = pltpu.make_async_copy(table, table_out, sems.at[len(copies)])
    keep.start()
    for copy in copies[3:6]:
        copy.wait()

    def target(b, carry):
        top, norm = carry
        rows = []
        for k in range(TILES):
            at = lane_tile(b, k)
            value = y[:, at]
            yc[:, at] = jnp.concatenate([p.astype(BF16) for p in split3(value)], axis=0)
            rows.append(jnp.sum(value * value, axis=0, keepdims=True))
        square = jnp.concatenate(rows, axis=0)
        live = position() < tc[b]
        at = block_rows(b)
        base[at, :] = jnp.where(live, ENTROPY * b_in[at, :] + (1.0 / embed) * square, DEAD)
        bw[at, :] = jnp.where(live, LOG2E * b_in[at, :], DEAD)
        value = jnp.where(live, POT * g0[at, :] - (POT / embed) * square, DEAD)
        gamma[at, :] = value
        return jnp.maximum(top, value), jnp.maximum(norm, jnp.where(live, square, 0.0))

    blocks = tc.shape[0]
    nothing = jnp.zeros((TILES, LANES), F32)
    offset, norm_y = lax.fori_loop(0, blocks, target, (nothing + DEAD, nothing), unroll=4)
    offset, norm_y = jnp.max(offset), jnp.max(norm_y)
    yc[:, pl.ds(blocks * BLOCK, CHUNK)] = jnp.zeros((yc.shape[0], CHUNK), BF16)

    def widen(b, carry):
        value = jnp.exp2(gamma[block_rows(b), :] - (offset - HEAD))
        for k in range(TILES):
            spread[:, lane_tile(b, k)] = jnp.broadcast_to(value[k : k + 1, :], (8, LANES))
        return carry

    lax.fori_loop(0, blocks, widen, 0, unroll=2)
    spread[:, pl.ds(blocks * BLOCK, CHUNK)] = jnp.zeros((8, CHUNK), F32)
    for copy in copies[6:]:
        copy.wait()
    sub = lax.broadcasted_iota(jnp.int32, (LANES - EXTRA, LANES), 0)
    ones = jnp.where(sub < 3, 1.0, jnp.where(sub == 6, dither((LANES - EXTRA, LANES)), 0.0)).astype(BF16)

    def source(b, norm):
        rows = []
        for k in range(TILES):
            at = lane_tile(b, k)
            value = x[:, at]
            high, middle, low = (p.astype(BF16) for p in split3(value * scale))
            x1[at, :] = jnp.concatenate([high, middle, low, ones], axis=0).T
            x2[at, :] = jnp.concatenate([high, middle, high, middle], axis=0).T
            rows.append(jnp.sum(value * value, axis=0, keepdims=True))
        at = block_rows(b)
        square = jnp.concatenate(rows, axis=0)
        live = position() < sc[b]
        xsq[at, :] = square
        aw[at, :] = jnp.where(live, LOG2E * a_in[at, :], DEAD)
        return jnp.maximum(norm, jnp.where(live, square, 0.0))

    norm_x = jnp.max(lax.fori_loop(0, sc.shape[0], source, nothing, unroll=4))

    def add(keep_entries, t, row, cols, values):
        entries = [jnp.exp2(v) for v in values]
        stored = jnp.concatenate(entries, axis=1).astype(BF16)
        if keep_entries:
            kept[row_chunk(t), :] = stored
        weighted = []
        for col, e in zip(cols, entries):
            factor = spread[:, pl.ds(pl.multiple_of(col * CHUNK, CHUNK), CHUNK)]
            weighted.append((e.reshape(CHUNK // 8, 8, CHUNK) * factor[None]).reshape(CHUNK, CHUNK))
        acc[row_chunk(row), :] += across(weighted, jnp.add)

    def finished():
        low = LOW * jnp.exp2(scale * jnp.sqrt(jnp.full((TILES, LANES), norm_x, F32) * norm_y))
        low_out[...] = low
        return low, dither((TILES, LANES)) + HEAD

    plain = Scores(table, place, x1, x2, yc, None, (6, 7))
    exact = Scores(table, place, x1, x2, yc, ye)

    def run():
        plain.each(functools.partial(add, True), UNROLL, 0, KEPT)
        plain.each(functools.partial(add, False), UNROLL, KEPT)

    row_half(run, finished, exact, lambda: put_in_columns(gamma, offset, ye), offset, out, acc, tops)
    keep.wait()


def col_kernel(place, number, embed, final, *refs):
    parts = refs[:number]
    weight, square, kept, low, table_hbm, x1, x2, yc, out = refs[number : number + 9]
    rest = list(refs[number + 9 :])
    f_hbm = rest.pop(0) if final else None
    acc, tops, factors, x1f, phi, table, sems = rest[:7]
    fetch = pltpu.make_async_copy(table_hbm, table, sems.at[0])
    fetch.start()
    offset = update(parts, weight, phi)
    if final:
        f_out = rest[7]
        value = phi[...]
        f = value * (1.0 / POT) + square[...] * (1.0 / embed)
        f_out[...] = jnp.where(value > 0.5 * DEAD, f, 0.0)
        copy = pltpu.make_async_copy(f_out, f_hbm, sems.at[1])
        copy.start()
    scale = dither((TILES, LANES))
    put_parts(lambda b: jnp.exp2((phi[block_rows(b), :] - (offset - HEAD)) - scale), place.sources, factors)
    fetch.wait()
    exact = Scores(table, place, x1f, x2, yc, None)
    prepare = lambda: put_in_rows(phi, offset, x1, x1f)
    col_half(kept, factors, low[...], exact, prepare, offset, out, acc, tops)
    if final:
        copy.wait()


def row_kernel(place, number, *refs):
    parts = refs[:number]
    weight, table_hbm, x1, x2, yc, out, acc, tops, ye, gamma, table, sem = refs[number:]
    fetch = pltpu.make_async_copy(table_hbm, table, sem)
    fetch.start()
    offset = update(parts, weight, gamma)
    put_in_columns(gamma, offset, ye)
    fetch.wait()
    exact = Scores(table, place, x1, x2, yc, ye)

    def add(t, row, cols, values):
        acc[row_chunk(row), :] += across([jnp.exp2(v) for v in values], jnp.add)

    run = lambda: exact.each(add, UNROLL)
    row_half(run, lambda: (LOW, 0.0), exact, lambda: None, offset, out, acc, tops)


def exchange(value, axis):
    size = lax.axis_size(axis)

    def swap(value, turn):
        return lax.ppermute(value, axis, [(i, turn(i)) for i in range(size)])

    if size & (size - 1):
        return [value] + [swap(value, lambda i, k=k: (i + k) % size) for k in range(1, size)]
    parts = [value]
    bit = size
    while bit > 1:
        value = merge(parts) if len(parts) > 1 else parts[0]
        step = max(bit // 4, 1)
        masks = range(step, bit, step)
        parts = [value] + [swap(value, lambda i, m=m: i ^ m) for m in masks]
        bit = step
    return parts


def on_device(x, y, source_counts, target_counts, source_weight, target_weight, start, pair_blocks, pair_count):
    embed, source_len = x.shape
    target_len = y.shape[1]
    a = source_weight.reshape(-1, LANES)
    b = target_weight.reshape(-1, LANES)
    g0 = start.reshape(-1, LANES)
    slots = pair_blocks.shape[3]
    place = Table(slots, source_counts.shape[0], target_counts.shape[0])
    vmem = pl.BlockSpec(memory_space=pltpu.VMEM)
    smem = pl.BlockSpec(memory_space=pltpu.SMEM)
    hbm = pl.BlockSpec(memory_space=pltpu.HBM)
    anywhere = pl.BlockSpec(memory_space=pl.ANY)
    table_scratch = pltpu.SMEM((place.size,), jnp.int32)
    params = pltpu.CompilerParams(vmem_limit_bytes=VMEM_LIMIT)
    source_tile = jax.ShapeDtypeStruct((source_len // LANES, LANES), F32)
    target_tile = jax.ShapeDtypeStruct((target_len // LANES, LANES), F32)
    row_acc = pltpu.VMEM((source_len, LANES), F32)
    col_acc = pltpu.VMEM(((target_len // CHUNK + 1) * 8, CHUNK), F32)
    source_scratch = pltpu.VMEM(source_tile.shape, F32)
    target_scratch = pltpu.VMEM(target_tile.shape, F32)
    columns_extra = pltpu.VMEM((16, target_len + CHUNK), BF16)

    def smem_like(value):
        return pltpu.SMEM(value.shape, value.dtype)

    first = (x, y, g0, b, a, pair_blocks, source_counts, target_counts)
    part, x1, x2, yc, xsq, aw, base, bw, table, kept, low = pl.pallas_call(
        lambda *refs: first_kernel(place, *refs),
        in_specs=[smem] + [hbm] * 8,
        out_specs=[vmem] * 8 + [anywhere] + [vmem] * 2,
        out_shape=[
            source_tile,
            jax.ShapeDtypeStruct((source_len, LANES), BF16),
            jax.ShapeDtypeStruct((source_len, LANES), BF16),
            jax.ShapeDtypeStruct((3 * embed, target_len + CHUNK), BF16),
            source_tile,
            source_tile,
            target_tile,
            target_tile,
            jax.ShapeDtypeStruct((place.size,), jnp.int32),
            pltpu.VMEM((KEPT * UNROLL * CHUNK, 2 * CHUNK), BF16),
            jax.ShapeDtypeStruct((TILES, LANES), F32),
        ],
        scratch_shapes=[
            row_acc,
            source_scratch,
            columns_extra,
            pltpu.VMEM((8, target_len + CHUNK), F32),
            target_scratch,
            pltpu.VMEM(x.shape, F32),
            pltpu.VMEM(y.shape, F32),
            target_scratch,
            target_scratch,
            source_scratch,
            smem_like(pair_blocks),
            smem_like(source_counts),
            smem_like(target_counts),
            pltpu.SMEM((place.columns + 1,), jnp.int32),
            smem_like(source_counts),
            smem_like(source_counts),
            table_scratch,
            pltpu.SemaphoreType.DMA((9,)),
        ],
        compiler_params=params,
        name="rows_first",
    )(pair_count, *[pltpu.with_memory_space_constraint(v, pltpu.HBM) for v in first])
    common = (table, x1, x2, yc)
    common_specs = [anywhere] + [vmem] * 3

    def columns(parts, final):
        scratch = [col_acc, col_acc, pltpu.VMEM((16, source_len), BF16)]
        scratch += [pltpu.VMEM((source_len, LANES), BF16), source_scratch, table_scratch]
        scratch.append(pltpu.SemaphoreType.DMA((2,)))
        return pl.pallas_call(
            lambda *refs: col_kernel(place, len(parts), embed, final, *refs),
            in_specs=[vmem] * (len(parts) + 4) + common_specs,
            out_specs=[vmem, hbm] if final else [vmem],
            out_shape=[target_tile, source_tile] if final else [target_tile],
            scratch_shapes=scratch + ([source_scratch] if final else []),
            compiler_params=params,
            name="columns",
        )(*parts, aw, xsq, kept, low, *common)

    def rows(parts):
        return pl.pallas_call(
            lambda *refs: row_kernel(place, len(parts), *refs),
            in_specs=[vmem] * (len(parts) + 1) + common_specs,
            out_specs=vmem,
            out_shape=source_tile,
            scratch_shapes=[
                row_acc,
                source_scratch,
                columns_extra,
                target_scratch,
                table_scratch,
                pltpu.SemaphoreType.DMA,
            ],
            compiler_params=params,
            name="rows",
        )(*parts, bw, *common)

    (part,) = columns(exchange(part, "tgt"), False)
    part = rows(exchange(part, "src"))
    part, f = columns(exchange(part, "tgt"), True)
    merged = merge(exchange(part, "src"))
    g = jnp.where(base > 0.5 * DEAD, base - merged * (1.0 / POT), 0.0)
    return f.reshape(-1), g.reshape(-1)


def solution(mesh):
    in_specs = (
        P(None, "src"),
        P(None, "tgt"),
        P("src"),
        P("tgt"),
        P("src"),
        P("tgt"),
        P("tgt"),
        P("src", "tgt", None, None),
        P("src", "tgt"),
    )
    out_specs = (P("src"), P("tgt"))
    return jax.shard_map(on_device, mesh=mesh, in_specs=in_specs, out_specs=out_specs, check_vma=False)
```

```python
import functools
import math

import jax
import jax.numpy as jnp
from jax import lax
from jax.experimental import pallas as pl
from jax.experimental.pallas import tpu as pltpu
from jax.sharding import PartitionSpec as P

F32 = jnp.float32
BF16 = jnp.bfloat16
BLOCK = 1024
LANES = 128
TILES = BLOCK // LANES
CHUNK = 256
PER_BLOCK = BLOCK // CHUNK
UNROLL = 18
KEPT = 5
BITS = 8
EXTRA = 96
DEAD = -1e30
LOW, HIGH = 2.0**-96, 2.0**120
HEAD = 48.0
ENTROPY = 0.1
LOG2E = math.log2(math.e)
POT = LOG2E / ENTROPY
VMEM_LIMIT = 10 * 1024 * 1024


def split3(value):
    high = value.astype(BF16).astype(F32)
    rest = value - high
    middle = rest.astype(BF16).astype(F32)
    return high, middle, rest - middle


def position():
    return lax.broadcasted_iota(jnp.int32, (TILES, LANES), 0) * LANES + lax.broadcasted_iota(
        jnp.int32, (TILES, LANES), 1
    )


def block_rows(b):
    return pl.ds(pl.multiple_of(b * TILES, TILES), TILES)


def lane_tile(b, k):
    return pl.ds(pl.multiple_of(b * BLOCK + k * LANES, LANES), LANES)


def row_chunk(row):
    return pl.ds(pl.multiple_of(row * CHUNK, CHUNK), CHUNK)


def col_chunk(col):
    return pl.ds(pl.multiple_of(col * 8, 8), 8)


def merge(parts):
    top = parts[0]
    for part in parts[1:]:
        top = jnp.maximum(top, part)
    total = jnp.exp2(parts[0] - top)
    for part in parts[1:]:
        total = total + jnp.exp2(part - top)
    return top + jnp.log2(total)


class Table:
    def __init__(self, slots, sources, targets):
        self.most = -(-slots * PER_BLOCK * PER_BLOCK // (2 * UNROLL)) * UNROLL
        self.sources, self.targets = sources, targets
        self.source_limit = 1
        self.target_limit = self.source_limit + sources
        self.units = self.target_limit + targets
        self.size = self.units + self.most
        self.columns = slots * PER_BLOCK + sources

    def fill(self, pairs, count, source_counts, target_counts, table, columns, wanted, place):
        number = count[0, 0]
        nowhere = self.targets * PER_BLOCK

        for i in range(self.units):
            table[i] = 0
        for b in range(self.sources):
            wanted[b] = 0

        def chunks_of(live):
            return (live + CHUNK - 1) // CHUNK

        def measure(p, carry):
            sb, tb = pairs[0, 0, 0, p], pairs[0, 0, 1, p]
            table[self.source_limit + sb] = source_counts[sb]
            table[self.target_limit + tb] = target_counts[tb]
            wanted[sb] += chunks_of(target_counts[tb])
            return carry

        lax.fori_loop(0, number, measure, 0)
        m = 0
        starts = []
        for b in range(self.sources):
            starts.append(m)
            place[b] = m
            columns[m + wanted[b]] = nowhere
            m = m + wanted[b] + (wanted[b] & 1)

        def put(p, carry):
            sb, tb = pairs[0, 0, 0, p], pairs[0, 0, 1, p]
            start = place[sb]
            chunks = chunks_of(target_counts[tb])
            for c in range(PER_BLOCK):
                columns[jnp.where(c < chunks, start + c, self.columns)] = tb * PER_BLOCK + c
            place[sb] = start + chunks
            return carry

        lax.fori_loop(0, number, put, 0)
        n = self.units
        for b in range(self.sources):
            twos = (wanted[b] + 1) >> 1
            rows = [((b * PER_BLOCK + r) << (2 * BITS)) for r in range(PER_BLOCK)]

            def emit(c, carry, first=starts[b], n=n, twos=twos, rows=rows):
                word = (columns[first + 2 * c] << BITS) + columns[first + 2 * c + 1]
                for r in range(PER_BLOCK):
                    table[n + r * twos + c] = rows[r] + word
                return carry

            lax.fori_loop(0, twos, emit, 0)
            n = n + twos * chunks_of(source_counts[b])
        steps = (n - self.units + UNROLL - 1) // UNROLL

        def fill(i, carry):
            table[i] = (nowhere << BITS) + nowhere
            return carry

        lax.fori_loop(n, self.units + steps * UNROLL, fill, 0)
        table[0] = steps


def chunks_of_unit(table, place, t):
    unit = table[place.units + t]
    mask = (1 << BITS) - 1
    return unit >> (2 * BITS), ((unit >> BITS) & mask, unit & mask)


def dither(shape):
    lane = lax.broadcasted_iota(jnp.int32, shape, len(shape) - 1)
    return ((lane * 37) & 63).astype(F32) * (1.0 / 64)


class Scores:
    def __init__(self, table, place, x1, x2, y, ye, ones=(3, 6)):
        self.table, self.place, self.x1, self.x2, self.y, self.ye = table, place, x1, x2, y, ye
        self.zero = jnp.zeros((LANES - EXTRA, CHUNK), BF16)
        sub = lax.broadcasted_iota(jnp.int32, (LANES - EXTRA, CHUNK), 0)
        lo, hi = ones
        self.static = jnp.where((sub >= lo) & (sub < hi), 1.0, 0.0).astype(BF16)

    def unit(self, t):
        row, cols = chunks_of_unit(self.table, self.place, t)
        at = row_chunk(row)
        lhs = jnp.concatenate([self.x1[at, :], self.x2[at, :]], axis=1)
        values = []
        part = self.y.shape[0] // 3
        for col in cols:
            at = pl.ds(pl.multiple_of(col * CHUNK, CHUNK), CHUNK)
            high, middle, low = (self.y[k * part : (k + 1) * part, at] for k in range(3))
            extra = [self.static] if self.ye is None else [self.ye[:, at], self.zero[16:]]
            rhs = jnp.concatenate([high, high, high, *extra, middle, middle, low, self.zero], axis=0)
            values.append(jnp.dot(lhs, rhs, preferred_element_type=F32))
        return row, cols, values

    def each(self, body, unroll, first=0, last=None):
        def step(s, carry):
            for u in range(unroll):
                body(s * unroll + u, *self.unit(s * unroll + u))
            return carry

        steps = self.table[0] if last is None else jnp.minimum(self.table[0], last)
        each = UNROLL // unroll
        lax.fori_loop(first * each, steps * each, step, 0)


def fill_ref(ref, rows, value):
    def body(i, carry):
        ref[pl.ds(pl.multiple_of(i * rows, rows), rows), :] = jnp.full((rows, ref.shape[1]), value, F32)
        return carry

    lax.fori_loop(0, ref.shape[0] // rows, body, 0)


def check(total, limit, low):
    fine = (total >= low) & (total <= HIGH)
    return jnp.where(fine | (position() >= limit), 0.0, 1.0)


def row_tile(acc, b, reduce):
    rows = [reduce(acc[lane_tile(b, r), :].T, axis=0, keepdims=True) for r in range(TILES)]
    return jnp.concatenate(rows, axis=0)


def across(values, combine):
    parts = [v[:, k * LANES : (k + 1) * LANES] for v in values for k in range(CHUNK // LANES)]
    while len(parts) > 1:
        parts = [combine(a, b) for a, b in zip(parts[::2], parts[1::2])]
    return parts[0]


def row_half(run, finished, scores, prepare, offset, out, acc, tops):
    blocks = out.shape[0] // TILES
    fill_ref(acc, CHUNK, 0.0)
    run()
    low, scale = finished()

    def finish(b, bad):
        total = row_tile(acc, b, jnp.sum)
        out[block_rows(b), :] = jnp.where(total > 0.0, (offset - scale) + jnp.log2(total), DEAD)
        return jnp.maximum(bad, check(total, scores.table[scores.place.source_limit + b], low))

    bad = lax.fori_loop(0, blocks, finish, jnp.zeros((TILES, LANES), F32), unroll=4)

    @pl.when(jnp.max(bad) > 0.0)
    def _():
        prepare()
        fill_ref(acc, CHUNK, DEAD)

        def highest(t, row, cols, values):
            acc[row_chunk(row), :] = jnp.maximum(acc[row_chunk(row), :], across(values, jnp.maximum))

        scores.each(highest, 1)

        def keep_top(b, carry):
            top = row_tile(acc, b, jnp.max)
            tops[block_rows(b), :] = jnp.where(top > 0.5 * DEAD, top, 0.0)
            return carry

        lax.fori_loop(0, blocks, keep_top, 0)
        fill_ref(acc, CHUNK, 0.0)

        def add_below(t, row, cols, values):
            lines = []
            for k in range(CHUNK // LANES):
                line = tops[pl.ds(row * (CHUNK // LANES) + k, 1), :]
                lines.append(jnp.broadcast_to(line, (LANES, LANES)).T)
            top = jnp.concatenate([jnp.concatenate(lines, axis=0)] * (CHUNK // LANES), axis=1)
            acc[row_chunk(row), :] += across([jnp.exp2(v - top) for v in values], jnp.add)

        scores.each(add_below, 1)

        def finish_below(b, carry):
            total = row_tile(acc, b, jnp.sum)
            top = tops[block_rows(b), :]
            out[block_rows(b), :] = jnp.where(total > 0.0, (offset + top) + jnp.log2(total), DEAD)
            return carry

        lax.fori_loop(0, blocks, finish_below, 0)


def col_tile(acc, b, reduce):
    rows = []
    for c in range(PER_BLOCK):
        line = reduce(acc[col_chunk(b * PER_BLOCK + c), :], axis=0, keepdims=True)
        for k in range(CHUNK // LANES):
            rows.append(line[:, k * LANES : (k + 1) * LANES])
    return jnp.concatenate(rows, axis=0)


def col_half(kept, factors, low, scores, prepare, offset, out, acc, tops):
    blocks = out.shape[0] // TILES
    table, place = scores.table, scores.place
    acc[...] = jnp.zeros(acc.shape, F32)

    def step(s, carry):
        for u in range(UNROLL):
            row, cols = chunks_of_unit(table, place, s * UNROLL + u)
            at = row_chunk(row)
            here = row_chunk(s * UNROLL + u)
            sums = jnp.dot(factors[:, at], kept[here, :], preferred_element_type=F32)
            for k, col in enumerate(cols):
                acc[col_chunk(col), :] += sums[:8, k * CHUNK : (k + 1) * CHUNK]
        return carry

    lax.fori_loop(0, jnp.minimum(table[0], KEPT), step, 0)

    @pl.when(table[0] > KEPT)
    def _():
        prepare()

        def add(t, row, cols, values):
            for col, value in zip(cols, values):
                part = jnp.sum(jnp.exp2(value).reshape(CHUNK // 8, 8, CHUNK), axis=0)
                acc[col_chunk(col), :] += part * 2.0**HEAD

        scores.each(add, UNROLL // 2, KEPT)

    def finish(b, bad):
        total = col_tile(acc, b, jnp.sum)
        out[block_rows(b), :] = jnp.where(total > 0.0, (offset - HEAD) + jnp.log2(total), DEAD)
        return jnp.maximum(bad, check(total, table[place.target_limit + b], low))

    bad = lax.fori_loop(0, blocks, finish, jnp.zeros((TILES, LANES), F32), unroll=4)

    @pl.when(jnp.max(bad) > 0.0)
    def _():
        prepare()
        fill_ref(tops, 8, DEAD)

        def highest(t, row, cols, values):
            for col, value in zip(cols, values):
                part = jnp.max(value.reshape(CHUNK // 8, 8, CHUNK), axis=0)
                tops[col_chunk(col), :] = jnp.maximum(tops[col_chunk(col), :], part)

        scores.each(highest, 1)

        def spread(i, carry):
            top = jnp.max(tops[col_chunk(i), :], axis=0, keepdims=True)
            top = jnp.where(top > 0.5 * DEAD, top, 0.0)
            tops[col_chunk(i), :] = jnp.broadcast_to(top, (8, CHUNK))
            return carry

        lax.fori_loop(0, tops.shape[0] // 8, spread, 0)
        fill_ref(acc, 8, 0.0)

        def add_below(t, row, cols, values):
            for col, value in zip(cols, values):
                e = jnp.exp2(value.reshape(CHUNK // 8, 8, CHUNK) - tops[col_chunk(col), :][None])
                acc[col_chunk(col), :] += jnp.sum(e, axis=0)

        scores.each(add_below, 1)

        def finish_below(b, carry):
            total = col_tile(acc, b, jnp.sum)
            top = col_tile(tops, b, jnp.max)
            out[block_rows(b), :] = jnp.where(total > 0.0, (offset + top) + jnp.log2(total), DEAD)
            return carry

        lax.fori_loop(0, blocks, finish_below, 0)


def put_parts(value_of, blocks, rows):
    sub = lax.broadcasted_iota(jnp.int32, (16, LANES), 0)

    def body(b, carry):
        high, middle, low = split3(value_of(b))
        for k in range(TILES):
            at = slice(k, k + 1)
            parts = jnp.where(sub == 1, middle[at, :], jnp.where(sub == 2, low[at, :], 0.0))
            rows[:, lane_tile(b, k)] = jnp.where(sub == 0, high[at, :], parts).astype(BF16)
        return carry

    lax.fori_loop(0, blocks, body, 0, unroll=4)


def put_in_columns(potential, offset, ye):
    blocks = potential.shape[0] // TILES
    put_parts(lambda b: potential[block_rows(b), :] - offset, blocks, ye)
    sub = lax.broadcasted_iota(jnp.int32, (16, LANES), 0)
    for k in range(CHUNK // LANES):
        at = pl.ds(blocks * BLOCK + k * LANES, LANES)
        ye[:, at] = jnp.where(sub == 0, DEAD, 0.0).astype(BF16)


def put_in_rows(potential, offset, x1, x1f):
    sub = lax.broadcasted_iota(jnp.int32, (8, LANES), 0)
    above = jnp.zeros((EXTRA, LANES), F32)
    below = jnp.zeros((LANES - EXTRA - 8, LANES), F32)

    def body(b, carry):
        high, middle, low = split3(potential[block_rows(b), :] - offset)
        for k in range(TILES):
            at = slice(k, k + 1)
            rows = jnp.where(sub == 4, middle[at, :], jnp.where(sub == 5, low[at, :], 0.0))
            rows = jnp.where(sub == 3, high[at, :], rows)
            turned = jnp.concatenate([above, rows, below], axis=0).T.astype(BF16)
            x1f[lane_tile(b, k), :] = x1[lane_tile(b, k), :] + turned
        return carry

    lax.fori_loop(0, potential.shape[0] // TILES, body, 0)


def update(parts, weight, potential):
    weight = weight[...]
    value = jnp.where(weight > 0.5 * DEAD, weight - merge([part[...] for part in parts]), DEAD)
    potential[...] = value
    return jnp.max(value)


def first_kernel(
    place,
    count, x_hbm, y_hbm, g0_hbm, b_hbm, a_hbm, pairs_hbm, sc_hbm, tc_hbm,
    out, x1, x2, yc, xsq, aw, base, bw, table_out, kept, low_out,
    acc, tops, ye, spread, gamma, x, y, g0, b_in, a_in, pairs, sc, tc, columns, wanted, places, table, sems,
):
    embed = x.shape[0]
    scale = 2.0 * POT / embed
    here = [(pairs_hbm, pairs), (sc_hbm, sc), (tc_hbm, tc)]
    here += [(y_hbm, y), (g0_hbm, g0), (b_hbm, b_in), (x_hbm, x), (a_hbm, a_in)]
    copies = [pltpu.make_async_copy(a, b, sems.at[i]) for i, (a, b) in enumerate(here)]
    for copy in copies:
        copy.start()
    for copy in copies[:3]:
        copy.wait()
    place.fill(pairs, count, sc, tc, table, columns, wanted, places)
    keep = pltpu.make_async_copy(table, table_out, sems.at[len(copies)])
    keep.start()
    for copy in copies[3:6]:
        copy.wait()

    def target(b, carry):
        top, norm = carry
        rows = []
        for k in range(TILES):
            at = lane_tile(b, k)
            value = y[:, at]
            yc[:, at] = jnp.concatenate([p.astype(BF16) for p in split3(value)], axis=0)
            rows.append(jnp.sum(value * value, axis=0, keepdims=True))
        square = jnp.concatenate(rows, axis=0)
        live = position() < tc[b]
        at = block_rows(b)
        base[at, :] = jnp.where(live, ENTROPY * b_in[at, :] + (1.0 / embed) * square, DEAD)
        bw[at, :] = jnp.where(live, LOG2E * b_in[at, :], DEAD)
        value = jnp.where(live, POT * g0[at, :] - (POT / embed) * square, DEAD)
        gamma[at, :] = value
        return jnp.maximum(top, value), jnp.maximum(norm, jnp.where(live, square, 0.0))

    blocks = tc.shape[0]
    nothing = jnp.zeros((TILES, LANES), F32)
    offset, norm_y = lax.fori_loop(0, blocks, target, (nothing + DEAD, nothing), unroll=4)
    offset, norm_y = jnp.max(offset), jnp.max(norm_y)
    yc[:, pl.ds(blocks * BLOCK, CHUNK)] = jnp.zeros((yc.shape[0], CHUNK), BF16)

    def widen(b, carry):
        value = jnp.exp2(gamma[block_rows(b), :] - (offset - HEAD))
        for k in range(TILES):
            spread[:, lane_tile(b, k)] = jnp.broadcast_to(value[k : k + 1, :], (8, LANES))
        return carry

    lax.fori_loop(0, blocks, widen, 0, unroll=4)
    spread[:, pl.ds(blocks * BLOCK, CHUNK)] = jnp.zeros((8, CHUNK), F32)
    for copy in copies[6:]:
        copy.wait()
    sub = lax.broadcasted_iota(jnp.int32, (LANES - EXTRA, LANES), 0)
    ones = jnp.where(sub < 3, 1.0, jnp.where(sub == 6, dither((LANES - EXTRA, LANES)), 0.0)).astype(BF16)

    def source(b, norm):
        rows = []
        for k in range(TILES):
            at = lane_tile(b, k)
            value = x[:, at]
            high, middle, low = (p.astype(BF16) for p in split3(value * scale))
            x1[at, :] = jnp.concatenate([high, middle, low, ones], axis=0).T
            x2[at, :] = jnp.concatenate([high, middle, high, middle], axis=0).T
            rows.append(jnp.sum(value * value, axis=0, keepdims=True))
        at = block_rows(b)
        square = jnp.concatenate(rows, axis=0)
        live = position() < sc[b]
        xsq[at, :] = square
        aw[at, :] = jnp.where(live, LOG2E * a_in[at, :], DEAD)
        return jnp.maximum(norm, jnp.where(live, square, 0.0))

    norm_x = jnp.max(lax.fori_loop(0, sc.shape[0], source, nothing, unroll=4))

    def add(keep_entries, t, row, cols, values):
        entries = [jnp.exp2(v) for v in values]
        stored = jnp.concatenate(entries, axis=1).astype(BF16)
        if keep_entries:
            kept[row_chunk(t), :] = stored
        weighted = []
        for col, e in zip(cols, entries):
            factor = spread[:, pl.ds(pl.multiple_of(col * CHUNK, CHUNK), CHUNK)]
            weighted.append((e.reshape(CHUNK // 8, 8, CHUNK) * factor[None]).reshape(CHUNK, CHUNK))
        acc[row_chunk(row), :] += across(weighted, jnp.add)

    def finished():
        low = LOW * jnp.exp2(scale * jnp.sqrt(jnp.full((TILES, LANES), norm_x, F32) * norm_y))
        low_out[...] = low
        return low, dither((TILES, LANES)) + HEAD

    plain = Scores(table, place, x1, x2, yc, None, (6, 7))
    exact = Scores(table, place, x1, x2, yc, ye)

    def run():
        plain.each(functools.partial(add, True), UNROLL, 0, KEPT)
        plain.each(functools.partial(add, False), UNROLL, KEPT)

    row_half(run, finished, exact, lambda: put_in_columns(gamma, offset, ye), offset, out, acc, tops)
    keep.wait()


def col_kernel(place, number, embed, final, *refs):
    parts = refs[:number]
    weight, square, kept, low, table_hbm, x1, x2, yc, out = refs[number : number + 9]
    rest = list(refs[number + 9 :])
    f_hbm = rest.pop(0) if final else None
    acc, tops, factors, x1f, phi, table, sems = rest[:7]
    fetch = pltpu.make_async_copy(table_hbm, table, sems.at[0])
    fetch.start()
    offset = update(parts, weight, phi)
    if final:
        f_out = rest[7]
        value = phi[...]
        f = value * (1.0 / POT) + square[...] * (1.0 / embed)
        f_out[...] = jnp.where(value > 0.5 * DEAD, f, 0.0)
        copy = pltpu.make_async_copy(f_out, f_hbm, sems.at[1])
        copy.start()
    scale = dither((TILES, LANES))
    put_parts(lambda b: jnp.exp2((phi[block_rows(b), :] - (offset - HEAD)) - scale), place.sources, factors)
    fetch.wait()
    exact = Scores(table, place, x1f, x2, yc, None)
    prepare = lambda: put_in_rows(phi, offset, x1, x1f)
    col_half(kept, factors, low[...], exact, prepare, offset, out, acc, tops)
    if final:
        copy.wait()


def row_kernel(place, number, *refs):
    parts = refs[:number]
    weight, table_hbm, x1, x2, yc, out, acc, tops, ye, gamma, table, sem = refs[number:]
    fetch = pltpu.make_async_copy(table_hbm, table, sem)
    fetch.start()
    offset = update(parts, weight, gamma)
    put_in_columns(gamma, offset, ye)
    fetch.wait()
    exact = Scores(table, place, x1, x2, yc, ye)

    def add(t, row, cols, values):
        acc[row_chunk(row), :] += across([jnp.exp2(v) for v in values], jnp.add)

    run = lambda: exact.each(add, UNROLL)
    row_half(run, lambda: (LOW, 0.0), exact, lambda: None, offset, out, acc, tops)


def exchange(value, axis):
    size = lax.axis_size(axis)

    def swap(value, turn):
        return lax.ppermute(value, axis, [(i, turn(i)) for i in range(size)])

    if size & (size - 1):
        return [value] + [swap(value, lambda i, k=k: (i + k) % size) for k in range(1, size)]
    parts = [value]
    bit = size
    while bit > 1:
        value = merge(parts) if len(parts) > 1 else parts[0]
        step = max(bit // 4, 1)
        masks = range(step, bit, step)
        parts = [value] + [swap(value, lambda i, m=m: i ^ m) for m in masks]
        bit = step
    return parts


def on_device(x, y, source_counts, target_counts, source_weight, target_weight, start, pair_blocks, pair_count):
    embed, source_len = x.shape
    target_len = y.shape[1]
    a = source_weight.reshape(-1, LANES)
    b = target_weight.reshape(-1, LANES)
    g0 = start.reshape(-1, LANES)
    slots = pair_blocks.shape[3]
    place = Table(slots, source_counts.shape[0], target_counts.shape[0])
    vmem = pl.BlockSpec(memory_space=pltpu.VMEM)
    smem = pl.BlockSpec(memory_space=pltpu.SMEM)
    hbm = pl.BlockSpec(memory_space=pltpu.HBM)
    anywhere = pl.BlockSpec(memory_space=pl.ANY)
    table_scratch = pltpu.SMEM((place.size,), jnp.int32)
    params = pltpu.CompilerParams(vmem_limit_bytes=VMEM_LIMIT)
    source_tile = jax.ShapeDtypeStruct((source_len // LANES, LANES), F32)
    target_tile = jax.ShapeDtypeStruct((target_len // LANES, LANES), F32)
    row_acc = pltpu.VMEM((source_len, LANES), F32)
    col_acc = pltpu.VMEM(((target_len // CHUNK + 1) * 8, CHUNK), F32)
    source_scratch = pltpu.VMEM(source_tile.shape, F32)
    target_scratch = pltpu.VMEM(target_tile.shape, F32)
    columns_extra = pltpu.VMEM((16, target_len + CHUNK), BF16)

    def smem_like(value):
        return pltpu.SMEM(value.shape, value.dtype)

    first = (x, y, g0, b, a, pair_blocks, source_counts, target_counts)
    part, x1, x2, yc, xsq, aw, base, bw, table, kept, low = pl.pallas_call(
        lambda *refs: first_kernel(place, *refs),
        in_specs=[smem] + [hbm] * 8,
        out_specs=[vmem] * 8 + [anywhere] + [vmem] * 2,
        out_shape=[
            source_tile,
            jax.ShapeDtypeStruct((source_len, LANES), BF16),
            jax.ShapeDtypeStruct((source_len, LANES), BF16),
            jax.ShapeDtypeStruct((3 * embed, target_len + CHUNK), BF16),
            source_tile,
            source_tile,
            target_tile,
            target_tile,
            jax.ShapeDtypeStruct((place.size,), jnp.int32),
            pltpu.VMEM((KEPT * UNROLL * CHUNK, 2 * CHUNK), BF16),
            jax.ShapeDtypeStruct((TILES, LANES), F32),
        ],
        scratch_shapes=[
            row_acc,
            source_scratch,
            columns_extra,
            pltpu.VMEM((8, target_len + CHUNK), F32),
            target_scratch,
            pltpu.VMEM(x.shape, F32),
            pltpu.VMEM(y.shape, F32),
            target_scratch,
            target_scratch,
            source_scratch,
            smem_like(pair_blocks),
            smem_like(source_counts),
            smem_like(target_counts),
            pltpu.SMEM((place.columns + 1,), jnp.int32),
            smem_like(source_counts),
            smem_like(source_counts),
            table_scratch,
            pltpu.SemaphoreType.DMA((9,)),
        ],
        compiler_params=params,
        name="rows_first",
    )(pair_count, *[pltpu.with_memory_space_constraint(v, pltpu.HBM) for v in first])
    common = (table, x1, x2, yc)
    common_specs = [anywhere] + [vmem] * 3

    def columns(parts, final):
        scratch = [col_acc, col_acc, pltpu.VMEM((16, source_len), BF16)]
        scratch += [pltpu.VMEM((source_len, LANES), BF16), source_scratch, table_scratch]
        scratch.append(pltpu.SemaphoreType.DMA((2,)))
        return pl.pallas_call(
            lambda *refs: col_kernel(place, len(parts), embed, final, *refs),
            in_specs=[vmem] * (len(parts) + 4) + common_specs,
            out_specs=[vmem, hbm] if final else [vmem],
            out_shape=[target_tile, source_tile] if final else [target_tile],
            scratch_shapes=scratch + ([source_scratch] if final else []),
            compiler_params=params,
            name="columns",
        )(*parts, aw, xsq, kept, low, *common)

    def rows(parts):
        return pl.pallas_call(
            lambda *refs: row_kernel(place, len(parts), *refs),
            in_specs=[vmem] * (len(parts) + 1) + common_specs,
            out_specs=vmem,
            out_shape=source_tile,
            scratch_shapes=[
                row_acc,
                source_scratch,
                columns_extra,
                target_scratch,
                table_scratch,
                pltpu.SemaphoreType.DMA,
            ],
            compiler_params=params,
            name="rows",
        )(*parts, bw, *common)

    (part,) = columns(exchange(part, "tgt"), False)
    part = rows(exchange(part, "src"))
    part, f = columns(exchange(part, "tgt"), True)
    merged = merge(exchange(part, "src"))
    g = jnp.where(base > 0.5 * DEAD, base - merged * (1.0 / POT), 0.0)
    return f.reshape(-1), g.reshape(-1)


def solution(mesh):
    in_specs = (
        P(None, "src"),
        P(None, "tgt"),
        P("src"),
        P("tgt"),
        P("src"),
        P("tgt"),
        P("tgt"),
        P("src", "tgt", None, None),
        P("src", "tgt"),
    )
    out_specs = (P("src"), P("tgt"))
    return jax.shard_map(on_device, mesh=mesh, in_specs=in_specs, out_specs=out_specs, check_vma=False)
```

```python
import functools
import math

import jax
import jax.numpy as jnp
from jax import lax
from jax.experimental import pallas as pl
from jax.experimental.pallas import tpu as pltpu
from jax.sharding import PartitionSpec as P

F32 = jnp.float32
BF16 = jnp.bfloat16
BLOCK = 1024
LANES = 128
TILES = BLOCK // LANES
CHUNK = 256
PER_BLOCK = BLOCK // CHUNK
UNROLL = 18
KEPT = 5
BITS = 8
EXTRA = 96
DEAD = -1e30
LOW, HIGH = 2.0**-96, 2.0**120
HEAD = 48.0
ENTROPY = 0.1
LOG2E = math.log2(math.e)
POT = LOG2E / ENTROPY
VMEM_LIMIT = 10 * 1024 * 1024


def split3(value):
    high = value.astype(BF16).astype(F32)
    rest = value - high
    middle = rest.astype(BF16).astype(F32)
    return high, middle, rest - middle


def position():
    return lax.broadcasted_iota(jnp.int32, (TILES, LANES), 0) * LANES + lax.broadcasted_iota(
        jnp.int32, (TILES, LANES), 1
    )


def block_rows(b):
    return pl.ds(pl.multiple_of(b * TILES, TILES), TILES)


def lane_tile(b, k):
    return pl.ds(pl.multiple_of(b * BLOCK + k * LANES, LANES), LANES)


def row_chunk(row):
    return pl.ds(pl.multiple_of(row * CHUNK, CHUNK), CHUNK)


def col_chunk(col):
    return pl.ds(pl.multiple_of(col * 8, 8), 8)


def merge(parts):
    top = parts[0]
    for part in parts[1:]:
        top = jnp.maximum(top, part)
    total = jnp.exp2(parts[0] - top)
    for part in parts[1:]:
        total = total + jnp.exp2(part - top)
    return top + jnp.log2(total)


class Table:
    def __init__(self, slots, sources, targets):
        self.most = -(-slots * PER_BLOCK * PER_BLOCK // (2 * UNROLL)) * UNROLL
        self.sources, self.targets = sources, targets
        self.source_limit = 1
        self.target_limit = self.source_limit + sources
        self.units = self.target_limit + targets
        self.size = self.units + self.most
        self.columns = slots * PER_BLOCK + sources

    def fill(self, pairs, count, source_counts, target_counts, table, columns, wanted, place):
        number = count[0, 0]
        nowhere = self.targets * PER_BLOCK

        for i in range(self.units):
            table[i] = 0
        for b in range(self.sources):
            wanted[b] = 0

        def chunks_of(live):
            return (live + CHUNK - 1) // CHUNK

        def measure(p, carry):
            sb, tb = pairs[0, 0, 0, p], pairs[0, 0, 1, p]
            table[self.source_limit + sb] = source_counts[sb]
            table[self.target_limit + tb] = target_counts[tb]
            wanted[sb] += chunks_of(target_counts[tb])
            return carry

        lax.fori_loop(0, number, measure, 0)
        m = 0
        starts = []
        for b in range(self.sources):
            starts.append(m)
            place[b] = m
            columns[m + wanted[b]] = nowhere
            m = m + wanted[b] + (wanted[b] & 1)

        def put(p, carry):
            sb, tb = pairs[0, 0, 0, p], pairs[0, 0, 1, p]
            start = place[sb]
            chunks = chunks_of(target_counts[tb])
            for c in range(PER_BLOCK):
                columns[jnp.where(c < chunks, start + c, self.columns)] = tb * PER_BLOCK + c
            place[sb] = start + chunks
            return carry

        lax.fori_loop(0, number, put, 0)
        n = self.units
        for b in range(self.sources):
            twos = (wanted[b] + 1) >> 1
            rows = [((b * PER_BLOCK + r) << (2 * BITS)) for r in range(PER_BLOCK)]

            def emit(c, carry, first=starts[b], n=n, twos=twos, rows=rows):
                word = (columns[first + 2 * c] << BITS) + columns[first + 2 * c + 1]
                for r in range(PER_BLOCK):
                    table[n + r * twos + c] = rows[r] + word
                return carry

            lax.fori_loop(0, twos, emit, 0)
            n = n + twos * chunks_of(source_counts[b])
        steps = (n - self.units + UNROLL - 1) // UNROLL

        def fill(i, carry):
            table[i] = (nowhere << BITS) + nowhere
            return carry

        lax.fori_loop(n, self.units + steps * UNROLL, fill, 0)
        table[0] = steps


def chunks_of_unit(table, place, t):
    unit = table[place.units + t]
    mask = (1 << BITS) - 1
    return unit >> (2 * BITS), ((unit >> BITS) & mask, unit & mask)


def dither(shape):
    lane = lax.broadcasted_iota(jnp.int32, shape, len(shape) - 1)
    return ((lane * 37) & 63).astype(F32) * (1.0 / 64)


class Scores:
    def __init__(self, table, place, x1, x2, y, ye, ones=(3, 6)):
        self.table, self.place, self.x1, self.x2, self.y, self.ye = table, place, x1, x2, y, ye
        self.zero = jnp.zeros((LANES - EXTRA, CHUNK), BF16)
        sub = lax.broadcasted_iota(jnp.int32, (LANES - EXTRA, CHUNK), 0)
        lo, hi = ones
        self.static = jnp.where((sub >= lo) & (sub < hi), 1.0, 0.0).astype(BF16)

    def unit(self, t):
        row, cols = chunks_of_unit(self.table, self.place, t)
        at = row_chunk(row)
        lhs = jnp.concatenate([self.x1[at, :], self.x2[at, :]], axis=1)
        values = []
        part = self.y.shape[0] // 3
        for col in cols:
            at = pl.ds(pl.multiple_of(col * CHUNK, CHUNK), CHUNK)
            high, middle, low = (self.y[k * part : (k + 1) * part, at] for k in range(3))
            extra = [self.static] if self.ye is None else [self.ye[:, at], self.zero[16:]]
            rhs = jnp.concatenate([high, high, high, *extra, middle, middle, low, self.zero], axis=0)
            values.append(jnp.dot(lhs, rhs, preferred_element_type=F32))
        return row, cols, values

    def each(self, body, unroll, first=0, last=None):
        def step(s, carry):
            for u in range(unroll):
                body(s * unroll + u, *self.unit(s * unroll + u))
            return carry

        steps = self.table[0] if last is None else jnp.minimum(self.table[0], last)
        each = UNROLL // unroll
        lax.fori_loop(first * each, steps * each, step, 0)


def fill_ref(ref, rows, value):
    def body(i, carry):
        ref[pl.ds(pl.multiple_of(i * rows, rows), rows), :] = jnp.full((rows, ref.shape[1]), value, F32)
        return carry

    lax.fori_loop(0, ref.shape[0] // rows, body, 0)


def check(total, limit, low):
    fine = (total >= low) & (total <= HIGH)
    return jnp.where(fine | (position() >= limit), 0.0, 1.0)


def row_tile(acc, b, reduce):
    rows = [reduce(acc[lane_tile(b, r), :].T, axis=0, keepdims=True) for r in range(TILES)]
    return jnp.concatenate(rows, axis=0)


def across(values, combine):
    parts = [v[:, k * LANES : (k + 1) * LANES] for v in values for k in range(CHUNK // LANES)]
    while len(parts) > 1:
        parts = [combine(a, b) for a, b in zip(parts[::2], parts[1::2])]
    return parts[0]


def row_half(run, finished, scores, prepare, offset, out, acc, tops):
    blocks = out.shape[0] // TILES
    fill_ref(acc, CHUNK, 0.0)
    run()
    low, scale = finished()

    def finish(b, bad):
        total = row_tile(acc, b, jnp.sum)
        out[block_rows(b), :] = jnp.where(total > 0.0, (offset - scale) + jnp.log2(total), DEAD)
        return jnp.maximum(bad, check(total, scores.table[scores.place.source_limit + b], low))

    bad = lax.fori_loop(0, blocks, finish, jnp.zeros((TILES, LANES), F32), unroll=8)

    @pl.when(jnp.max(bad) > 0.0)
    def _():
        prepare()
        fill_ref(acc, CHUNK, DEAD)

        def highest(t, row, cols, values):
            acc[row_chunk(row), :] = jnp.maximum(acc[row_chunk(row), :], across(values, jnp.maximum))

        scores.each(highest, 1)

        def keep_top(b, carry):
            top = row_tile(acc, b, jnp.max)
            tops[block_rows(b), :] = jnp.where(top > 0.5 * DEAD, top, 0.0)
            return carry

        lax.fori_loop(0, blocks, keep_top, 0)
        fill_ref(acc, CHUNK, 0.0)

        def add_below(t, row, cols, values):
            lines = []
            for k in range(CHUNK // LANES):
                line = tops[pl.ds(row * (CHUNK // LANES) + k, 1), :]
                lines.append(jnp.broadcast_to(line, (LANES, LANES)).T)
            top = jnp.concatenate([jnp.concatenate(lines, axis=0)] * (CHUNK // LANES), axis=1)
            acc[row_chunk(row), :] += across([jnp.exp2(v - top) for v in values], jnp.add)

        scores.each(add_below, 1)

        def finish_below(b, carry):
            total = row_tile(acc, b, jnp.sum)
            top = tops[block_rows(b), :]
            out[block_rows(b), :] = jnp.where(total > 0.0, (offset + top) + jnp.log2(total), DEAD)
            return carry

        lax.fori_loop(0, blocks, finish_below, 0)


def col_tile(acc, b, reduce):
    rows = []
    for c in range(PER_BLOCK):
        line = reduce(acc[col_chunk(b * PER_BLOCK + c), :], axis=0, keepdims=True)
        for k in range(CHUNK // LANES):
            rows.append(line[:, k * LANES : (k + 1) * LANES])
    return jnp.concatenate(rows, axis=0)


def col_half(kept, factors, low, scores, prepare, offset, out, acc, tops):
    blocks = out.shape[0] // TILES
    table, place = scores.table, scores.place
    acc[...] = jnp.zeros(acc.shape, F32)

    def step(s, carry):
        for u in range(UNROLL):
            row, cols = chunks_of_unit(table, place, s * UNROLL + u)
            at = row_chunk(row)
            here = row_chunk(s * UNROLL + u)
            sums = jnp.dot(factors[:, at], kept[here, :], preferred_element_type=F32)
            for k, col in enumerate(cols):
                acc[col_chunk(col), :] += sums[:8, k * CHUNK : (k + 1) * CHUNK]
        return carry

    lax.fori_loop(0, jnp.minimum(table[0], KEPT), step, 0)

    @pl.when(table[0] > KEPT)
    def _():
        prepare()

        def add(t, row, cols, values):
            for col, value in zip(cols, values):
                part = jnp.sum(jnp.exp2(value).reshape(CHUNK // 8, 8, CHUNK), axis=0)
                acc[col_chunk(col), :] += part * 2.0**HEAD

        scores.each(add, UNROLL // 2, KEPT)

    def finish(b, bad):
        total = col_tile(acc, b, jnp.sum)
        out[block_rows(b), :] = jnp.where(total > 0.0, (offset - HEAD) + jnp.log2(total), DEAD)
        return jnp.maximum(bad, check(total, table[place.target_limit + b], low))

    bad = lax.fori_loop(0, blocks, finish, jnp.zeros((TILES, LANES), F32), unroll=8)

    @pl.when(jnp.max(bad) > 0.0)
    def _():
        prepare()
        fill_ref(tops, 8, DEAD)

        def highest(t, row, cols, values):
            for col, value in zip(cols, values):
                part = jnp.max(value.reshape(CHUNK // 8, 8, CHUNK), axis=0)
                tops[col_chunk(col), :] = jnp.maximum(tops[col_chunk(col), :], part)

        scores.each(highest, 1)

        def spread(i, carry):
            top = jnp.max(tops[col_chunk(i), :], axis=0, keepdims=True)
            top = jnp.where(top > 0.5 * DEAD, top, 0.0)
            tops[col_chunk(i), :] = jnp.broadcast_to(top, (8, CHUNK))
            return carry

        lax.fori_loop(0, tops.shape[0] // 8, spread, 0)
        fill_ref(acc, 8, 0.0)

        def add_below(t, row, cols, values):
            for col, value in zip(cols, values):
                e = jnp.exp2(value.reshape(CHUNK // 8, 8, CHUNK) - tops[col_chunk(col), :][None])
                acc[col_chunk(col), :] += jnp.sum(e, axis=0)

        scores.each(add_below, 1)

        def finish_below(b, carry):
            total = col_tile(acc, b, jnp.sum)
            top = col_tile(tops, b, jnp.max)
            out[block_rows(b), :] = jnp.where(total > 0.0, (offset + top) + jnp.log2(total), DEAD)
            return carry

        lax.fori_loop(0, blocks, finish_below, 0)


def put_parts(value_of, blocks, rows):
    sub = lax.broadcasted_iota(jnp.int32, (16, LANES), 0)

    def body(b, carry):
        high, middle, low = split3(value_of(b))
        for k in range(TILES):
            at = slice(k, k + 1)
            parts = jnp.where(sub == 1, middle[at, :], jnp.where(sub == 2, low[at, :], 0.0))
            rows[:, lane_tile(b, k)] = jnp.where(sub == 0, high[at, :], parts).astype(BF16)
        return carry

    lax.fori_loop(0, blocks, body, 0, unroll=4)


def put_in_columns(potential, offset, ye):
    blocks = potential.shape[0] // TILES
    put_parts(lambda b: potential[block_rows(b), :] - offset, blocks, ye)
    sub = lax.broadcasted_iota(jnp.int32, (16, LANES), 0)
    for k in range(CHUNK // LANES):
        at = pl.ds(blocks * BLOCK + k * LANES, LANES)
        ye[:, at] = jnp.where(sub == 0, DEAD, 0.0).astype(BF16)


def put_in_rows(potential, offset, x1, x1f):
    sub = lax.broadcasted_iota(jnp.int32, (8, LANES), 0)
    above = jnp.zeros((EXTRA, LANES), F32)
    below = jnp.zeros((LANES - EXTRA - 8, LANES), F32)

    def body(b, carry):
        high, middle, low = split3(potential[block_rows(b), :] - offset)
        for k in range(TILES):
            at = slice(k, k + 1)
            rows = jnp.where(sub == 4, middle[at, :], jnp.where(sub == 5, low[at, :], 0.0))
            rows = jnp.where(sub == 3, high[at, :], rows)
            turned = jnp.concatenate([above, rows, below], axis=0).T.astype(BF16)
            x1f[lane_tile(b, k), :] = x1[lane_tile(b, k), :] + turned
        return carry

    lax.fori_loop(0, potential.shape[0] // TILES, body, 0)


def update(parts, weight, potential):
    weight = weight[...]
    value = jnp.where(weight > 0.5 * DEAD, weight - merge([part[...] for part in parts]), DEAD)
    potential[...] = value
    return jnp.max(value)


def first_kernel(
    place,
    count, x_hbm, y_hbm, g0_hbm, b_hbm, a_hbm, pairs_hbm, sc_hbm, tc_hbm,
    out, x1, x2, yc, xsq, aw, base, bw, table_out, kept, low_out,
    acc, tops, ye, spread, gamma, x, y, g0, b_in, a_in, pairs, sc, tc, columns, wanted, places, table, sems,
):
    embed = x.shape[0]
    scale = 2.0 * POT / embed
    here = [(pairs_hbm, pairs), (sc_hbm, sc), (tc_hbm, tc)]
    here += [(y_hbm, y), (g0_hbm, g0), (b_hbm, b_in), (x_hbm, x), (a_hbm, a_in)]
    copies = [pltpu.make_async_copy(a, b, sems.at[i]) for i, (a, b) in enumerate(here)]
    for copy in copies:
        copy.start()
    for copy in copies[:3]:
        copy.wait()
    place.fill(pairs, count, sc, tc, table, columns, wanted, places)
    keep = pltpu.make_async_copy(table, table_out, sems.at[len(copies)])
    keep.start()
    for copy in copies[3:6]:
        copy.wait()

    def target(b, carry):
        top, norm = carry
        rows = []
        for k in range(TILES):
            at = lane_tile(b, k)
            value = y[:, at]
            yc[:, at] = jnp.concatenate([p.astype(BF16) for p in split3(value)], axis=0)
            rows.append(jnp.sum(value * value, axis=0, keepdims=True))
        square = jnp.concatenate(rows, axis=0)
        live = position() < tc[b]
        at = block_rows(b)
        base[at, :] = jnp.where(live, ENTROPY * b_in[at, :] + (1.0 / embed) * square, DEAD)
        bw[at, :] = jnp.where(live, LOG2E * b_in[at, :], DEAD)
        value = jnp.where(live, POT * g0[at, :] - (POT / embed) * square, DEAD)
        gamma[at, :] = value
        return jnp.maximum(top, value), jnp.maximum(norm, jnp.where(live, square, 0.0))

    blocks = tc.shape[0]
    nothing = jnp.zeros((TILES, LANES), F32)
    offset, norm_y = lax.fori_loop(0, blocks, target, (nothing + DEAD, nothing), unroll=4)
    offset, norm_y = jnp.max(offset), jnp.max(norm_y)
    yc[:, pl.ds(blocks * BLOCK, CHUNK)] = jnp.zeros((yc.shape[0], CHUNK), BF16)

    def widen(b, carry):
        value = jnp.exp2(gamma[block_rows(b), :] - (offset - HEAD))
        for k in range(TILES):
            spread[:, lane_tile(b, k)] = jnp.broadcast_to(value[k : k + 1, :], (8, LANES))
        return carry

    lax.fori_loop(0, blocks, widen, 0, unroll=4)
    spread[:, pl.ds(blocks * BLOCK, CHUNK)] = jnp.zeros((8, CHUNK), F32)
    for copy in copies[6:]:
        copy.wait()
    sub = lax.broadcasted_iota(jnp.int32, (LANES - EXTRA, LANES), 0)
    ones = jnp.where(sub < 3, 1.0, jnp.where(sub == 6, dither((LANES - EXTRA, LANES)), 0.0)).astype(BF16)

    def source(b, norm):
        rows = []
        for k in range(TILES):
            at = lane_tile(b, k)
            value = x[:, at]
            high, middle, low = (p.astype(BF16) for p in split3(value * scale))
            x1[at, :] = jnp.concatenate([high, middle, low, ones], axis=0).T
            x2[at, :] = jnp.concatenate([high, middle, high, middle], axis=0).T
            rows.append(jnp.sum(value * value, axis=0, keepdims=True))
        at = block_rows(b)
        square = jnp.concatenate(rows, axis=0)
        live = position() < sc[b]
        xsq[at, :] = square
        aw[at, :] = jnp.where(live, LOG2E * a_in[at, :], DEAD)
        return jnp.maximum(norm, jnp.where(live, square, 0.0))

    norm_x = jnp.max(lax.fori_loop(0, sc.shape[0], source, nothing, unroll=4))

    def add(keep_entries, t, row, cols, values):
        entries = [jnp.exp2(v) for v in values]
        stored = jnp.concatenate(entries, axis=1).astype(BF16)
        if keep_entries:
            kept[row_chunk(t), :] = stored
        weighted = []
        for col, e in zip(cols, entries):
            factor = spread[:, pl.ds(pl.multiple_of(col * CHUNK, CHUNK), CHUNK)]
            weighted.append((e.reshape(CHUNK // 8, 8, CHUNK) * factor[None]).reshape(CHUNK, CHUNK))
        acc[row_chunk(row), :] += across(weighted, jnp.add)

    def finished():
        low = LOW * jnp.exp2(scale * jnp.sqrt(jnp.full((TILES, LANES), norm_x, F32) * norm_y))
        low_out[...] = low
        return low, dither((TILES, LANES)) + HEAD

    plain = Scores(table, place, x1, x2, yc, None, (6, 7))
    exact = Scores(table, place, x1, x2, yc, ye)

    def run():
        plain.each(functools.partial(add, True), UNROLL, 0, KEPT)
        plain.each(functools.partial(add, False), UNROLL, KEPT)

    row_half(run, finished, exact, lambda: put_in_columns(gamma, offset, ye), offset, out, acc, tops)
    keep.wait()


def col_kernel(place, number, embed, final, *refs):
    parts = refs[:number]
    weight, square, kept, low, table_hbm, x1, x2, yc, out = refs[number : number + 9]
    rest = list(refs[number + 9 :])
    f_hbm = rest.pop(0) if final else None
    acc, tops, factors, x1f, phi, table, sems = rest[:7]
    fetch = pltpu.make_async_copy(table_hbm, table, sems.at[0])
    fetch.start()
    offset = update(parts, weight, phi)
    if final:
        f_out = rest[7]
        value = phi[...]
        f = value * (1.0 / POT) + square[...] * (1.0 / embed)
        f_out[...] = jnp.where(value > 0.5 * DEAD, f, 0.0)
        copy = pltpu.make_async_copy(f_out, f_hbm, sems.at[1])
        copy.start()
    scale = dither((TILES, LANES))
    put_parts(lambda b: jnp.exp2((phi[block_rows(b), :] - (offset - HEAD)) - scale), place.sources, factors)
    fetch.wait()
    exact = Scores(table, place, x1f, x2, yc, None)
    prepare = lambda: put_in_rows(phi, offset, x1, x1f)
    col_half(kept, factors, low[...], exact, prepare, offset, out, acc, tops)
    if final:
        copy.wait()


def row_kernel(place, number, *refs):
    parts = refs[:number]
    weight, table_hbm, x1, x2, yc, out, acc, tops, ye, gamma, table, sem = refs[number:]
    fetch = pltpu.make_async_copy(table_hbm, table, sem)
    fetch.start()
    offset = update(parts, weight, gamma)
    put_in_columns(gamma, offset, ye)
    fetch.wait()
    exact = Scores(table, place, x1, x2, yc, ye)

    def add(t, row, cols, values):
        acc[row_chunk(row), :] += across([jnp.exp2(v) for v in values], jnp.add)

    run = lambda: exact.each(add, UNROLL)
    row_half(run, lambda: (LOW, 0.0), exact, lambda: None, offset, out, acc, tops)


def exchange(value, axis):
    size = lax.axis_size(axis)

    def swap(value, turn):
        return lax.ppermute(value, axis, [(i, turn(i)) for i in range(size)])

    if size & (size - 1):
        return [value] + [swap(value, lambda i, k=k: (i + k) % size) for k in range(1, size)]
    parts = [value]
    bit = size
    while bit > 1:
        value = merge(parts) if len(parts) > 1 else parts[0]
        step = max(bit // 4, 1)
        masks = range(step, bit, step)
        parts = [value] + [swap(value, lambda i, m=m: i ^ m) for m in masks]
        bit = step
    return parts


def on_device(x, y, source_counts, target_counts, source_weight, target_weight, start, pair_blocks, pair_count):
    embed, source_len = x.shape
    target_len = y.shape[1]
    a = source_weight.reshape(-1, LANES)
    b = target_weight.reshape(-1, LANES)
    g0 = start.reshape(-1, LANES)
    slots = pair_blocks.shape[3]
    place = Table(slots, source_counts.shape[0], target_counts.shape[0])
    vmem = pl.BlockSpec(memory_space=pltpu.VMEM)
    smem = pl.BlockSpec(memory_space=pltpu.SMEM)
    hbm = pl.BlockSpec(memory_space=pltpu.HBM)
    anywhere = pl.BlockSpec(memory_space=pl.ANY)
    table_scratch = pltpu.SMEM((place.size,), jnp.int32)
    params = pltpu.CompilerParams(vmem_limit_bytes=VMEM_LIMIT)
    source_tile = jax.ShapeDtypeStruct((source_len // LANES, LANES), F32)
    target_tile = jax.ShapeDtypeStruct((target_len // LANES, LANES), F32)
    row_acc = pltpu.VMEM((source_len, LANES), F32)
    col_acc = pltpu.VMEM(((target_len // CHUNK + 1) * 8, CHUNK), F32)
    source_scratch = pltpu.VMEM(source_tile.shape, F32)
    target_scratch = pltpu.VMEM(target_tile.shape, F32)
    columns_extra = pltpu.VMEM((16, target_len + CHUNK), BF16)

    def smem_like(value):
        return pltpu.SMEM(value.shape, value.dtype)

    first = (x, y, g0, b, a, pair_blocks, source_counts, target_counts)
    part, x1, x2, yc, xsq, aw, base, bw, table, kept, low = pl.pallas_call(
        lambda *refs: first_kernel(place, *refs),
        in_specs=[smem] + [hbm] * 8,
        out_specs=[vmem] * 8 + [anywhere] + [vmem] * 2,
        out_shape=[
            source_tile,
            jax.ShapeDtypeStruct((source_len, LANES), BF16),
            jax.ShapeDtypeStruct((source_len, LANES), BF16),
            jax.ShapeDtypeStruct((3 * embed, target_len + CHUNK), BF16),
            source_tile,
            source_tile,
            target_tile,
            target_tile,
            jax.ShapeDtypeStruct((place.size,), jnp.int32),
            pltpu.VMEM((KEPT * UNROLL * CHUNK, 2 * CHUNK), BF16),
            jax.ShapeDtypeStruct((TILES, LANES), F32),
        ],
        scratch_shapes=[
            row_acc,
            source_scratch,
            columns_extra,
            pltpu.VMEM((8, target_len + CHUNK), F32),
            target_scratch,
            pltpu.VMEM(x.shape, F32),
            pltpu.VMEM(y.shape, F32),
            target_scratch,
            target_scratch,
            source_scratch,
            smem_like(pair_blocks),
            smem_like(source_counts),
            smem_like(target_counts),
            pltpu.SMEM((place.columns + 1,), jnp.int32),
            smem_like(source_counts),
            smem_like(source_counts),
            table_scratch,
            pltpu.SemaphoreType.DMA((9,)),
        ],
        compiler_params=params,
        name="rows_first",
    )(pair_count, *[pltpu.with_memory_space_constraint(v, pltpu.HBM) for v in first])
    common = (table, x1, x2, yc)
    common_specs = [anywhere] + [vmem] * 3

    def columns(parts, final):
        scratch = [col_acc, col_acc, pltpu.VMEM((16, source_len), BF16)]
        scratch += [pltpu.VMEM((source_len, LANES), BF16), source_scratch, table_scratch]
        scratch.append(pltpu.SemaphoreType.DMA((2,)))
        return pl.pallas_call(
            lambda *refs: col_kernel(place, len(parts), embed, final, *refs),
            in_specs=[vmem] * (len(parts) + 4) + common_specs,
            out_specs=[vmem, hbm] if final else [vmem],
            out_shape=[target_tile, source_tile] if final else [target_tile],
            scratch_shapes=scratch + ([source_scratch] if final else []),
            compiler_params=params,
            name="columns",
        )(*parts, aw, xsq, kept, low, *common)

    def rows(parts):
        return pl.pallas_call(
            lambda *refs: row_kernel(place, len(parts), *refs),
            in_specs=[vmem] * (len(parts) + 1) + common_specs,
            out_specs=vmem,
            out_shape=source_tile,
            scratch_shapes=[
                row_acc,
                source_scratch,
                columns_extra,
                target_scratch,
                table_scratch,
                pltpu.SemaphoreType.DMA,
            ],
            compiler_params=params,
            name="rows",
        )(*parts, bw, *common)

    (part,) = columns(exchange(part, "tgt"), False)
    part = rows(exchange(part, "src"))
    part, f = columns(exchange(part, "tgt"), True)
    merged = merge(exchange(part, "src"))
    g = jnp.where(base > 0.5 * DEAD, base - merged * (1.0 / POT), 0.0)
    return f.reshape(-1), g.reshape(-1)


def solution(mesh):
    in_specs = (
        P(None, "src"),
        P(None, "tgt"),
        P("src"),
        P("tgt"),
        P("src"),
        P("tgt"),
        P("tgt"),
        P("src", "tgt", None, None),
        P("src", "tgt"),
    )
    out_specs = (P("src"), P("tgt"))
    return jax.shard_map(on_device, mesh=mesh, in_specs=in_specs, out_specs=out_specs, check_vma=False)
```
